512 devices in a mesh: group: 16 (over z), dev: 32 (over x, y, core).
Axes of the slice: x: 4, y: 4, z: 16, core: 2. Of those that a mesh axis runs over, the one named last changes fastest.
Arguments:
- positions: float32 [3, 16384, 256], P(None, ('group', 'dev')), may hold values from -3 to 3
- velocities: float32 [3, 16384, 256], P(None, ('group', 'dev')), may hold values from -3 to 3
- masses: float32 [16384, 256], P(('group', 'dev')), may hold values from 0.005 to 0.05
- counts: int32 [16384], P(('group', 'dev')), may hold values from 64 to 256, as said below
- walls: int32 [16384, 256], P(('group', 'dev')), may hold values 0 or 1
- neighbours: int32 [16384, 3], P(('group', 'dev')), may hold values from 0 to 103, as said below
- send_cells: int32 [16, 32, 32, 2], P('group', 'dev'), may hold values from -1 to 31, as said below
- owners: int32 [16, 1024], P('group'), may hold values from 0 to 31, as said below
Outputs:
- new_state: float32 [6, 16384, 256], P(None, ('group', 'dev'))
- new_density: float32 [16384, 256], P(('group', 'dev'))
The draws below stay inside these ranges and needn't reach their ends.
Inputs may be any that keep to these rules, and one draw needn't show every extreme that they name: `counts`: every device holds at least one cell with 256 particles. `send_cells`: A device never sends to itself; slot 0 to every other device of its group holds a cell. `neighbours`: A cell never names its own row; on each device every rim row and every filled incoming slot is named at least once, and no empty incoming slot is named. `owners`: each device of a group owns exactly 32 cells afterwards; each device keeps 32 - 8 * 2 of its cells and hands exactly 2 cells to each of 8 other devices of its group, and none to the rest.
All inputs are finite; a program needn't handle non-finite values. No bound on the sum of `walls` on one device may be relied on, other than what follows from the above.
Results may differ from the reference program's by a relative error of at most 0.0003.
Values sent between devices are 32-bit elements; how exact they have to be, the bound alone decides.
No kernel may reach another device: no remote copies, remote signals or barrier semaphores. Data moves between devices by JAX's collectives and lax.ppermute only.
A program may use at most 64 MiB of HBM per device.

```python
import math
import jax
import jax.numpy as jnp
from jax import lax

BLOCK_SIZE = 256
CELLS_DEV = 32
NEAR_CELLS = 3
RIM_CELLS = 4
SEND_SLOTS = 2
CAPACITY = 2
MOVE_SHIFTS = 8
CELLS_ALL = 16384
N_GROUP = 16
N_DEV = 32


def link_layout(key):
    base = jax.random.fold_in(key, 11)
    key_cells, key_keep, key_perm, key_local = jax.random.split(base, 4)
    shape = (N_GROUP, N_DEV, N_DEV, SEND_SLOTS)
    picked = jax.random.randint(key_cells, shape, 0, CELLS_DEV).astype(jnp.int32)
    coin = jax.random.randint(key_keep, shape, 0, 2).astype(jnp.int32)
    slot_axis = lax.broadcasted_iota(jnp.int32, shape, 3)
    source_axis = lax.broadcasted_iota(jnp.int32, shape, 1)
    target_axis = lax.broadcasted_iota(jnp.int32, shape, 2)
    keep = jnp.where(slot_axis == 0, 1, coin)
    keep = jnp.where(source_axis == target_axis, 0, keep)
    send_list = jnp.where(keep == 1, picked, -1).astype(jnp.int32)
    incoming = jnp.transpose(keep, (0, 2, 1, 3)).reshape(N_GROUP * N_DEV, N_DEV * SEND_SLOTS)
    halo_ids = 2 * RIM_CELLS + CELLS_DEV + jnp.arange(N_DEV * SEND_SLOTS, dtype=jnp.int32)
    halo_ids = jnp.where(incoming == 1, halo_ids[None, :], -1)
    rim_ids = jnp.concatenate([jnp.arange(RIM_CELLS, dtype=jnp.int32), RIM_CELLS + CELLS_DEV + jnp.arange(RIM_CELLS, dtype=jnp.int32)])
    total = CELLS_DEV * NEAR_CELLS
    filler = total - N_DEV * SEND_SLOTS - 2 * RIM_CELLS
    device_count = N_GROUP * N_DEV
    template = jnp.concatenate([halo_ids, jnp.broadcast_to(rim_ids[None, :], (device_count, 2 * RIM_CELLS)), jnp.full((device_count, filler), -1, jnp.int32)], 1)
    device_keys = jax.random.split(key_perm, device_count)
    orders = jax.vmap(lambda one_key: jax.random.permutation(one_key, total))(device_keys).astype(jnp.int32)
    shuffled = jnp.take_along_axis(template, orders, 1)
    owner_cell = lax.broadcasted_iota(jnp.int32, (device_count, total), 1) // NEAR_CELLS
    stride = jax.random.randint(key_local, (device_count, total), 1, CELLS_DEV).astype(jnp.int32)
    local_rows = RIM_CELLS + (owner_cell + stride) % CELLS_DEV
    refs = jnp.where(shuffled < 0, local_rows, shuffled).astype(jnp.int32)
    return (send_list, refs.reshape(CELLS_ALL, NEAR_CELLS))


def draw_send_cells(key, part):
    return link_layout(key)[0]


def draw_neighbours(key, part):
    return link_layout(key)[1]


def draw_owners(key, part):
    base = jax.random.fold_in(key, 23)
    key_shift, key_order = jax.random.split(base, 2)
    group_keys = jax.random.split(key_shift, N_GROUP)
    shifts = jax.vmap(lambda one_key: jax.random.permutation(one_key, N_DEV - 1)[:MOVE_SHIFTS])(group_keys).astype(jnp.int32) + 1
    movers = MOVE_SHIFTS * CAPACITY
    per_slot = jnp.concatenate([jnp.repeat(shifts, CAPACITY, axis=1), jnp.zeros((N_GROUP, CELLS_DEV - movers), jnp.int32)], 1)
    device_keys = jax.random.split(key_order, N_GROUP * N_DEV)
    orders = jax.vmap(lambda one_key: jax.random.permutation(one_key, CELLS_DEV))(device_keys).astype(jnp.int32)
    orders = orders.reshape(N_GROUP, N_DEV, CELLS_DEV)
    spread = jnp.take_along_axis(jnp.broadcast_to(per_slot[:, None, :], (N_GROUP, N_DEV, CELLS_DEV)), orders, 2)
    device_axis = lax.broadcasted_iota(jnp.int32, (N_GROUP, N_DEV, CELLS_DEV), 1)
    return ((device_axis + spread) % N_DEV).astype(jnp.int32).reshape(N_GROUP, N_DEV * CELLS_DEV)


def draw_counts(key, part):
    base = jax.random.fold_in(key, 37)
    key_count, key_full = jax.random.split(base, 2)
    device_count = N_GROUP * N_DEV
    filled = jax.random.randint(key_count, (device_count, CELLS_DEV), BLOCK_SIZE // 4, BLOCK_SIZE + 1).astype(jnp.int32)
    full_cell = jax.random.randint(key_full, (device_count, 1), 0, CELLS_DEV).astype(jnp.int32)
    cell_axis = lax.broadcasted_iota(jnp.int32, (device_count, CELLS_DEV), 1)
    filled = jnp.where(cell_axis == full_cell, BLOCK_SIZE, filled)
    return filled.reshape(CELLS_ALL).astype(jnp.int32)


def set_ends(drawn, stream_key, smallest, high):
    longest = drawn.shape.index(max(drawn.shape))
    spots = []
    for shift in (0, 1):
        where = [jax.random.randint(jax.random.fold_in(stream_key, axis), (), 0, length) for axis, length in enumerate(drawn.shape)]
        where[longest] = (where[longest] + shift) % drawn.shape[longest]
        spots.append(tuple(where))
    return drawn.at[spots[0]].set(smallest).at[spots[1]].set(high)


def block_levels(own_key, dims, cuts, least, largest):
    gain = 1.0
    for axis_at, shards_of in cuts:
        steps = jax.random.uniform(jax.random.fold_in(jax.random.fold_in(own_key, 6), axis_at), (shards_of,), jnp.float32, least / len(cuts), largest / len(cuts))
        gain = gain * jnp.repeat(jnp.exp(steps), dims[axis_at] // shards_of).reshape((-1,) + (1,) * (len(dims) - 1 - axis_at))
    return gain


def gaussian(stream_key, extent, deviation, most, cuts=(), kind=jnp.bfloat16):
    result = jax.random.normal(stream_key, extent, jnp.float32) * deviation
    if len(cuts) > 0:
        result = block_levels(stream_key, extent, cuts, -0.22, 0.18) * result
    return jnp.clip(result, min=-most, max=most).astype(kind)


def setup_inputs(seed: int = 0) -> dict:
    key_list = jax.random.split(jax.random.key(seed), 9)
    positions = gaussian(key_list[0], (3, CELLS_ALL, BLOCK_SIZE), 1.0, 3.0, ((1, 512),), jnp.float32)
    velocities = gaussian(key_list[1], (3, CELLS_ALL, BLOCK_SIZE), 0.5, 3.0, ((1, 512),), jnp.float32)
    masses = jnp.clip(jnp.exp(math.log(0.05) - 2.3025851 * jax.random.uniform(key_list[2], (CELLS_ALL, BLOCK_SIZE), jnp.float32) ** block_levels(key_list[2], (CELLS_ALL, BLOCK_SIZE), ((0, 512),), -0.2, 0.2)), 0.005, 0.05)
    counts = draw_counts(jax.random.fold_in(key_list[8], 71), 0)
    walls = set_ends((jax.random.randint(key_list[4], (CELLS_ALL, BLOCK_SIZE), 0, 4) < 1).astype(jnp.int32), jax.random.fold_in(key_list[4], 1), 0, 1)
    neighbours = draw_neighbours(jax.random.fold_in(key_list[8], 71), 0)
    send_cells = draw_send_cells(jax.random.fold_in(key_list[8], 71), 0)
    owners = draw_owners(jax.random.fold_in(key_list[8], 71), 0)
    return dict(positions=positions, velocities=velocities, masses=masses, counts=counts, walls=walls, neighbours=neighbours, send_cells=send_cells, owners=owners)


SUPPORT = 4.0
STIFFNESS = 2.0
REST_DENSITY = 0.8
VISCOSITY = 0.5
COHESION = 0.3
ADHESION = 0.8
GRAVITY = 1.0
TIME_STEP = 0.5


def pair_density(own_pos, lookup, columns):
    remote = lookup[:, columns, :]
    distance = jnp.zeros((own_pos.shape[1], own_pos.shape[2], columns.shape[1], lookup.shape[2]), jnp.float32)
    for component in range(3):
        offset = own_pos[component][:, :, None, None] - remote[component][:, None, :, :]
        distance = distance + offset * offset
    weight = jnp.maximum(1.0 - distance / SUPPORT, 0.0)
    return jnp.sum(remote[3][:, None, :, :] * weight * weight * weight, axis=(2, 3))


def pair_force(own_pos, own_vel, own_q, lookup, columns):
    remote = lookup[:, columns, :]
    distance = jnp.zeros((own_pos.shape[1], own_pos.shape[2], columns.shape[1], lookup.shape[2]), jnp.float32)
    offsets = []
    for component in range(3):
        offset = own_pos[component][:, :, None, None] - remote[component][:, None, :, :]
        offsets.append(offset)
        distance = distance + offset * offset
    weight = jnp.maximum(1.0 - distance / SUPPORT, 0.0)
    cube = weight * weight * weight
    pushes = remote[6][:, None] * (own_q[:, :, None, None] + remote[8][:, None]) * (6.0 / SUPPORT) * weight * weight - remote[7][:, None] * weight
    damping = VISCOSITY * remote[6][:, None] * cube
    total_damping = jnp.sum(damping, axis=(2, 3))
    rows = []
    for component in range(3):
        rows.append(jnp.sum(offsets[component] * pushes + damping * remote[3 + component][:, None], axis=(2, 3)) - own_vel[component] * total_damping)
    return jnp.stack(rows, 0)


def group_table(field, send_cells, group_index):
    last_group = field.shape[1] - 1
    below = lax.dynamic_index_in_dim(field, jnp.maximum(group_index - 1, 0), 1, keepdims=False)[:, :, CELLS_DEV - RIM_CELLS:]
    below = below * (group_index > 0).astype(jnp.float32)
    above = lax.dynamic_index_in_dim(field, jnp.minimum(group_index + 1, last_group), 1, keepdims=False)[:, :, :RIM_CELLS]
    above = above * (group_index < last_group).astype(jnp.float32)
    own_cells = lax.dynamic_index_in_dim(field, group_index, 1, keepdims=False)
    send_list = lax.dynamic_index_in_dim(send_cells, group_index, 0, keepdims=False)
    source = jnp.arange(N_DEV, dtype=jnp.int32)[:, None, None]
    picked = own_cells[:, source, jnp.maximum(send_list, 0)]
    picked = picked * (send_list >= 0).astype(jnp.float32)[None, :, :, :, None]
    peer_rows = jnp.transpose(picked, (0, 2, 1, 3, 4)).reshape(field.shape[0], N_DEV, N_DEV * SEND_SLOTS, BLOCK_SIZE)
    return jnp.concatenate([below, own_cells, above, peer_rows], axis=2)


def reference(positions, velocities, masses, counts, walls, neighbours, send_cells, owners):
    particle_slot = lax.broadcasted_iota(jnp.int32, (CELLS_ALL, BLOCK_SIZE), 1)
    active = (particle_slot < counts[:, None]).astype(jnp.float32)
    wall_mask = walls.astype(jnp.float32) * active
    fluid_mask = active - wall_mask
    mass_eff = masses * active
    bond = mass_eff * (COHESION + (ADHESION - COHESION) * wall_mask)
    near = neighbours.reshape(N_GROUP, N_DEV, CELLS_DEV, NEAR_CELLS)
    self_rows = RIM_CELLS + jnp.arange(CELLS_DEV, dtype=jnp.int32)

    def split_devices(field):
        return field.reshape(field.shape[0], N_GROUP, N_DEV, CELLS_DEV, BLOCK_SIZE)

    dens_field = split_devices(jnp.concatenate([positions, mass_eff[None]], 0))

    def density_group(group_index):
        lookup = group_table(dens_field, send_cells, group_index)

        def per_device(device_index):
            columns = jnp.concatenate([self_rows[:, None], near[group_index, device_index]], 1)
            return pair_density(dens_field[0:3, group_index, device_index], lookup[:, device_index], columns)

        return lax.map(per_device, jnp.arange(N_DEV, dtype=jnp.int32))

    density = lax.map(density_group, jnp.arange(N_GROUP, dtype=jnp.int32)).reshape(CELLS_ALL, BLOCK_SIZE)
    safe_rho = active * density + (1.0 - active)
    pressure_q = active * STIFFNESS * (density - REST_DENSITY) / (safe_rho * safe_rho)
    force_field = split_devices(jnp.concatenate([positions, velocities, mass_eff[None], bond[None], pressure_q[None]], 0))

    def force_group(group_index):
        lookup = group_table(force_field, send_cells, group_index)

        def per_device(device_index):
            columns = jnp.concatenate([self_rows[:, None], near[group_index, device_index]], 1)
            own_block = force_field[:, group_index, device_index]
            return pair_force(own_block[0:3], own_block[3:6], own_block[8], lookup[:, device_index], columns)

        return lax.map(per_device, jnp.arange(N_DEV, dtype=jnp.int32))

    acceleration = lax.map(force_group, jnp.arange(N_GROUP, dtype=jnp.int32))
    acceleration = jnp.transpose(acceleration, (2, 0, 1, 3, 4)).reshape(3, CELLS_ALL, BLOCK_SIZE)
    gravity_vec = jnp.array([0.0, 0.0, GRAVITY], jnp.float32)[:, None, None]
    acceleration = acceleration - gravity_vec
    new_vel = velocities + TIME_STEP * fluid_mask[None] * acceleration
    new_pos = positions + TIME_STEP * fluid_mask[None] * new_vel
    moved = jnp.concatenate([new_pos, new_vel, density[None]], 0) * active[None]
    moved = moved.reshape(7, N_GROUP, N_DEV * CELLS_DEV, BLOCK_SIZE)
    order = jnp.argsort(owners, axis=1, stable=True).astype(jnp.int32)
    settled = jnp.take_along_axis(moved, order[None, :, :, None], axis=2).reshape(7, CELLS_ALL, BLOCK_SIZE)
    return settled[0:6], settled[6]
```

```python
import jax
import jax.numpy as jnp
from jax import lax
from jax.experimental import pallas as pl
from jax.experimental.pallas import tpu as pltpu
from jax.sharding import PartitionSpec as P

RIM = 4
SLOTS = 2
STIFFNESS = 2.0
REST_DENSITY = 0.8
VISCOSITY = 0.5
COHESION = 0.3
ADHESION = 0.8
GRAVITY = 1.0
TIME_STEP = 0.5

F32 = jnp.float32
BF16 = jnp.bfloat16
VMEM = pl.BlockSpec(memory_space=pltpu.VMEM)
SMEM = pl.BlockSpec(memory_space=pltpu.SMEM)


def call(kernel, outs, specs, scratch=(), flops=0):
    return pl.pallas_call(
        kernel,
        out_shape=[jax.ShapeDtypeStruct(s, t) for s, t in outs],
        in_specs=specs,
        out_specs=[VMEM] * len(outs),
        scratch_shapes=list(scratch),
        compiler_params=pltpu.CompilerParams(vmem_limit_bytes=48 * 2**20),
        cost_estimate=pl.CostEstimate(flops=flops, bytes_accessed=2**20, transcendentals=0),
        name=kernel.__name__,
    )


def contract(a, b, dim):
    return lax.dot_general(a, b, (((dim,), (0,)), ((), ())), preferred_element_type=F32)


def pieces(value, count):
    parts = []
    for _ in range(count):
        part = value.astype(BF16).astype(F32)
        parts.append(part)
        value = value - part
    return parts


def prepare(counts, sends, pos, vel, mass, walls, own, send, head, tail, fluid):
    cells, width = mass.shape
    m = mass[...]
    root = jnp.exp(jnp.log(m) * (1.0 / 3.0))
    root = root - (root * root * root - m) / (3.0 * root * root)
    wall = walls[...].astype(F32)
    bond = root * root * (COHESION + (ADHESION - COHESION) * wall)
    free = 1.0 - wall
    lane = lax.broadcasted_iota(jnp.int32, (1, width), 1)
    for c in range(cells):
        row = slice(c, c + 1)
        active = lane < counts[c]
        for k in range(3):
            own[c, k : k + 1, :] = pos[k, row, :]
            own[c, 4 + k : 5 + k, :] = vel[k, row, :]
        own[c, 3:4, :] = jnp.where(active, root[row], 0.0)
        own[c, 7:8, :] = jnp.where(active, bond[row], 0.0)
        fluid[row, :] = jnp.where(active, free[row], 0.0)
    head[...] = own[0:RIM]
    tail[...] = own[cells - RIM : cells]
    for t in range(send.shape[0] // SLOTS):
        for k in range(SLOTS):
            cell = sends[0, 0, t, k]
            tile = own[jnp.maximum(cell, 0)]
            send[t * SLOTS + k] = jnp.where(cell >= 0, tile, 0.0)


def segments(below, own, above, rest):
    start = 0
    for ref in (below, own, above, rest):
        yield start, ref
        start += ref.shape[0]


def weigh(near, tab, mine, c):
    for k in range(near.shape[1] + 1):
        row = RIM + c if k == 0 else near[c, k - 1]
        yield row, jnp.maximum(contract(tab[row], mine[c], 0), 0.0)


def densities(counts, near, sends, below, own, above, rest, rho, q, send_q, tab, mine):
    cells, _, width = own.shape
    sub = lax.broadcasted_iota(jnp.int32, (8, width), 0)

    def squared(tile):
        return jnp.sum(jnp.where(sub < 3, tile * tile, 0.0), axis=0, keepdims=True)

    for start, ref in segments(below, own, above, rest):

        def source(i, carry, start=start, ref=ref):
            tile = ref[i]
            root = tile[3:4]
            far = root * (1.0 - 0.25 * squared(tile))
            value = jnp.where(
                sub < 3,
                tile * (0.5 * root),
                jnp.where(sub == 3, far, jnp.where(sub == 4, -0.25 * root, 0.0)),
            )
            a, b, c = pieces(value, 3)
            tab[start + i] = jnp.concatenate([a, b, a, c, a, b], 0).astype(BF16)
            return carry

        lax.fori_loop(0, ref.shape[0], source, 0, unroll=4)

    def target(i, carry):
        tile = own[i]
        value = jnp.where(
            sub < 3,
            tile,
            jnp.where(sub == 3, 1.0, jnp.where(sub == 4, squared(tile), 0.0)),
        )
        a, b, c = pieces(value, 3)
        mine[i] = jnp.concatenate([a, a, b, a, c, b], 0).astype(BF16)
        return carry

    lax.fori_loop(0, cells, target, 0, unroll=4)

    def cell(i, carry):
        for c in (2 * i, 2 * i + 1):
            total = jnp.zeros((8, width), F32)
            for _, w in weigh(near, tab, mine, c):
                total = total + jnp.sum((w * w * w).reshape(width // 8, 8, width), axis=0)
            rho[pl.ds(c, 1), :] = jnp.sum(total, axis=0, keepdims=True)
        return carry

    lax.fori_loop(0, cells // 2, cell, 0)
    lane = lax.broadcasted_iota(jnp.int32, (1, width), 1)
    for c in range(cells):
        row = rho[c : c + 1, :]
        active = lane < counts[c]
        safe = jnp.where(active, row, 1.0)
        value = STIFFNESS * (row - REST_DENSITY) / (safe * safe)
        q[c : c + 1, :] = jnp.where(active, value, 0.0)
        rho[c : c + 1, :] = jnp.where(active, row, 0.0)
    for t in range(send_q.shape[0] // SLOTS):
        for k in range(SLOTS):
            pick = jnp.maximum(sends[0, 0, t, k], 0)
            send_q[t * SLOTS + k : t * SLOTS + k + 1, :] = q[pl.ds(pick, 1), :]


def forces(
    counts, near, outs, below, own, above, rest, q_below, q, q_above, q_rest, rho, fluid, tab, mine,
    moved, outbox, feat,
):
    cells, _, width = own.shape
    sub = lax.broadcasted_iota(jnp.int32, (8, width), 0)

    for (start, ref), (_, q_ref) in zip(
        segments(below, own, above, rest), segments(q_below, q, q_above, q_rest)
    ):

        def source(i, carry, start=start, ref=ref, q_ref=q_ref):
            tile = ref[i]
            row_q = q_ref[pl.ds(i, 1), :]
            bond = tile[7:8]
            first = jnp.where(
                sub < 3,
                tile * bond,
                jnp.where(sub == 3, bond, jnp.where(sub < 7, tile, 0.0)),
            )
            spot = jnp.where(sub < 3, tile, 1.0)
            spot = jnp.where(sub < 4, spot, row_q * pltpu.roll(spot, 4, 0))
            second = spot * (1.5 * tile[3:4])
            rows = pieces(first, 2) + pieces(second, 3) + [jnp.zeros((8, width), F32)]
            feat[start + i] = jnp.concatenate(rows, 0).astype(BF16)
            return carry

        lax.fori_loop(0, ref.shape[0], source, 0, unroll=4)

    lane = lax.broadcasted_iota(jnp.int32, (1, width), 1)

    def cell(c, carry):
        feats, odd, even = [], [], []
        for row, w in weigh(near, tab, mine, c):
            feats.append(feat[row])
            square = w * w
            high = square.astype(BF16)
            low = (square - high.astype(F32)).astype(BF16)
            once = w.astype(BF16)
            odd.append(jnp.concatenate([once, (square * w).astype(BF16)], 1))
            even.append(jnp.concatenate([high, low], 1))
        feats = jnp.concatenate(feats, 1)
        o13 = contract(feats[0:16], jnp.concatenate(odd, 0), 1)
        o2 = contract(feats[16:48], jnp.concatenate(even, 0), 1)
        o13 = o13[0:8] + o13[8:16]
        o2 = o2[:, :width] + o2[:, width:]
        o2 = o2[0:8] + o2[8:16] + o2[16:24]
        tile = own[c]
        row_rho = rho[pl.ds(c, 1), :]
        mix = q[pl.ds(c, 1), :] * o2 + pltpu.roll(o2, 4, 0) - o13[:, :width]
        speed = pltpu.roll(tile, 4, 0)
        drag = pltpu.roll(o13[:, width:], 4, 0) - speed * row_rho
        acc = tile * mix[3:4] - mix + VISCOSITY * drag
        acc = acc - jnp.where(sub == 2, GRAVITY, 0.0)
        step = TIME_STEP * fluid[pl.ds(c, 1), :]
        speed = speed + step * acc
        place = tile + step * speed
        result = jnp.where(
            sub < 3,
            place,
            jnp.where(sub < 6, pltpu.roll(speed, 3, 0), jnp.where(sub == 6, row_rho, 0.0)),
        )
        moved[c] = jnp.where(lane < counts[c], result, 0.0)
        return carry

    lax.fori_loop(0, cells, cell, 0)
    for t in range(outbox.shape[0] // SLOTS):
        for k in range(SLOTS):
            outbox[t * SLOTS + k] = moved[outs[t, k]]


def settle(kept, arrived, moved, inbox, state, density):
    cells = moved.shape[0]

    def put(place, tile):
        @pl.when(place < cells)
        def _():
            for k in range(6):
                state[k, pl.ds(place, 1), :] = tile[k : k + 1]
            density[pl.ds(place, 1), :] = tile[6:7]

    for c in range(cells):
        put(kept[c], moved[c])
    for t in range(inbox.shape[0] // SLOTS):
        for k in range(SLOTS):
            put(arrived[t, k], inbox[t * SLOTS + k])


def routes(owners, cells, peers):
    me = lax.axis_index("dev")
    ids = jnp.arange(cells, dtype=jnp.int32)
    devs = jnp.arange(peers, dtype=jnp.int32)
    slots = jnp.arange(SLOTS, dtype=jnp.int32)
    per_dev = owners.reshape(peers, cells)
    arrivals = jnp.sum((per_dev == me).astype(jnp.int32), 1)
    before = jnp.sum(jnp.where(devs[None, :] < devs[:, None], arrivals[None, :], 0), 1)
    arrived = jnp.where(
        (slots[None, :] < arrivals[:, None]) & (devs[:, None] != me),
        before[:, None] + slots[None, :],
        cells,
    )
    targets = jnp.sum(jnp.where(devs[:, None] == me, per_dev, 0), 0)
    same = (targets[None, :] == targets[:, None]) & (ids[None, :] < ids[:, None])
    rank = jnp.sum(same.astype(jnp.int32), 1)
    mine = jnp.sum(jnp.where(devs < me, arrivals, 0))
    kept = jnp.where(targets == me, mine + rank, cells)
    hit = (targets[None, None, :] == devs[:, None, None]) & (
        rank[None, None, :] == slots[None, :, None]
    )
    outs = jnp.sum(jnp.where(hit, ids[None, None, :], 0), 2)
    return kept, arrived, outs


def shards(positions, velocities, masses, counts, walls, neighbours, send_cells, owners):
    cells, width = masses.shape
    peers = lax.axis_size("dev")
    total = 2 * RIM + cells + SLOTS * peers
    groups = lax.axis_size("group")
    up = [(i, i + 1) for i in range(groups - 1)]
    down = [(i + 1, i) for i in range(groups - 1)]

    def exchange(x):
        return lax.all_to_all(x, "dev", split_axis=0, concat_axis=0, tiled=True)

    kept, arrived, outs = routes(owners[0], cells, peers)
    own, send, head, tail, fluid = call(
        prepare,
        [
            ((cells, 8, width), F32),
            ((SLOTS * peers, 8, width), F32),
            ((RIM, 8, width), F32),
            ((RIM, 8, width), F32),
            ((cells, width), F32),
        ],
        [SMEM] * 2 + [VMEM] * 4,
    )(counts, send_cells, positions, velocities, masses, walls)
    rest = exchange(send)
    below = lax.ppermute(tail, "group", up)
    above = lax.ppermute(head, "group", down)
    rho, q, send_q, tab, mine = call(
        densities,
        [
            ((cells, width), F32),
            ((cells, width), F32),
            ((SLOTS * peers, width), F32),
            ((total, 48, width), BF16),
            ((cells, 48, width), BF16),
        ],
        [SMEM] * 3 + [VMEM] * 4,
    )(counts, neighbours, send_cells, below, own, above, rest)
    q_rest = exchange(send_q)
    q_below = lax.ppermute(q[cells - RIM :], "group", up)
    q_above = lax.ppermute(q[:RIM], "group", down)
    moved, outbox = call(
        forces,
        [((cells, 8, width), F32), ((SLOTS * peers, 8, width), F32)],
        [SMEM] * 3 + [VMEM] * 12,
        [pltpu.VMEM((total, 48, width), BF16)],
    )(
        counts, neighbours, outs, below, own, above, rest,
        q_below, q, q_above, q_rest, rho, fluid, tab, mine,
    )
    inbox = exchange(outbox)
    state, density = call(
        settle,
        [((6, cells, width), F32), ((cells, width), F32)],
        [SMEM] * 2 + [VMEM] * 2,
    )(kept, arrived, moved, inbox)
    return state, density


def solution(mesh):
    return jax.shard_map(
        shards,
        mesh=mesh,
        in_specs=(
            P(None, ("group", "dev"), None),
            P(None, ("group", "dev"), None),
            P(("group", "dev"), None),
            P(("group", "dev")),
            P(("group", "dev"), None),
            P(("group", "dev"), None),
            P("group", "dev", None, None),
            P("group", None),
        ),
        out_specs=(P(None, ("group", "dev"), None), P(("group", "dev"), None)),
        check_vma=False,
    )
```

```python
import jax
import jax.numpy as jnp
from jax import lax
from jax.experimental import pallas as pl
from jax.experimental.pallas import tpu as pltpu
from jax.sharding import PartitionSpec as P

RIM = 4
SLOTS = 2
STIFFNESS = 2.0
REST_DENSITY = 0.8
VISCOSITY = 0.5
COHESION = 0.3
ADHESION = 0.8
GRAVITY = 1.0
TIME_STEP = 0.5

F32 = jnp.float32
BF16 = jnp.bfloat16
HBM = pl.BlockSpec(memory_space=pltpu.HBM)
VMEM = pl.BlockSpec(memory_space=pltpu.VMEM)


class Moves:
    def __init__(self, ins, outs):
        self.ins, self.outs = list(ins), list(outs)
        self.waited, self.saved = set(), set()
        for copy in self.ins:
            copy.start()

    def need(self, *which):
        for i in which:
            if i not in self.waited:
                self.waited.add(i)
                self.ins[i].wait()

    def save(self, *which):
        for i in which:
            if i not in self.saved:
                self.saved.add(i)
                self.outs[i].start()


def call(kernel, room, ints, held, near, outs, scratch=()):
    n_in, n_near, n_out = len(ints) + len(held), len(near), len(outs)

    def body(*refs):
        sources, refs = refs[:n_in], refs[n_in:]
        close, refs = refs[:n_near], refs[n_near:]
        targets, refs = refs[:n_out], refs[n_out:]
        inner, refs = refs[:n_in], refs[n_in:]
        results, refs = refs[:n_out], refs[n_out:]
        in_sems, out_sems, rest = refs[0], refs[1], refs[2:]
        moves = Moves(
            [pltpu.make_async_copy(a, b, in_sems.at[i]) for i, (a, b) in enumerate(zip(sources, inner))],
            [pltpu.make_async_copy(a, b, out_sems.at[i]) for i, (a, b) in enumerate(zip(results, targets))],
        )
        kernel(moves, *inner, *close, *results, *rest)
        moves.need(*range(n_in))
        moves.save(*range(n_out))
        for copy in moves.outs:
            copy.wait()

    return pl.pallas_call(
        body,
        out_shape=[jax.ShapeDtypeStruct(*o) for o in outs],
        in_specs=[HBM] * n_in + [VMEM] * n_near,
        out_specs=[HBM] * n_out,
        scratch_shapes=[pltpu.SMEM(x.shape, x.dtype) for x in ints]
        + [pltpu.VMEM(x.shape, x.dtype) for x in held]
        + [pltpu.VMEM(*o) for o in outs]
        + [pltpu.SemaphoreType.DMA((n_in,)), pltpu.SemaphoreType.DMA((n_out,))]
        + list(scratch),
        compiler_params=pltpu.CompilerParams(vmem_limit_bytes=(64 << 20) - (room << 10)),
        name=kernel.__name__,
    )(*ints, *held, *near)


def contract(a, b, dim):
    return lax.dot_general(a, b, (((dim,), (0,)), ((), ())), preferred_element_type=F32)


def pieces(value, count):
    parts = []
    for _ in range(count):
        part = value.astype(BF16).astype(F32)
        parts.append(part)
        value = value - part
    return parts


def prepare(moves, counts, sends, pos, vel, mass, walls, own, send, head, tail, fluid):
    cells, width = mass.shape
    moves.need(*range(6))
    m = mass[...]
    root = jnp.exp(jnp.log(m) * (1.0 / 3.0))
    root = root - (root * root * root - m) / (3.0 * root * root)
    wall = walls[...].astype(F32)
    bond = root * root * (COHESION + (ADHESION - COHESION) * wall)
    free = 1.0 - wall
    lane = lax.broadcasted_iota(jnp.int32, (1, width), 1)
    for c in range(cells):
        row = slice(c, c + 1)
        active = lane < counts[c]
        for k in range(3):
            own[c, k : k + 1, :] = pos[k, row, :]
            own[c, 4 + k : 5 + k, :] = vel[k, row, :]
        own[c, 3:4, :] = jnp.where(active, root[row], 0.0)
        own[c, 7:8, :] = jnp.where(active, bond[row], 0.0)
        fluid[row, :] = jnp.where(active, free[row], 0.0)
    head[...] = own[0:RIM]
    tail[...] = own[cells - RIM : cells]
    for t in range(send.shape[0] // SLOTS):
        for k in range(SLOTS):
            cell = sends[0, 0, k, t]
            tile = own[jnp.maximum(cell, 0)]
            send[t * SLOTS + k] = jnp.where(cell >= 0, tile, 0.0)


def segments(below, own, above, rest):
    start = 0
    for ref in (below, own, above, rest):
        yield start, ref
        start += ref.shape[0]


def weigh(near, tab, mine, c):
    for k in range(near.shape[0] + 1):
        row = RIM + c if k == 0 else near[k - 1, c]
        yield row, jnp.maximum(contract(tab[row], mine[c], 0), 0.0)


def densities(
    moves, counts, near, sends, own, below, above, rest, rho, q, q_head, q_tail, send_q, tab, mine, tiles,
):
    moves.need(0, 1, 2, 3)
    cells, _, width = own.shape
    sub = lax.broadcasted_iota(jnp.int32, (8, width), 0)

    def squared(tile):
        return jnp.sum(jnp.where(sub < 3, tile * tile, 0.0), axis=0, keepdims=True)

    for start, ref in segments(below, own, above, rest):

        def source(i, carry, start=start, ref=ref):
            tile = ref[i]
            root = tile[3:4]
            far = root * (1.0 - 0.25 * squared(tile))
            value = jnp.where(
                sub < 3,
                tile * (0.5 * root),
                jnp.where(sub == 3, far, jnp.where(sub == 4, -0.25 * root, 0.0)),
            )
            a, b, c = pieces(value, 3)
            tab[start + i] = jnp.concatenate([a, b, a, c, a, b], 0).astype(BF16)
            tiles[start + i] = tile
            return carry

        lax.fori_loop(0, ref.shape[0], source, 0, unroll=4)

    def target(i, carry):
        tile = own[i]
        value = jnp.where(
            sub < 3,
            tile,
            jnp.where(sub == 3, 1.0, jnp.where(sub == 4, squared(tile), 0.0)),
        )
        a, b, c = pieces(value, 3)
        mine[i] = jnp.concatenate([a, a, b, a, c, b], 0).astype(BF16)
        return carry

    lax.fori_loop(0, cells, target, 0, unroll=4)
    moves.save(5, 6, 7)

    def cell(i, carry):
        for c in (2 * i, 2 * i + 1):
            total = jnp.zeros((8, width), F32)
            for _, w in weigh(near, tab, mine, c):
                total = total + jnp.sum((w * w * w).reshape(width // 8, 8, width), axis=0)
            rho[pl.ds(c, 1), :] = jnp.sum(total, axis=0, keepdims=True)
        return carry

    lax.fori_loop(0, cells // 2, cell, 0)
    lane = lax.broadcasted_iota(jnp.int32, (1, width), 1)
    for c in range(cells):
        row = rho[c : c + 1, :]
        active = lane < counts[c]
        safe = jnp.where(active, row, 1.0)
        value = STIFFNESS * (row - REST_DENSITY) / (safe * safe)
        q[c : c + 1, :] = jnp.where(active, value, 0.0)
        rho[c : c + 1, :] = jnp.where(active, row, 0.0)
    for r in range(RIM):
        q_head[r] = q[r : r + 1, :]
        q_tail[r] = q[cells - RIM + r : cells - RIM + r + 1, :]
    for t in range(send_q.shape[0] // SLOTS):
        for k in range(SLOTS):
            pick = jnp.maximum(sends[0, 0, k, t], 0)
            send_q[t * SLOTS + k] = q[pl.ds(pick, 1), :]


def forces(
    moves, counts, near, outs, tiles, q, rho, fluid, tab, mine, q_below, q_above, q_rest,
    moved, outbox, feat,
):
    cells, _, width = moved.shape
    moves.need(3, 4)
    sub = lax.broadcasted_iota(jnp.int32, (8, width), 0)

    for start, q_ref in segments(q_below, q, q_above, q_rest):

        def source(i, carry, start=start, q_ref=q_ref):
            tile = tiles[start + i]
            row_q = q_ref[i] if q_ref.ndim == 3 else q_ref[pl.ds(i, 1), :]
            bond = tile[7:8]
            first = jnp.where(
                sub < 3,
                tile * bond,
                jnp.where(sub == 3, bond, jnp.where(sub < 7, tile, 0.0)),
            )
            spot = jnp.where(sub < 3, tile, 1.0)
            spot = jnp.where(sub < 4, spot, row_q * pltpu.roll(spot, 4, 0))
            second = spot * (1.5 * tile[3:4])
            rows = pieces(first, 2) + pieces(second, 3) + [jnp.zeros((8, width), F32)]
            feat[start + i] = jnp.concatenate(rows, 0).astype(BF16)
            return carry

        lax.fori_loop(0, q_ref.shape[0], source, 0, unroll=4)

    lane = lax.broadcasted_iota(jnp.int32, (1, width), 1)

    def cell(c, carry):
        feats, odd, even = [], [], []
        for row, w in weigh(near, tab, mine, c):
            feats.append(feat[row])
            square = w * w
            high = square.astype(BF16)
            low = (square - high.astype(F32)).astype(BF16)
            once = w.astype(BF16)
            odd.append(jnp.concatenate([once, (square * w).astype(BF16)], 1))
            even.append(jnp.concatenate([high, low], 1))
        feats = jnp.concatenate(feats, 1)
        o13 = contract(feats[0:16], jnp.concatenate(odd, 0), 1)
        o2 = contract(feats[16:48], jnp.concatenate(even, 0), 1)
        o13 = o13[0:8] + o13[8:16]
        o2 = o2[:, :width] + o2[:, width:]
        o2 = o2[0:8] + o2[8:16] + o2[16:24]
        tile = tiles[RIM + c]
        row_rho = rho[pl.ds(c, 1), :]
        mix = q[pl.ds(c, 1), :] * o2 + pltpu.roll(o2, 4, 0) - o13[:, :width]
        speed = pltpu.roll(tile, 4, 0)
        drag = pltpu.roll(o13[:, width:], 4, 0) - speed * row_rho
        acc = tile * mix[3:4] - mix + VISCOSITY * drag
        acc = acc - jnp.where(sub == 2, GRAVITY, 0.0)
        step = TIME_STEP * fluid[pl.ds(c, 1), :]
        speed = speed + step * acc
        place = tile + step * speed
        result = jnp.where(
            sub < 3,
            place,
            jnp.where(sub < 6, pltpu.roll(speed, 3, 0), jnp.where(sub == 6, row_rho, 0.0)),
        )
        moved[c] = jnp.where(lane < counts[c], result, 0.0)
        return carry

    moves.need(*range(9))
    lax.fori_loop(0, cells, cell, 0)
    moves.save(0)
    for t in range(outbox.shape[0] // SLOTS):
        for k in range(SLOTS):
            outbox[t * SLOTS + k] = moved[outs[t, k]]


def settle(moves, kept, arrived, moved, inbox, state, density):
    cells = moved.shape[0]
    moves.need(0, 1, 2)

    def put(place, tile):
        @pl.when(place < cells)
        def _():
            for k in range(6):
                state[k, pl.ds(place, 1), :] = tile[k : k + 1]
            density[pl.ds(place, 1), :] = tile[6:7]

    for c in range(cells):
        put(kept[c], moved[c])
    for t in range(inbox.shape[0] // SLOTS):
        for k in range(SLOTS):
            put(arrived[t, k], inbox[t * SLOTS + k])


def routes(owners, cells, peers):
    me = lax.axis_index("dev")
    ids = jnp.arange(cells, dtype=jnp.int32)
    devs = jnp.arange(peers, dtype=jnp.int32)
    slots = jnp.arange(SLOTS, dtype=jnp.int32)
    per_dev = owners.reshape(peers, cells)
    arrivals = jnp.sum((per_dev == me).astype(jnp.int32), 1)
    before = jnp.sum(jnp.where(devs[None, :] < devs[:, None], arrivals[None, :], 0), 1)
    arrived = jnp.where(
        (slots[None, :] < arrivals[:, None]) & (devs[:, None] != me),
        before[:, None] + slots[None, :],
        cells,
    )
    targets = jnp.sum(jnp.where(devs[:, None] == me, per_dev, 0), 0)
    same = (targets[None, :] == targets[:, None]) & (ids[None, :] < ids[:, None])
    rank = jnp.sum(same.astype(jnp.int32), 1)
    mine = jnp.sum(jnp.where(devs < me, arrivals, 0))
    kept = jnp.where(targets == me, mine + rank, cells)
    hit = (targets[None, None, :] == devs[:, None, None]) & (
        rank[None, None, :] == slots[None, :, None]
    )
    outs = jnp.sum(jnp.where(hit, ids[None, None, :], 0), 2)
    return kept, arrived, outs


def shards(positions, velocities, masses, counts, walls, neighbours, send_cells, owners):
    cells, width = masses.shape
    peers = lax.axis_size("dev")
    total = 2 * RIM + cells + SLOTS * peers
    groups = lax.axis_size("group")
    up = [(i, i + 1) for i in range(groups - 1)]
    down = [(i + 1, i) for i in range(groups - 1)]

    def exchange(x):
        return lax.all_to_all(x, "dev", split_axis=0, concat_axis=0, tiled=True)

    kept, arrived, outs = routes(owners[0], cells, peers)
    near = neighbours.T
    sends = jnp.swapaxes(send_cells, 2, 3)
    own, send, head, tail, fluid = call(
        prepare,
        4096,
        [counts, sends],
        [positions, velocities, masses, walls],
        [],
        [
            ((cells, 8, width), F32),
            ((SLOTS * peers, 8, width), F32),
            ((RIM, 8, width), F32),
            ((RIM, 8, width), F32),
            ((cells, width), F32),
        ],
    )
    rest = exchange(send)
    below = lax.ppermute(tail, "group", up)
    above = lax.ppermute(head, "group", down)
    rho, q, q_head, q_tail, send_q, tab, mine, tiles = call(
        densities,
        4096,
        [counts, near, sends],
        [own],
        [below, above, rest],
        [
            ((cells, width), F32),
            ((cells, width), F32),
            ((RIM, 1, width), F32),
            ((RIM, 1, width), F32),
            ((SLOTS * peers, 1, width), F32),
            ((total, 48, width), BF16),
            ((cells, 48, width), BF16),
            ((total, 8, width), F32),
        ],
    )
    q_rest = exchange(send_q)
    q_below = lax.ppermute(q_tail, "group", up)
    q_above = lax.ppermute(q_head, "group", down)
    moved, outbox = call(
        forces,
        4096,
        [counts, near, outs],
        [tiles, q, rho, fluid, tab, mine],
        [q_below, q_above, q_rest],
        [((cells, 8, width), F32), ((SLOTS * peers, 8, width), F32)],
        [pltpu.VMEM((total, 48, width), BF16)],
    )
    inbox = exchange(outbox)
    return call(
        settle,
        12000,
        [kept, arrived],
        [moved],
        [inbox],
        [((6, cells, width), F32), ((cells, width), F32)],
    )


def solution(mesh):
    return jax.shard_map(
        shards,
        mesh=mesh,
        in_specs=(
            P(None, ("group", "dev"), None),
            P(None, ("group", "dev"), None),
            P(("group", "dev"), None),
            P(("group", "dev")),
            P(("group", "dev"), None),
            P(("group", "dev"), None),
            P("group", "dev", None, None),
            P("group", None),
        ),
        out_specs=(P(None, ("group", "dev"), None), P(("group", "dev"), None)),
        check_vma=False,
    )
```

```python
import jax
import jax.numpy as jnp
from jax import lax
from jax.experimental import pallas as pl
from jax.experimental.pallas import tpu as pltpu
from jax.sharding import PartitionSpec as P

RIM = 4
SLOTS = 2
MOVERS = 16
STIFFNESS = 2.0
REST_DENSITY = 0.8
VISCOSITY = 0.5
COHESION = 0.3
ADHESION = 0.8
GRAVITY = 1.0
TIME_STEP = 0.5

F32 = jnp.float32
BF16 = jnp.bfloat16
HBM = pl.BlockSpec(memory_space=pltpu.HBM)
VMEM = pl.BlockSpec(memory_space=pltpu.VMEM)


class Moves:
    def __init__(self, ins, outs):
        self.ins, self.outs = list(ins), list(outs)
        self.waited, self.saved = set(), set()
        for copy in self.ins:
            copy.start()

    def need(self, *which):
        for i in which:
            if i not in self.waited:
                self.waited.add(i)
                self.ins[i].wait()

    def save(self, *which):
        for i in which:
            if i not in self.saved:
                self.saved.add(i)
                self.outs[i].start()


def call(kernel, room, ints, held, near, outs, scratch=()):
    n_in, n_near, n_out = len(ints) + len(held), len(near), len(outs)

    def body(*refs):
        sources, refs = refs[:n_in], refs[n_in:]
        close, refs = refs[:n_near], refs[n_near:]
        targets, refs = refs[:n_out], refs[n_out:]
        inner, refs = refs[:n_in], refs[n_in:]
        results, refs = refs[:n_out], refs[n_out:]
        in_sems, out_sems, rest = refs[0], refs[1], refs[2:]
        moves = Moves(
            [pltpu.make_async_copy(a, b, in_sems.at[i]) for i, (a, b) in enumerate(zip(sources, inner))],
            [pltpu.make_async_copy(a, b, out_sems.at[i]) for i, (a, b) in enumerate(zip(results, targets))],
        )
        kernel(moves, *inner, *close, *results, *rest)
        moves.need(*range(n_in))
        moves.save(*range(n_out))
        for copy in moves.outs:
            copy.wait()

    return pl.pallas_call(
        body,
        out_shape=[jax.ShapeDtypeStruct(*o) for o in outs],
        in_specs=[HBM] * n_in + [VMEM] * n_near,
        out_specs=[HBM] * n_out,
        scratch_shapes=[pltpu.SMEM(x.shape, x.dtype) for x in ints]
        + [pltpu.VMEM(x.shape, x.dtype) for x in held]
        + [pltpu.VMEM(*o) for o in outs]
        + [pltpu.SemaphoreType.DMA((n_in,)), pltpu.SemaphoreType.DMA((n_out,))]
        + list(scratch),
        compiler_params=pltpu.CompilerParams(vmem_limit_bytes=(64 << 20) - (room << 10)),
        name=kernel.__name__,
    )(*ints, *held, *near)


def contract(a, b, dim):
    return lax.dot_general(a, b, (((dim,), (0,)), ((), ())), preferred_element_type=F32)


def pieces(value, count):
    parts = []
    for _ in range(count):
        part = value.astype(BF16).astype(F32)
        parts.append(part)
        value = value - part
    return parts


def prepare(moves, counts, sends, pos, vel, mass, walls, own, send, head, tail, fluid):
    cells, width = mass.shape
    moves.need(*range(6))
    m = mass[...]
    root = jnp.exp(jnp.log(m) * (1.0 / 3.0))
    root = root - (root * root * root - m) / (3.0 * root * root)
    wall = walls[...].astype(F32)
    bond = root * root * (COHESION + (ADHESION - COHESION) * wall)
    free = 1.0 - wall
    lane = lax.broadcasted_iota(jnp.int32, (1, width), 1)
    for c in range(cells):
        row = slice(c, c + 1)
        active = lane < counts[c]
        for k in range(3):
            own[c, k : k + 1, :] = pos[k, row, :]
            own[c, 4 + k : 5 + k, :] = vel[k, row, :]
        own[c, 3:4, :] = jnp.where(active, root[row], 0.0)
        own[c, 7:8, :] = jnp.where(active, bond[row], 0.0)
        fluid[row, :] = jnp.where(active, free[row], 0.0)
    head[...] = own[0:RIM]
    tail[...] = own[cells - RIM : cells]
    for t in range(send.shape[0] // SLOTS):
        for k in range(SLOTS):
            cell = sends[0, 0, k, t]
            tile = own[jnp.maximum(cell, 0)]
            send[t * SLOTS + k] = jnp.where(cell >= 0, tile, 0.0)


def segments(below, own, above, rest):
    start = 0
    for ref in (below, own, above, rest):
        yield start, ref
        start += ref.shape[0]


def weigh(near, tab, mine, c):
    for k in range(near.shape[0] + 1):
        row = RIM + c if k == 0 else near[k - 1, c]
        yield row, jnp.maximum(contract(tab[row], mine[c], 0), 0.0)


def densities(
    moves, counts, near, sends, own, below, above, rest, rho, q, q_head, q_tail, send_q, tab, mine, tiles,
):
    moves.need(0, 1, 2, 3)
    cells, _, width = own.shape
    sub = lax.broadcasted_iota(jnp.int32, (8, width), 0)

    def squared(tile):
        return jnp.sum(jnp.where(sub < 3, tile * tile, 0.0), axis=0, keepdims=True)

    for start, ref in segments(below, own, above, rest):

        def source(i, carry, start=start, ref=ref):
            tile = ref[i]
            root = tile[3:4]
            far = root * (1.0 - 0.25 * squared(tile))
            value = jnp.where(
                sub < 3,
                tile * (0.5 * root),
                jnp.where(sub == 3, far, jnp.where(sub == 4, -0.25 * root, 0.0)),
            )
            a, b, c = pieces(value, 3)
            tab[start + i] = jnp.concatenate([a, b, a, c, a, b], 0).astype(BF16)
            tiles[start + i] = tile
            return carry

        lax.fori_loop(0, ref.shape[0], source, 0, unroll=4)

    def target(i, carry):
        tile = own[i]
        value = jnp.where(
            sub < 3,
            tile,
            jnp.where(sub == 3, 1.0, jnp.where(sub == 4, squared(tile), 0.0)),
        )
        a, b, c = pieces(value, 3)
        mine[i] = jnp.concatenate([a, a, b, a, c, b], 0).astype(BF16)
        return carry

    lax.fori_loop(0, cells, target, 0, unroll=4)
    moves.save(5, 6, 7)

    def cell(i, carry):
        for c in (2 * i, 2 * i + 1):
            total = jnp.zeros((8, width), F32)
            for _, w in weigh(near, tab, mine, c):
                total = total + jnp.sum((w * w * w).reshape(width // 8, 8, width), axis=0)
            rho[pl.ds(c, 1), :] = jnp.sum(total, axis=0, keepdims=True)
        return carry

    lax.fori_loop(0, cells // 2, cell, 0)
    lane = lax.broadcasted_iota(jnp.int32, (1, width), 1)
    for c in range(cells):
        row = rho[c : c + 1, :]
        active = lane < counts[c]
        safe = jnp.where(active, row, 1.0)
        value = STIFFNESS * (row - REST_DENSITY) / (safe * safe)
        q[c : c + 1, :] = jnp.where(active, value, 0.0)
        rho[c : c + 1, :] = jnp.where(active, row, 0.0)
    for r in range(RIM):
        q_head[r] = q[r : r + 1, :]
        q_tail[r] = q[cells - RIM + r : cells - RIM + r + 1, :]
    for t in range(send_q.shape[0] // SLOTS):
        for k in range(SLOTS):
            pick = jnp.maximum(sends[0, 0, k, t], 0)
            send_q[t * SLOTS + k] = q[pl.ds(pick, 1), :]


def first_features(tile, sub):
    bond = tile[7:8]
    value = jnp.where(
        sub < 3,
        tile * bond,
        jnp.where(sub == 3, bond, jnp.where(sub < 7, tile, 0.0)),
    )
    return jnp.concatenate(pieces(value, 2), 0).astype(BF16)


def second_features(tile, row_q, sub):
    spot = jnp.where(sub < 3, tile, 1.0)
    spot = jnp.where(sub < 4, spot, row_q * pltpu.roll(spot, 4, 0))
    value = spot * (1.5 * tile[3:4])
    rows = pieces(value, 3) + [jnp.zeros_like(value)]
    return jnp.concatenate(rows, 0).astype(BF16)


def pair_sums(near, tab, mine, feat1, feat2, c, sub):
    feats1, feats2, odd, even = [], [], [], []
    for row, w in weigh(near, tab, mine, c):
        square = w * w
        if feat1 is not None:
            feats1.append(feat1[row])
            odd.append(jnp.concatenate([w.astype(BF16), (square * w).astype(BF16)], 1))
        if feat2 is not None:
            feats2.append(feat2[row])
            high = square.astype(BF16)
            low = (square - high.astype(F32)).astype(BF16)
            even.append(jnp.concatenate([high, low], 1))
    first = second = None
    if feat1 is not None:
        first = contract(jnp.concatenate(feats1, 1), jnp.concatenate(odd, 0), 1)
        first = first[0:8] + first[8:16]
        width = first.shape[1] // 2
        first = jnp.where(sub < 4, first[:, :width], first[:, width:])
    if feat2 is not None:
        second = contract(jnp.concatenate(feats2, 1), jnp.concatenate(even, 0), 1)
        width = second.shape[1] // 2
        second = second[:, :width] + second[:, width:]
        second = second[0:8] + second[8:16] + second[16:24]
    return first, second


def advance(first, second, tile, row_q, row_rho, row_fluid, active, sub):
    mix = row_q * second + pltpu.roll(second, 4, 0) - first
    speed = pltpu.roll(tile, 4, 0)
    drag = pltpu.roll(first, 4, 0) - speed * row_rho
    acc = tile * mix[3:4] - mix + VISCOSITY * drag
    acc = acc - jnp.where(sub == 2, GRAVITY, 0.0)
    step = TIME_STEP * row_fluid
    speed = speed + step * acc
    place = tile + step * speed
    result = jnp.where(
        sub < 3,
        place,
        jnp.where(sub < 6, pltpu.roll(speed, 3, 0), jnp.where(sub == 6, row_rho, 0.0)),
    )
    return jnp.where(active, result, 0.0)


def rows_and_lanes(width):
    return (
        lax.broadcasted_iota(jnp.int32, (8, width), 0),
        lax.broadcasted_iota(jnp.int32, (1, width), 1),
    )


def forces_early(moves, near, movers, tiles, tab, mine, early, feat1):
    sub, _ = rows_and_lanes(tiles.shape[2])
    moves.need(0, 1, 2)

    def source(i, carry):
        feat1[i] = first_features(tiles[i], sub)
        return carry

    lax.fori_loop(0, tiles.shape[0], source, 0, unroll=8)
    moves.save(1)
    moves.need(3, 4)

    def cell(i, carry):
        early[i], _ = pair_sums(near, tab, mine, feat1, None, movers[i], sub)
        return carry

    lax.fori_loop(0, early.shape[0], cell, 0)


def forces_late(
    moves, counts, near, movers, outs, tiles, q, rho, fluid, tab, mine, early, q_below, q_above, q_rest,
    outbox, feat2, moved,
):
    sub, lane = rows_and_lanes(tiles.shape[2])
    moves.need(4, 5)
    for start, q_ref in segments(q_below, q, q_above, q_rest):

        def source(i, carry, start=start, q_ref=q_ref):
            row_q = q_ref[i] if q_ref.ndim == 3 else q_ref[pl.ds(i, 1), :]
            feat2[start + i] = second_features(tiles[start + i], row_q, sub)
            return carry

        lax.fori_loop(0, q_ref.shape[0], source, 0, unroll=4)

    moves.save(1)
    moves.need(*range(11))

    def cell(i, carry):
        c = movers[i]
        _, second = pair_sums(near, tab, mine, None, feat2, c, sub)
        row = pl.ds(c, 1)
        moved[i] = advance(
            early[i], second, tiles[RIM + c], q[row, :], rho[row, :], fluid[row, :], lane < counts[c], sub
        )
        return carry

    lax.fori_loop(0, early.shape[0], cell, 0)
    for t in range(outbox.shape[0] // SLOTS):
        for k in range(SLOTS):
            outbox[t * SLOTS + k] = moved[outs[t, k]]


def forces_staying(
    moves, counts, near, stayers, tiles, q, rho, fluid, tab, mine, feat1, feat2, stayed
):
    sub, lane = rows_and_lanes(tiles.shape[2])
    moves.need(*range(11))

    def cell(i, carry):
        c = stayers[i]
        first, second = pair_sums(near, tab, mine, feat1, feat2, c, sub)
        row = pl.ds(c, 1)
        stayed[i] = advance(
            first, second, tiles[RIM + c], q[row, :], rho[row, :], fluid[row, :], lane < counts[c], sub
        )
        return carry

    lax.fori_loop(0, stayed.shape[0], cell, 0)


def settle(moves, first, arrived, stayed, inbox, state, density):
    cells = state.shape[1]
    moves.need(0, 1, 2)

    def put(place, tile):
        for k in range(6):
            state[k, pl.ds(place, 1), :] = tile[k : k + 1]
        density[pl.ds(place, 1), :] = tile[6:7]

    for i in range(stayed.shape[0]):
        put(first[0] + i, stayed[i])
    for t in range(inbox.shape[0] // SLOTS):

        @pl.when(arrived[t] < cells)
        def _():
            for k in range(SLOTS):
                put(arrived[t] + k, inbox[t * SLOTS + k])


def routes(owners, cells, peers):
    me = lax.axis_index("dev")
    ids = jnp.arange(cells, dtype=jnp.int32)
    devs = jnp.arange(peers, dtype=jnp.int32)
    slots = jnp.arange(SLOTS, dtype=jnp.int32)
    halves = jnp.arange(MOVERS, dtype=jnp.int32)
    per_dev = owners.reshape(peers, cells)
    arrivals = jnp.sum((per_dev == me).astype(jnp.int32), 1)
    before = jnp.sum(jnp.where(devs[None, :] < devs[:, None], arrivals[None, :], 0), 1)
    arrived = jnp.where((arrivals > 0) & (devs != me), before, cells)
    first = jnp.sum(jnp.where(devs == me, before, 0)).reshape(1)
    targets = jnp.sum(jnp.where(devs[:, None] == me, per_dev, 0), 0)
    earlier = ids[None, :] < ids[:, None]
    rank = jnp.sum(((targets[None, :] == targets[:, None]) & earlier).astype(jnp.int32), 1)
    leaves = targets != me
    order = jnp.sum(((leaves[None, :] == leaves[:, None]) & earlier).astype(jnp.int32), 1)
    spot = order[None, :] == halves[:, None]
    movers = jnp.sum(jnp.where(spot & leaves[None, :], ids[None, :], 0), 1)
    stayers = jnp.sum(jnp.where(spot & ~leaves[None, :], ids[None, :], 0), 1)
    hit = (targets[None, None, :] == devs[:, None, None]) & (
        rank[None, None, :] == slots[None, :, None]
    )
    hit = hit & (devs != me)[:, None, None]
    outs = jnp.sum(jnp.where(hit, order[None, None, :], 0), 2)
    return first, arrived, movers, stayers, outs


def shards(positions, velocities, masses, counts, walls, neighbours, send_cells, owners):
    cells, width = masses.shape
    peers = lax.axis_size("dev")
    total = 2 * RIM + cells + SLOTS * peers
    groups = lax.axis_size("group")
    up = [(i, i + 1) for i in range(groups - 1)]
    down = [(i + 1, i) for i in range(groups - 1)]

    def exchange(x):
        return lax.all_to_all(x, "dev", split_axis=0, concat_axis=0, tiled=True)

    first, arrived, movers, stayers, outs = routes(owners[0], cells, peers)
    near = neighbours.T
    sends = jnp.swapaxes(send_cells, 2, 3)
    own, send, head, tail, fluid = call(
        prepare,
        4096,
        [counts, sends],
        [positions, velocities, masses, walls],
        [],
        [
            ((cells, 8, width), F32),
            ((SLOTS * peers, 8, width), F32),
            ((RIM, 8, width), F32),
            ((RIM, 8, width), F32),
            ((cells, width), F32),
        ],
    )
    rest = exchange(send)
    below = lax.ppermute(tail, "group", up)
    above = lax.ppermute(head, "group", down)
    rho, q, q_head, q_tail, send_q, tab, mine, tiles = call(
        densities,
        4096,
        [counts, near, sends],
        [own],
        [below, above, rest],
        [
            ((cells, width), F32),
            ((cells, width), F32),
            ((RIM, 1, width), F32),
            ((RIM, 1, width), F32),
            ((SLOTS * peers, 1, width), F32),
            ((total, 48, width), BF16),
            ((cells, 48, width), BF16),
            ((total, 8, width), F32),
        ],
    )
    q_rest = exchange(send_q)
    q_below = lax.ppermute(q_tail, "group", up)
    q_above = lax.ppermute(q_head, "group", down)
    early, feat1 = call(
        forces_early,
        4096,
        [near, movers],
        [tiles, tab, mine],
        [],
        [((MOVERS, 8, width), F32), ((total, 16, width), BF16)],
    )
    outbox, feat2 = call(
        forces_late,
        4096,
        [counts, near, movers, outs],
        [tiles, q, rho, fluid, tab, mine, early],
        [q_below, q_above, q_rest],
        [((SLOTS * peers, 8, width), F32), ((total, 32, width), BF16)],
        [pltpu.VMEM((MOVERS, 8, width), F32)],
    )
    inbox = exchange(outbox)
    [stayed] = call(
        forces_staying,
        4096,
        [counts, near, stayers],
        [tiles, q, rho, fluid, tab, mine, feat1, feat2],
        [],
        [((cells - MOVERS, 8, width), F32)],
    )
    return call(
        settle,
        12000,
        [first, arrived],
        [stayed],
        [inbox],
        [((6, cells, width), F32), ((cells, width), F32)],
    )


def solution(mesh):
    return jax.shard_map(
        shards,
        mesh=mesh,
        in_specs=(
            P(None, ("group", "dev"), None),
            P(None, ("group", "dev"), None),
            P(("group", "dev"), None),
            P(("group", "dev")),
            P(("group", "dev"), None),
            P(("group", "dev"), None),
            P("group", "dev", None, None),
            P("group", None),
        ),
        out_specs=(P(None, ("group", "dev"), None), P(("group", "dev"), None)),
        check_vma=False,
    )
```

```python
import jax
import jax.numpy as jnp
from jax import lax
from jax.experimental import pallas as pl
from jax.experimental.pallas import tpu as pltpu
from jax.sharding import PartitionSpec as P

RIM = 4
SLOTS = 2
MOVERS = 16
STEP = 8
STIFFNESS = 2.0
REST_DENSITY = 0.8
VISCOSITY = 0.5
COHESION = 0.3
ADHESION = 0.8
GRAVITY = 1.0
TIME_STEP = 0.5

F32 = jnp.float32
BF16 = jnp.bfloat16
HBM = pl.BlockSpec(memory_space=pltpu.HBM)
VMEM = pl.BlockSpec(memory_space=pltpu.VMEM)


class Moves:
    def __init__(self, ins, outs):
        self.ins, self.outs = list(ins), list(outs)
        self.waited, self.saved = set(), set()
        for copy in self.ins:
            copy.start()

    def need(self, *which):
        for i in which:
            if i not in self.waited:
                self.waited.add(i)
                self.ins[i].wait()

    def save(self, *which):
        for i in which:
            if i not in self.saved:
                self.saved.add(i)
                self.outs[i].start()


def call(kernel, room, ints, held, near, outs, scratch=()):
    n_in, n_near, n_out = len(ints) + len(held), len(near), len(outs)

    def body(*refs):
        sources, refs = refs[:n_in], refs[n_in:]
        close, refs = refs[:n_near], refs[n_near:]
        targets, refs = refs[:n_out], refs[n_out:]
        inner, refs = refs[:n_in], refs[n_in:]
        results, refs = refs[:n_out], refs[n_out:]
        in_sems, out_sems, rest = refs[0], refs[1], refs[2:]
        moves = Moves(
            [pltpu.make_async_copy(a, b, in_sems.at[i]) for i, (a, b) in enumerate(zip(sources, inner))],
            [pltpu.make_async_copy(a, b, out_sems.at[i]) for i, (a, b) in enumerate(zip(results, targets))],
        )
        kernel(moves, *inner, *close, *results, *rest)
        moves.need(*range(n_in))
        moves.save(*range(n_out))
        for copy in moves.outs:
            copy.wait()

    return pl.pallas_call(
        body,
        out_shape=[jax.ShapeDtypeStruct(*o) for o in outs],
        in_specs=[HBM] * n_in + [VMEM] * n_near,
        out_specs=[HBM] * n_out,
        scratch_shapes=[pltpu.SMEM(x.shape, x.dtype) for x in ints]
        + [pltpu.VMEM(x.shape, x.dtype) for x in held]
        + [pltpu.VMEM(*o) for o in outs]
        + [pltpu.SemaphoreType.DMA((n_in,)), pltpu.SemaphoreType.DMA((n_out,))]
        + list(scratch),
        compiler_params=pltpu.CompilerParams(vmem_limit_bytes=(64 << 20) - (room << 10)),
        name=kernel.__name__,
    )(*ints, *held, *near)


def contract(a, b, dim):
    return lax.dot_general(a, b, (((dim,), (0,)), ((), ())), preferred_element_type=F32)


def pieces(value, count):
    parts = []
    for _ in range(count):
        part = value.astype(BF16).astype(F32)
        parts.append(part)
        value = value - part
    return parts


def prepare(moves, counts, sends, pos, vel, mass, walls, own, send, head, tail, fluid):
    cells, width = mass.shape
    moves.need(*range(6))
    m = mass[...]
    root = jnp.exp(jnp.log(m) * (1.0 / 3.0))
    root = root - (root * root * root - m) / (3.0 * root * root)
    wall = walls[...].astype(F32)
    bond = root * root * (COHESION + (ADHESION - COHESION) * wall)
    free = 1.0 - wall
    lane = lax.broadcasted_iota(jnp.int32, (1, width), 1)
    for c in range(cells):
        row = slice(c, c + 1)
        active = lane < counts[c]
        for k in range(3):
            own[c, k : k + 1, :] = pos[k, row, :]
            own[c, 4 + k : 5 + k, :] = vel[k, row, :]
        own[c, 3:4, :] = jnp.where(active, root[row], 0.0)
        own[c, 7:8, :] = jnp.where(active, bond[row], 0.0)
        fluid[row, :] = jnp.where(active, free[row], 0.0)
    head[...] = own[0:RIM]
    tail[...] = own[cells - RIM : cells]
    for t in range(send.shape[0] // SLOTS):
        for k in range(SLOTS):
            cell = sends[0, 0, k, t]
            tile = own[jnp.maximum(cell, 0)]
            send[t * SLOTS + k] = jnp.where(cell >= 0, tile, 0.0)


def segments(below, own, above, rest):
    start = 0
    for ref in (below, own, above, rest):
        yield start, ref
        start += ref.shape[0]


def weigh(near, tab, mine, c):
    for k in range(near.shape[0] + 1):
        row = RIM + c if k == 0 else near[k - 1, c]
        yield row, jnp.maximum(contract(tab[row], mine[c], 0), 0.0)


def densities(
    moves, counts, near, sends, own, below, above, rest, rho, q, q_head, q_tail, send_q, tab, mine, tiles,
):
    moves.need(0, 1, 2, 3)
    cells, _, width = own.shape
    sub = lax.broadcasted_iota(jnp.int32, (8, width), 0)

    def squared(tile):
        return jnp.sum(jnp.where(sub < 3, tile * tile, 0.0), axis=0, keepdims=True)

    for start, ref in segments(below, own, above, rest):

        def source(i, carry, start=start, ref=ref):
            tile = ref[i]
            root = tile[3:4]
            far = root * (1.0 - 0.25 * squared(tile))
            value = jnp.where(
                sub < 3,
                tile * (0.5 * root),
                jnp.where(sub == 3, far, jnp.where(sub == 4, -0.25 * root, 0.0)),
            )
            a, b, c = pieces(value, 3)
            tab[start + i] = jnp.concatenate([a, b, a, c, a, b], 0).astype(BF16)
            tiles[start + i] = tile
            return carry

        lax.fori_loop(0, ref.shape[0], source, 0, unroll=4)

    def target(i, carry):
        tile = own[i]
        value = jnp.where(
            sub < 3,
            tile,
            jnp.where(sub == 3, 1.0, jnp.where(sub == 4, squared(tile), 0.0)),
        )
        a, b, c = pieces(value, 3)
        mine[i] = jnp.concatenate([a, a, b, a, c, b], 0).astype(BF16)
        return carry

    lax.fori_loop(0, cells, target, 0, unroll=4)
    moves.save(5, 6, 7)

    def cell(i, carry):
        for c in [STEP * i + k for k in range(STEP)]:
            total = jnp.zeros((8, width), F32)
            for _, w in weigh(near, tab, mine, c):
                total = total + jnp.sum((w * w * w).reshape(width // 8, 8, width), axis=0)
            rho[pl.ds(c, 1), :] = jnp.sum(total, axis=0, keepdims=True)
        return carry

    lax.fori_loop(0, cells // STEP, cell, 0)
    lane = lax.broadcasted_iota(jnp.int32, (1, width), 1)
    for c in range(cells):
        row = rho[c : c + 1, :]
        active = lane < counts[c]
        safe = jnp.where(active, row, 1.0)
        value = STIFFNESS * (row - REST_DENSITY) / (safe * safe)
        q[c : c + 1, :] = jnp.where(active, value, 0.0)
        rho[c : c + 1, :] = jnp.where(active, row, 0.0)
    for r in range(RIM):
        q_head[r] = q[r : r + 1, :]
        q_tail[r] = q[cells - RIM + r : cells - RIM + r + 1, :]
    for t in range(send_q.shape[0] // SLOTS):
        for k in range(SLOTS):
            pick = jnp.maximum(sends[0, 0, k, t], 0)
            send_q[t * SLOTS + k] = q[pl.ds(pick, 1), :]


def first_features(tile, sub):
    bond = tile[7:8]
    value = jnp.where(
        sub < 3,
        tile * bond,
        jnp.where(sub == 3, bond, jnp.where(sub < 7, tile, 0.0)),
    )
    return jnp.concatenate(pieces(value, 2), 0).astype(BF16)


def second_features(tile, row_q, sub):
    spot = jnp.where(sub < 3, tile, 1.0)
    spot = jnp.where(sub < 4, spot, row_q * pltpu.roll(spot, 4, 0))
    value = spot * (1.5 * tile[3:4])
    rows = pieces(value, 3) + [jnp.zeros_like(value)]
    return jnp.concatenate(rows, 0).astype(BF16)


class Pairs:
    def __init__(self, near, tab, mine, feat1, feat2):
        self.near, self.tab, self.mine, self.feat1, self.feat2 = near, tab, mine, feat1, feat2

    def row(self, c, k):
        return RIM + c if k == 0 else self.near[k - 1, c]

    def make(self, c, k, part, odd, even):
        width = odd.shape[1] // 2
        half = width // 2
        source = self.tab[self.row(c, k), :, part * half : part * half + half]
        w = jnp.maximum(contract(source, self.mine[c], 0), 0.0)
        square = w * w
        once, high = w.astype(BF16), square.astype(BF16)
        rows = slice(k * width + part * half, k * width + part * half + half)
        odd[rows, :width] = once
        odd[rows, width:] = once * high
        even[rows, :width] = high
        even[rows, width:] = (square - high.astype(F32)).astype(BF16)

    def fill(self, c, odd, even):
        for k in range(self.near.shape[0] + 1):
            self.make(c, k, 0, odd, even)
            self.make(c, k, 1, odd, even)

    def step(self, c, odd, even, later, next_odd, next_even, sub):
        width = odd.shape[1] // 2
        first = second = 0.0
        for k in range(self.near.shape[0] + 1):
            row = self.row(c, k)
            rows = slice(k * width, k * width + width)
            self.make(later, k, 0, next_odd, next_even)
            first = first + contract(self.feat1[row], odd[rows], 1)
            self.make(later, k, 1, next_odd, next_even)
            second = second + contract(self.feat2[row], even[rows], 1)
        first = first[0:8] + first[8:16]
        first = jnp.where(sub < 4, first[:, :width], first[:, width:])
        second = second[:, :width] + second[:, width:]
        return first, second[0:8] + second[8:16] + second[16:24]


def sweep(pairs, order, count, buffers, finish, sub):
    a, b = buffers[0:2], buffers[2:4]
    pairs.fill(order[0], *a)

    def two(t, carry):
        for i, now, then in ((2 * t, a, b), (2 * t + 1, b, a)):
            c = order[i]
            later = order[jnp.minimum(i + 1, count - 1)]
            finish(i, c, *pairs.step(c, *now, later, *then, sub))
        return carry

    lax.fori_loop(0, count // 2, two, 0)


def advance(first, second, tile, row_q, row_rho, row_fluid, active, sub):
    mix = row_q * second + pltpu.roll(second, 4, 0) - first
    speed = pltpu.roll(tile, 4, 0)
    drag = pltpu.roll(first, 4, 0) - speed * row_rho
    acc = tile * mix[3:4] - mix + VISCOSITY * drag
    acc = acc - jnp.where(sub == 2, GRAVITY, 0.0)
    step = TIME_STEP * row_fluid
    speed = speed + step * acc
    place = tile + step * speed
    result = jnp.where(
        sub < 3,
        place,
        jnp.where(sub < 6, pltpu.roll(speed, 3, 0), jnp.where(sub == 6, row_rho, 0.0)),
    )
    return jnp.where(active, result, 0.0)


def rows_and_lanes(width):
    return (
        lax.broadcasted_iota(jnp.int32, (8, width), 0),
        lax.broadcasted_iota(jnp.int32, (1, width), 1),
    )


def forces_moving(
    moves, counts, near, movers, outs, tiles, q, rho, fluid, tab, mine, q_below, q_above, q_rest,
    outbox, feat1, feat2, moved, *buffers,
):
    sub, lane = rows_and_lanes(tiles.shape[2])
    moves.need(4, 5)
    for start, q_ref in segments(q_below, q, q_above, q_rest):

        def source(i, carry, start=start, q_ref=q_ref):
            row_q = q_ref[i] if q_ref.ndim == 3 else q_ref[pl.ds(i, 1), :]
            tile = tiles[start + i]
            feat1[start + i] = first_features(tile, sub)
            feat2[start + i] = second_features(tile, row_q, sub)
            return carry

        lax.fori_loop(0, q_ref.shape[0], source, 0, unroll=4)

    moves.save(1, 2)
    moves.need(*range(10))

    def finish(i, c, first, second):
        row = pl.ds(c, 1)
        moved[i] = advance(
            first, second, tiles[RIM + c], q[row, :], rho[row, :], fluid[row, :], lane < counts[c], sub
        )

    sweep(Pairs(near, tab, mine, feat1, feat2), movers, MOVERS, buffers, finish, sub)
    for t in range(outbox.shape[0] // SLOTS):
        for k in range(SLOTS):
            outbox[t * SLOTS + k] = moved[outs[t, k]]


def forces_staying(
    moves, counts, near, stayers, tiles, q, rho, fluid, tab, mine, feat1, feat2, stayed, *buffers
):
    sub, lane = rows_and_lanes(tiles.shape[2])
    moves.need(*range(11))

    def finish(i, c, first, second):
        row = pl.ds(c, 1)
        stayed[i] = advance(
            first, second, tiles[RIM + c], q[row, :], rho[row, :], fluid[row, :], lane < counts[c], sub
        )

    sweep(Pairs(near, tab, mine, feat1, feat2), stayers, stayed.shape[0], buffers, finish, sub)


def settle(moves, first, arrived, stayed, inbox, state, density):
    cells = state.shape[1]
    moves.need(0, 1, 2)

    def put(place, tile):
        for k in range(6):
            state[k, pl.ds(place, 1), :] = tile[k : k + 1]
        density[pl.ds(place, 1), :] = tile[6:7]

    for i in range(stayed.shape[0]):
        put(first[0] + i, stayed[i])
    for t in range(inbox.shape[0] // SLOTS):

        @pl.when(arrived[t] < cells)
        def _():
            for k in range(SLOTS):
                put(arrived[t] + k, inbox[t * SLOTS + k])


def routes(owners, cells, peers):
    me = lax.axis_index("dev")
    ids = jnp.arange(cells, dtype=jnp.int32)
    devs = jnp.arange(peers, dtype=jnp.int32)
    slots = jnp.arange(SLOTS, dtype=jnp.int32)
    halves = jnp.arange(MOVERS, dtype=jnp.int32)
    per_dev = owners.reshape(peers, cells)
    arrivals = jnp.sum((per_dev == me).astype(jnp.int32), 1)
    before = jnp.sum(jnp.where(devs[None, :] < devs[:, None], arrivals[None, :], 0), 1)
    arrived = jnp.where((arrivals > 0) & (devs != me), before, cells)
    first = jnp.sum(jnp.where(devs == me, before, 0)).reshape(1)
    targets = jnp.sum(jnp.where(devs[:, None] == me, per_dev, 0), 0)
    earlier = ids[None, :] < ids[:, None]
    rank = jnp.sum(((targets[None, :] == targets[:, None]) & earlier).astype(jnp.int32), 1)
    leaves = targets != me
    order = jnp.sum(((leaves[None, :] == leaves[:, None]) & earlier).astype(jnp.int32), 1)
    spot = order[None, :] == halves[:, None]
    movers = jnp.sum(jnp.where(spot & leaves[None, :], ids[None, :], 0), 1)
    stayers = jnp.sum(jnp.where(spot & ~leaves[None, :], ids[None, :], 0), 1)
    hit = (targets[None, None, :] == devs[:, None, None]) & (
        rank[None, None, :] == slots[None, :, None]
    )
    hit = hit & (devs != me)[:, None, None]
    outs = jnp.sum(jnp.where(hit, order[None, None, :], 0), 2)
    return first, arrived, movers, stayers, outs


def shards(positions, velocities, masses, counts, walls, neighbours, send_cells, owners):
    cells, width = masses.shape
    peers = lax.axis_size("dev")
    total = 2 * RIM + cells + SLOTS * peers
    groups = lax.axis_size("group")
    up = [(i, i + 1) for i in range(groups - 1)]
    down = [(i + 1, i) for i in range(groups - 1)]

    def exchange(x):
        return lax.all_to_all(x, "dev", split_axis=0, concat_axis=0, tiled=True)

    first, arrived, movers, stayers, outs = routes(owners[0], cells, peers)
    near = neighbours.T
    sends = jnp.swapaxes(send_cells, 2, 3)
    own, send, head, tail, fluid = call(
        prepare,
        4096,
        [counts, sends],
        [positions, velocities, masses, walls],
        [],
        [
            ((cells, 8, width), F32),
            ((SLOTS * peers, 8, width), F32),
            ((RIM, 8, width), F32),
            ((RIM, 8, width), F32),
            ((cells, width), F32),
        ],
    )
    rest = exchange(send)
    below = lax.ppermute(tail, "group", up)
    above = lax.ppermute(head, "group", down)
    rho, q, q_head, q_tail, send_q, tab, mine, tiles = call(
        densities,
        4096,
        [counts, near, sends],
        [own],
        [below, above, rest],
        [
            ((cells, width), F32),
            ((cells, width), F32),
            ((RIM, 1, width), F32),
            ((RIM, 1, width), F32),
            ((SLOTS * peers, 1, width), F32),
            ((total, 48, width), BF16),
            ((cells, 48, width), BF16),
            ((total, 8, width), F32),
        ],
    )
    q_rest = exchange(send_q)
    q_below = lax.ppermute(q_tail, "group", up)
    q_above = lax.ppermute(q_head, "group", down)
    partners = neighbours.shape[1] + 1
    buffers = [pltpu.VMEM((partners * width, 2 * width), BF16)] * 4
    outbox, feat1, feat2 = call(
        forces_moving,
        4096,
        [counts, near, movers, outs],
        [tiles, q, rho, fluid, tab, mine],
        [q_below, q_above, q_rest],
        [
            ((SLOTS * peers, 8, width), F32),
            ((total, 16, width), BF16),
            ((total, 32, width), BF16),
        ],
        [pltpu.VMEM((MOVERS, 8, width), F32)] + buffers,
    )
    inbox = exchange(outbox)
    [stayed] = call(
        forces_staying,
        4096,
        [counts, near, stayers],
        [tiles, q, rho, fluid, tab, mine, feat1, feat2],
        [],
        [((cells - MOVERS, 8, width), F32)],
        buffers,
    )
    return call(
        settle,
        12000,
        [first, arrived],
        [stayed],
        [inbox],
        [((6, cells, width), F32), ((cells, width), F32)],
    )


def solution(mesh):
    return jax.shard_map(
        shards,
        mesh=mesh,
        in_specs=(
            P(None, ("group", "dev"), None),
            P(None, ("group", "dev"), None),
            P(("group", "dev"), None),
            P(("group", "dev")),
            P(("group", "dev"), None),
            P(("group", "dev"), None),
            P("group", "dev", None, None),
            P("group", None),
        ),
        out_specs=(P(None, ("group", "dev"), None), P(("group", "dev"), None)),
        check_vma=False,
    )
```

```python
import jax
import jax.numpy as jnp
from jax import lax
from jax.experimental import pallas as pl
from jax.experimental.pallas import tpu as pltpu
from jax.sharding import PartitionSpec as P

RIM = 4
SLOTS = 2
MOVERS = 16
STEP = 8
JOB_ROW, JOB_CELL, JOB_COUNT, MOVING, STAYING, OUTS, PLAN = 0, 128, 256, 272, 304, 336, 512
STIFFNESS = 2.0
REST_DENSITY = 0.8
VISCOSITY = 0.5
COHESION = 0.3
ADHESION = 0.8
GRAVITY = 1.0
TIME_STEP = 0.5

F32 = jnp.float32
BF16 = jnp.bfloat16
HBM = pl.BlockSpec(memory_space=pltpu.HBM)
VMEM = pl.BlockSpec(memory_space=pltpu.VMEM)


class Moves:
    def __init__(self, ins, outs):
        self.ins, self.outs = list(ins), list(outs)
        self.waited, self.saved = set(), set()
        for copy in self.ins:
            copy.start()

    def need(self, *which):
        for i in which:
            if i not in self.waited:
                self.waited.add(i)
                self.ins[i].wait()

    def save(self, *which):
        for i in which:
            if i not in self.saved:
                self.saved.add(i)
                self.outs[i].start()


def call(kernel, room, ints, held, near, outs, scratch=(), into=()):
    n_in, n_near, n_out = len(ints) + len(held), len(near), len(outs)

    def body(*refs):
        sources, refs = refs[:n_in], refs[n_in:]
        close, refs = refs[:n_near], refs[n_near:]
        targets, refs = refs[:n_out], refs[n_out:]
        inner, refs = list(refs[: n_in - len(into)]), refs[n_in - len(into) :]
        results, refs = refs[:n_out], refs[n_out:]
        for i, (out, start) in enumerate(into):
            rows = pl.ds(start, held[i].shape[0])
            inner.insert(len(ints) + i, results[out].at[rows])
        in_sems, out_sems, rest = refs[0], refs[1], refs[2:]
        moves = Moves(
            [pltpu.make_async_copy(a, b, in_sems.at[i]) for i, (a, b) in enumerate(zip(sources, inner))],
            [pltpu.make_async_copy(a, b, out_sems.at[i]) for i, (a, b) in enumerate(zip(results, targets))],
        )
        kernel(moves, *inner, *close, *results, *rest)
        moves.need(*range(n_in))
        moves.save(*range(n_out))
        for copy in moves.outs:
            copy.wait()

    return pl.pallas_call(
        body,
        out_shape=[jax.ShapeDtypeStruct(*o) for o in outs],
        in_specs=[HBM] * n_in + [VMEM] * n_near,
        out_specs=[HBM] * n_out,
        scratch_shapes=[pltpu.SMEM(x.shape, x.dtype) for x in ints]
        + [pltpu.VMEM(x.shape, x.dtype) for x in held[len(into) :]]
        + [(pltpu.SMEM if len(o[0]) == 1 else pltpu.VMEM)(*o) for o in outs]
        + [pltpu.SemaphoreType.DMA((n_in,)), pltpu.SemaphoreType.DMA((n_out,))]
        + list(scratch),
        compiler_params=pltpu.CompilerParams(vmem_limit_bytes=(64 << 20) - (room << 10)),
        name=kernel.__name__,
    )(*ints, *held, *near)


def contract(a, b, dim):
    return lax.dot_general(a, b, (((dim,), (0,)), ((), ())), preferred_element_type=F32)


def pieces(value, count):
    parts = []
    for _ in range(count):
        part = value.astype(BF16).astype(F32)
        parts.append(part)
        value = value - part
    return parts


def prepare(moves, counts, sends, pos, vel, mass, walls, own, send, head, tail, fluid):
    cells, width = mass.shape
    moves.need(*range(6))
    m = mass[...]
    root = jnp.exp(jnp.log(m) * (1.0 / 3.0))
    root = root - (root * root * root - m) / (3.0 * root * root)
    wall = walls[...].astype(F32)
    bond = root * root * (COHESION + (ADHESION - COHESION) * wall)
    free = 1.0 - wall
    lane = lax.broadcasted_iota(jnp.int32, (1, width), 1)
    for c in range(cells):
        row = slice(c, c + 1)
        active = lane < counts[c]
        for k in range(3):
            own[c, k : k + 1, :] = pos[k, row, :]
            own[c, 4 + k : 5 + k, :] = vel[k, row, :]
        own[c, 3:4, :] = jnp.where(active, root[row], 0.0)
        own[c, 7:8, :] = jnp.where(active, bond[row], 0.0)
        fluid[row, :] = jnp.where(active, free[row], 0.0)
    head[...] = own[0:RIM]
    tail[...] = own[cells - RIM : cells]
    for t in range(send.shape[0] // SLOTS):
        for k in range(SLOTS):
            cell = sends[0, 0, k, t]
            tile = own[jnp.maximum(cell, 0)]
            send[t * SLOTS + k] = jnp.where(cell >= 0, tile, 0.0)


def segments(below, own, above, rest):
    start = 0
    for ref in (below, own, above, rest):
        yield start, ref
        start += ref.shape[0]


def squared(tile, sub):
    return jnp.sum(jnp.where(sub < 3, tile * tile, 0.0), axis=0, keepdims=True)


def source_rows(tile, sub):
    root = tile[3:4]
    far = root * (1.0 - 0.25 * squared(tile, sub))
    value = jnp.where(
        sub < 3,
        tile * (0.5 * root),
        jnp.where(sub == 3, far, jnp.where(sub == 4, -0.25 * root, 0.0)),
    )
    a, b, c = pieces(value, 3)
    return jnp.concatenate([a, b, a, c, a, b], 0).astype(BF16)


def target_rows(tile, sub):
    value = jnp.where(
        sub < 3,
        tile,
        jnp.where(sub == 3, 1.0, jnp.where(sub == 4, squared(tile, sub), 0.0)),
    )
    a, b, c = pieces(value, 3)
    return jnp.concatenate([a, a, b, a, c, b], 0).astype(BF16)


def cubes(source, target):
    w = jnp.maximum(contract(source, target, 0), 0.0)
    return jnp.sum((w * w * w).reshape(w.shape[0] // 8, 8, w.shape[1]), axis=0)


def run_jobs(rows, cells, count, tab, first_row, mine, sums):
    last = mine.shape[0] - 1

    def some(t, carry):
        for k in range(STEP):
            c = cells(t * STEP + k)
            value = cubes(tab[rows(t * STEP + k) - first_row], mine[jnp.minimum(c, last)])
            sums[c] = sums[c] + value
        return carry

    lax.fori_loop(0, lax.div(count + (STEP - 1), STEP), some, 0)


def home(moves, near, owners, tiles, owners_v, sums, tab, mine, plan, landing, jobs, seen):
    cells, _, width = tiles.shape
    sub, _ = rows_and_lanes(width)
    me = lax.axis_index("dev")
    moves.need(0, 2)

    def build(i, carry):
        tab[i] = source_rows(tiles[i], sub)
        mine[i] = target_rows(tiles[i], sub)
        return carry

    lax.fori_loop(0, cells, build, 0, unroll=4)
    moves.save(1, 2)

    def alone(t, carry):
        for k in range(STEP):
            c = t * STEP + k
            sums[c] = cubes(tab[c], mine[c])
        return carry

    lax.fori_loop(0, cells // STEP, alone, 0)
    sums[cells] = jnp.zeros((8, width), F32)
    local, away = jnp.int32(0), jnp.int32(0)
    for k in range(near.shape[0]):
        for c in range(cells):
            row = near[k, c]
            inside = (row >= RIM) & (row < RIM + cells)
            jobs[local] = row
            jobs[128 + local] = c
            plan[JOB_ROW + away] = row
            plan[JOB_CELL + away] = c
            local = local + inside.astype(jnp.int32)
            away = away + 1 - inside.astype(jnp.int32)
    for k in range(STEP):
        jobs[local + k] = RIM
        jobs[128 + local + k] = cells
        plan[JOB_ROW + away + k] = RIM
        plan[JOB_CELL + away + k] = cells
    plan[JOB_COUNT] = away
    run_jobs(lambda i: jobs[i], lambda i: jobs[128 + i], local, tab, RIM, mine, sums)
    moves.save(0)

    moves.need(1, 3)
    for d in range(seen.shape[0]):
        seen[d] = 0
    for i in range(seen.shape[0] * SLOTS):
        plan[OUTS + i] = 0
    moving, staying = jnp.int32(0), jnp.int32(0)
    for c in range(cells):
        to = owners[0, me * cells + c]
        leaves = (to != me).astype(jnp.int32)
        plan[MOVING + moving] = c
        plan[STAYING + staying] = c
        spot = jnp.where(to != me, to * SLOTS + seen[to], seen.shape[0] * SLOTS)
        plan[OUTS + spot] = moving
        seen[to] = seen[to] + leaves
        moving = moving + leaves
        staying = staying + 1 - leaves
    moves.save(3)
    entries = owners_v.shape[1]
    dev = lax.broadcasted_iota(jnp.int32, (entries, 128), 1)
    entry = lax.broadcasted_iota(jnp.int32, (entries, 128), 0)
    belongs = (entry >= dev * cells) & (entry < dev * cells + cells)
    ours = jnp.broadcast_to((owners_v[...] == me).astype(F32), (8, entries)).astype(BF16)
    arrivals = contract(ours, jnp.where(belongs, 1.0, 0.0).astype(BF16), 1)
    earlier = lax.broadcasted_iota(jnp.int32, (128, 128), 0) < lax.broadcasted_iota(
        jnp.int32, (128, 128), 1
    )
    before = contract(arrivals.astype(BF16), jnp.where(earlier, 1.0, 0.0).astype(BF16), 1)
    lane = lax.broadcasted_iota(jnp.int32, (8, 128), 1)
    kind = lax.broadcasted_iota(jnp.int32, (8, 128), 0)
    place = before.astype(jnp.int32)
    comes = (arrivals > 0.0) & (lane != me)
    landing[...] = jnp.where((kind == 0) & ~comes, cells, place)


def densities(
    moves, counts, plan, sends, tab_own, tiles_own, mine, sums, below, above, rest,
    rho, q, q_head, q_tail, send_q, tab, tiles,
):
    cells, _, width = mine.shape
    sub, lane = rows_and_lanes(width)
    for start, ref in ((0, below), (RIM + cells, above), (2 * RIM + cells, rest)):

        def source(i, carry, start=start, ref=ref):
            tile = ref[i]
            tab[start + i] = source_rows(tile, sub)
            tiles[start + i] = tile
            return carry

        lax.fori_loop(0, ref.shape[0], source, 0, unroll=4)

    moves.need(*range(7))
    moves.save(5, 6)
    run_jobs(
        lambda i: plan[JOB_ROW + i], lambda i: plan[JOB_CELL + i], plan[JOB_COUNT], tab, 0, mine, sums
    )
    for c in range(cells):
        row = jnp.sum(sums[c], axis=0, keepdims=True)
        active = lane < counts[c]
        safe = jnp.where(active, row, 1.0)
        value = STIFFNESS * (row - REST_DENSITY) / (safe * safe)
        q[c : c + 1, :] = jnp.where(active, value, 0.0)
        rho[c : c + 1, :] = jnp.where(active, row, 0.0)
    for r in range(RIM):
        q_head[r] = q[r : r + 1, :]
        q_tail[r] = q[cells - RIM + r : cells - RIM + r + 1, :]
    for t in range(send_q.shape[0] // SLOTS):
        for k in range(SLOTS):
            pick = jnp.maximum(sends[0, 0, k, t], 0)
            send_q[t * SLOTS + k] = q[pl.ds(pick, 1), :]


def first_features(tile, sub):
    bond = tile[7:8]
    value = jnp.where(
        sub < 3,
        tile * bond,
        jnp.where(sub == 3, bond, jnp.where(sub < 7, tile, 0.0)),
    )
    return jnp.concatenate(pieces(value, 2), 0).astype(BF16)


def second_features(tile, row_q, sub):
    spot = jnp.where(sub < 3, tile, 1.0)
    spot = jnp.where(sub < 4, spot, row_q * pltpu.roll(spot, 4, 0))
    value = spot * (1.5 * tile[3:4])
    rows = pieces(value, 3) + [jnp.zeros_like(value)]
    return jnp.concatenate(rows, 0).astype(BF16)


class Pairs:
    def __init__(self, near, tab, mine, feat1, feat2):
        self.near, self.tab, self.mine, self.feat1, self.feat2 = near, tab, mine, feat1, feat2

    def row(self, c, k):
        return RIM + c if k == 0 else self.near[k - 1, c]

    def make(self, c, k, part, odd, even):
        width = odd.shape[1] // 2
        half = width // 2
        source = self.tab[self.row(c, k), :, part * half : part * half + half]
        w = jnp.maximum(contract(source, self.mine[c], 0), 0.0)
        square = w * w
        once, high = w.astype(BF16), square.astype(BF16)
        rows = slice(k * width + part * half, k * width + part * half + half)
        odd[rows, :width] = once
        odd[rows, width:] = once * high
        even[rows, :width] = high
        even[rows, width:] = (square - high.astype(F32)).astype(BF16)

    def fill(self, c, odd, even):
        for k in range(self.near.shape[0] + 1):
            self.make(c, k, 0, odd, even)
            self.make(c, k, 1, odd, even)

    def step(self, c, odd, even, later, next_odd, next_even, sub):
        width = odd.shape[1] // 2
        first = second = 0.0
        for k in range(self.near.shape[0] + 1):
            row = self.row(c, k)
            rows = slice(k * width, k * width + width)
            self.make(later, k, 0, next_odd, next_even)
            first = first + contract(self.feat1[row], odd[rows], 1)
            self.make(later, k, 1, next_odd, next_even)
            second = second + contract(self.feat2[row], even[rows], 1)
        first = first[0:8] + first[8:16]
        first = jnp.where(sub < 4, first[:, :width], first[:, width:])
        second = second[:, :width] + second[:, width:]
        return first, second[0:8] + second[8:16] + second[16:24]


def sweep(pairs, order, start, count, buffers, finish, sub):
    a, b = buffers[0:2], buffers[2:4]
    pairs.fill(order[start], *a)

    def two(t, carry):
        for i, now, then in ((2 * t, a, b), (2 * t + 1, b, a)):
            c = order[start + i]
            later = order[start + jnp.minimum(i + 1, count - 1)]
            finish(i, c, *pairs.step(c, *now, later, *then, sub))
        return carry

    lax.fori_loop(0, count // 2, two, 0)


def advance(first, second, tile, row_q, row_rho, row_fluid, active, sub):
    mix = row_q * second + pltpu.roll(second, 4, 0) - first
    speed = pltpu.roll(tile, 4, 0)
    drag = pltpu.roll(first, 4, 0) - speed * row_rho
    acc = tile * mix[3:4] - mix + VISCOSITY * drag
    acc = acc - jnp.where(sub == 2, GRAVITY, 0.0)
    step = TIME_STEP * row_fluid
    speed = speed + step * acc
    place = tile + step * speed
    result = jnp.where(
        sub < 3,
        place,
        jnp.where(sub < 6, pltpu.roll(speed, 3, 0), jnp.where(sub == 6, row_rho, 0.0)),
    )
    return jnp.where(active, result, 0.0)


def rows_and_lanes(width):
    return (
        lax.broadcasted_iota(jnp.int32, (8, width), 0),
        lax.broadcasted_iota(jnp.int32, (1, width), 1),
    )


def forces_moving(
    moves, counts, near, plan, tiles, q, rho, fluid, tab, mine, q_below, q_above, q_rest,
    outbox, feat1, feat2, moved, *buffers,
):
    sub, lane = rows_and_lanes(tiles.shape[2])
    moves.need(3, 4)
    for start, q_ref in segments(q_below, q, q_above, q_rest):

        def source(i, carry, start=start, q_ref=q_ref):
            row_q = q_ref[i] if q_ref.ndim == 3 else q_ref[pl.ds(i, 1), :]
            tile = tiles[start + i]
            feat1[start + i] = first_features(tile, sub)
            feat2[start + i] = second_features(tile, row_q, sub)
            return carry

        lax.fori_loop(0, q_ref.shape[0], source, 0, unroll=4)

    moves.save(1, 2)
    moves.need(*range(9))

    def finish(i, c, first, second):
        row = pl.ds(c, 1)
        moved[i] = advance(
            first, second, tiles[RIM + c], q[row, :], rho[row, :], fluid[row, :], lane < counts[c], sub
        )

    sweep(
        Pairs(near, tab, mine, feat1, feat2), plan, MOVING, MOVERS, buffers, finish, sub
    )
    for t in range(outbox.shape[0] // SLOTS):
        for k in range(SLOTS):
            outbox[t * SLOTS + k] = moved[plan[OUTS + t * SLOTS + k]]


def forces_staying(
    moves, counts, near, plan, tiles, q, rho, fluid, tab, mine, feat1, feat2, stayed, *buffers
):
    sub, lane = rows_and_lanes(tiles.shape[2])
    moves.need(*range(11))

    def finish(i, c, first, second):
        row = pl.ds(c, 1)
        stayed[i] = advance(
            first, second, tiles[RIM + c], q[row, :], rho[row, :], fluid[row, :], lane < counts[c], sub
        )

    sweep(
        Pairs(near, tab, mine, feat1, feat2), plan, STAYING, stayed.shape[0], buffers, finish, sub
    )


def settle(moves, landing, stayed, inbox, state, density):
    cells = state.shape[1]
    me = lax.axis_index("dev")
    moves.need(0, 1)

    def put(place, tile):
        for k in range(6):
            state[k, pl.ds(place, 1), :] = tile[k : k + 1]
        density[pl.ds(place, 1), :] = tile[6:7]

    for i in range(stayed.shape[0]):
        put(landing[1, me] + i, stayed[i])
    for t in range(inbox.shape[0] // SLOTS):

        @pl.when(landing[0, t] < cells)
        def _():
            for k in range(SLOTS):
                put(landing[0, t] + k, inbox[t * SLOTS + k])


def shards(positions, velocities, masses, counts, walls, neighbours, send_cells, owners):
    cells, width = masses.shape
    peers = lax.axis_size("dev")
    total = 2 * RIM + cells + SLOTS * peers
    groups = lax.axis_size("group")
    up = [(i, i + 1) for i in range(groups - 1)]
    down = [(i + 1, i) for i in range(groups - 1)]

    def exchange(x):
        return lax.all_to_all(x, "dev", split_axis=0, concat_axis=0, tiled=True)

    near = neighbours.T
    sends = jnp.swapaxes(send_cells, 2, 3)
    own, send, head, tail, fluid = call(
        prepare,
        4096,
        [counts, sends],
        [positions, velocities, masses, walls],
        [],
        [
            ((cells, 8, width), F32),
            ((SLOTS * peers, 8, width), F32),
            ((RIM, 8, width), F32),
            ((RIM, 8, width), F32),
            ((cells, width), F32),
        ],
    )
    rest = exchange(send)
    below = lax.ppermute(tail, "group", up)
    above = lax.ppermute(head, "group", down)
    sums, tab_own, mine, plan, landing = call(
        home,
        4096,
        [near, owners],
        [own, owners],
        [],
        [
            ((cells + 1, 8, width), F32),
            ((cells, 48, width), BF16),
            ((cells, 48, width), BF16),
            ((PLAN,), jnp.int32),
            ((8, 128), jnp.int32),
        ],
        [pltpu.SMEM((256,), jnp.int32), pltpu.SMEM((peers,), jnp.int32)],
    )
    rho, q, q_head, q_tail, send_q, tab, tiles = call(
        densities,
        4096,
        [counts, plan, sends],
        [tab_own, own, mine, sums],
        [below, above, rest],
        [
            ((cells, width), F32),
            ((cells, width), F32),
            ((RIM, 1, width), F32),
            ((RIM, 1, width), F32),
            ((SLOTS * peers, 1, width), F32),
            ((total, 48, width), BF16),
            ((total, 8, width), F32),
        ],
        into=[(5, RIM), (6, RIM)],
    )
    q_rest = exchange(send_q)
    q_below = lax.ppermute(q_tail, "group", up)
    q_above = lax.ppermute(q_head, "group", down)
    partners = neighbours.shape[1] + 1
    buffers = [pltpu.VMEM((partners * width, 2 * width), BF16)] * 4
    outbox, feat1, feat2 = call(
        forces_moving,
        4096,
        [counts, near, plan],
        [tiles, q, rho, fluid, tab, mine],
        [q_below, q_above, q_rest],
        [
            ((SLOTS * peers, 8, width), F32),
            ((total, 16, width), BF16),
            ((total, 32, width), BF16),
        ],
        [pltpu.VMEM((MOVERS, 8, width), F32)] + buffers,
    )
    inbox = exchange(outbox)
    [stayed] = call(
        forces_staying,
        4096,
        [counts, near, plan],
        [tiles, q, rho, fluid, tab, mine, feat1, feat2],
        [],
        [((cells - MOVERS, 8, width), F32)],
        buffers,
    )
    return call(
        settle,
        12000,
        [landing],
        [stayed],
        [inbox],
        [((6, cells, width), F32), ((cells, width), F32)],
    )


def solution(mesh):
    return jax.shard_map(
        shards,
        mesh=mesh,
        in_specs=(
            P(None, ("group", "dev"), None),
            P(None, ("group", "dev"), None),
            P(("group", "dev"), None),
            P(("group", "dev")),
            P(("group", "dev"), None),
            P(("group", "dev"), None),
            P("group", "dev", None, None),
            P("group", None),
        ),
        out_specs=(P(None, ("group", "dev"), None), P(("group", "dev"), None)),
        check_vma=False,
    )
```

```python
import functools

import jax
import jax.numpy as jnp
from jax import lax
from jax.experimental import pallas as pl
from jax.experimental.pallas import tpu as pltpu
from jax.sharding import PartitionSpec as P

RIM = 4
SLOTS = 2
MOVERS = 16
STEP = 8
JOB_ROW, JOB_CELL, JOB_COUNT, MOVING, STAYING, OUTS, PLAN = 0, 128, 256, 272, 304, 336, 512
STIFFNESS = 2.0
REST_DENSITY = 0.8
VISCOSITY = 0.5
COHESION = 0.3
ADHESION = 0.8
GRAVITY = 1.0
TIME_STEP = 0.5

F32 = jnp.float32
BF16 = jnp.bfloat16
HBM = pl.BlockSpec(memory_space=pltpu.HBM)
VMEM = pl.BlockSpec(memory_space=pltpu.VMEM)


class Moves:
    def __init__(self, ins, outs):
        self.ins, self.outs = list(ins), list(outs)
        self.waited, self.saved = set(), set()
        for copy in self.ins:
            copy.start()

    def need(self, *which):
        for i in which:
            if i not in self.waited:
                self.waited.add(i)
                self.ins[i].wait()

    def save(self, *which):
        for i in which:
            if i not in self.saved:
                self.saved.add(i)
                self.outs[i].start()


def call(kernel, room, ints, held, near, outs, scratch=(), into=()):
    n_in, n_near, n_out = len(ints) + len(held), len(near), len(outs)

    def body(*refs):
        sources, refs = refs[:n_in], refs[n_in:]
        close, refs = refs[:n_near], refs[n_near:]
        targets, refs = refs[:n_out], refs[n_out:]
        inner, refs = list(refs[: n_in - len(into)]), refs[n_in - len(into) :]
        results, refs = refs[:n_out], refs[n_out:]
        sources = list(sources)
        for i, (out, start, count) in enumerate(into):
            target = (*results, *refs[2:])[out]
            inner.insert(len(ints) + i, target.at[pl.ds(start, count)])
            sources[len(ints) + i] = sources[len(ints) + i].at[pl.ds(0, count)]
        in_sems, out_sems, rest = refs[0], refs[1], refs[2:]
        moves = Moves(
            [pltpu.make_async_copy(a, b, in_sems.at[i]) for i, (a, b) in enumerate(zip(sources, inner))],
            [pltpu.make_async_copy(a, b, out_sems.at[i]) for i, (a, b) in enumerate(zip(results, targets))],
        )
        kernel(moves, *inner, *close, *results, *rest)
        moves.need(*range(n_in))
        moves.save(*range(n_out))
        for copy in moves.outs:
            copy.wait()

    return pl.pallas_call(
        body,
        out_shape=[jax.ShapeDtypeStruct(*o) for o in outs],
        in_specs=[HBM] * n_in + [VMEM] * n_near,
        out_specs=[HBM] * n_out,
        scratch_shapes=[pltpu.SMEM(x.shape, x.dtype) for x in ints]
        + [pltpu.VMEM(x.shape, x.dtype) for x in held[len(into) :]]
        + [(pltpu.SMEM if len(o[0]) == 1 else pltpu.VMEM)(*o) for o in outs]
        + [pltpu.SemaphoreType.DMA((n_in,)), pltpu.SemaphoreType.DMA((n_out,))]
        + list(scratch),
        compiler_params=pltpu.CompilerParams(vmem_limit_bytes=(64 << 20) - (room << 10)),
        name=getattr(kernel, "func", kernel).__name__,
    )(*ints, *held, *near)


def contract(a, b, dim):
    return lax.dot_general(a, b, (((dim,), (0,)), ((), ())), preferred_element_type=F32)


def pieces(value, count):
    parts = []
    for _ in range(count):
        part = value.astype(BF16).astype(F32)
        parts.append(part)
        value = value - part
    return parts


def prepare(moves, counts, sends, pos, vel, mass, walls, own, send, head, tail, fluid):
    cells, width = mass.shape
    moves.need(*range(6))
    m = mass[...]
    root = jnp.exp(jnp.log(m) * (1.0 / 3.0))
    root = root - (root * root * root - m) / (3.0 * root * root)
    wall = walls[...].astype(F32)
    bond = root * root * (COHESION + (ADHESION - COHESION) * wall)
    free = 1.0 - wall
    lane = lax.broadcasted_iota(jnp.int32, (1, width), 1)
    for c in range(cells):
        row = slice(c, c + 1)
        active = lane < counts[c]
        for k in range(3):
            own[c, k : k + 1, :] = pos[k, row, :]
            own[c, 4 + k : 5 + k, :] = vel[k, row, :]
        own[c, 3:4, :] = jnp.where(active, root[row], 0.0)
        own[c, 7:8, :] = jnp.where(active, bond[row], 0.0)
        fluid[row, :] = jnp.where(active, free[row], 0.0)
    head[...] = own[0:RIM]
    tail[...] = jnp.zeros(tail.shape, F32)
    tail[0:RIM] = own[cells - RIM : cells]
    for t in range(send.shape[0] // SLOTS):
        for k in range(SLOTS):
            cell = sends[0, 0, k, t]
            tile = own[jnp.maximum(cell, 0)]
            send[t * SLOTS + k] = jnp.where(cell >= 0, tile, 0.0)


def squared(tile, sub):
    return jnp.sum(jnp.where(sub < 3, tile * tile, 0.0), axis=0, keepdims=True)


def source_rows(tile, sub):
    root = tile[3:4]
    far = root * (1.0 - 0.25 * squared(tile, sub))
    value = jnp.where(
        sub < 3,
        tile * (0.5 * root),
        jnp.where(sub == 3, far, jnp.where(sub == 4, -0.25 * root, 0.0)),
    )
    a, b, c = pieces(value, 3)
    return jnp.concatenate([a, b, a, c, a, b], 0).astype(BF16)


def target_rows(tile, sub):
    value = jnp.where(
        sub < 3,
        tile,
        jnp.where(sub == 3, 1.0, jnp.where(sub == 4, squared(tile, sub), 0.0)),
    )
    a, b, c = pieces(value, 3)
    return jnp.concatenate([a, a, b, a, c, b], 0).astype(BF16)


def cubes(source, target):
    w = jnp.maximum(contract(source, target, 0), 0.0)
    return jnp.sum((w * w * w).reshape(w.shape[0] // 8, 8, w.shape[1]), axis=0)


def run_jobs(rows, cells, count, tab, first_row, mine, sums):
    last = mine.shape[0] - 1

    def some(t, carry):
        for k in range(STEP):
            c = cells(t * STEP + k)
            value = cubes(tab[rows(t * STEP + k) - first_row], mine[jnp.minimum(c, last)])
            sums[c] = sums[c] + value
        return carry

    lax.fori_loop(0, lax.div(count + (STEP - 1), STEP), some, 0)


def home(moves, near, tiles, sums, tab, mine, plan, jobs):
    cells, _, width = tiles.shape
    sub, _ = rows_and_lanes(width)
    moves.need(0, 1)

    def build(i, carry):
        tab[i] = source_rows(tiles[i], sub)
        mine[i] = target_rows(tiles[i], sub)
        return carry

    lax.fori_loop(0, cells, build, 0, unroll=4)
    moves.save(1, 2)

    def alone(t, carry):
        for k in range(STEP):
            c = t * STEP + k
            sums[c] = cubes(tab[c], mine[c])
        return carry

    lax.fori_loop(0, cells // STEP, alone, 0)
    sums[cells] = jnp.zeros((8, width), F32)
    local, away = jnp.int32(0), jnp.int32(0)
    for k in range(near.shape[0]):
        for c in range(cells):
            row = near[k, c]
            inside = (row >= RIM) & (row < RIM + cells)
            jobs[local] = row
            jobs[128 + local] = c
            plan[JOB_ROW + away] = row
            plan[JOB_CELL + away] = c
            local = local + inside.astype(jnp.int32)
            away = away + 1 - inside.astype(jnp.int32)
    for k in range(STEP):
        jobs[local + k] = RIM
        jobs[128 + local + k] = cells
        plan[JOB_ROW + away + k] = RIM
        plan[JOB_CELL + away + k] = cells
    plan[JOB_COUNT] = away
    run_jobs(lambda i: jobs[i], lambda i: jobs[128 + i], local, tab, RIM, mine, sums)
    moves.save(0)


def routing(moves, owners, owners_v, after, plan, landing, seen, *, cells):
    me = lax.axis_index("dev")
    moves.need(0, 1)
    for d in range(seen.shape[0]):
        seen[d] = 0
    for i in range(seen.shape[0] * SLOTS):
        plan[OUTS + i] = 0
    moving, staying = jnp.int32(0), jnp.int32(0)
    for c in range(cells):
        to = owners[0, me * cells + c]
        leaves = (to != me).astype(jnp.int32)
        plan[MOVING + moving] = c
        plan[STAYING + staying] = c
        spot = jnp.where(to != me, to * SLOTS + seen[to], seen.shape[0] * SLOTS)
        plan[OUTS + spot] = moving
        seen[to] = seen[to] + leaves
        moving = moving + leaves
        staying = staying + 1 - leaves
    moves.save(0)
    entries = owners_v.shape[1]
    dev = lax.broadcasted_iota(jnp.int32, (entries, 128), 1)
    entry = lax.broadcasted_iota(jnp.int32, (entries, 128), 0)
    belongs = (entry >= dev * cells) & (entry < dev * cells + cells)
    ours = jnp.broadcast_to((owners_v[...] == me).astype(F32), (8, entries)).astype(BF16)
    arrivals = contract(ours, jnp.where(belongs, 1.0, 0.0).astype(BF16), 1)
    earlier = lax.broadcasted_iota(jnp.int32, (128, 128), 0) < lax.broadcasted_iota(
        jnp.int32, (128, 128), 1
    )
    before = contract(arrivals.astype(BF16), jnp.where(earlier, 1.0, 0.0).astype(BF16), 1)
    lane = lax.broadcasted_iota(jnp.int32, (8, 128), 1)
    kind = lax.broadcasted_iota(jnp.int32, (8, 128), 0)
    place = before.astype(jnp.int32)
    comes = (arrivals > 0.0) & (lane != me)
    landing[...] = jnp.where((kind == 0) & ~comes, cells, place)


def densities(
    moves, counts, plan, sends, tab_own, tiles_own, below, above, rest, mine, sums,
    rho, q, q_head, q_tail, send_q, tab, tiles,
):
    cells, _, width = mine.shape
    sub, lane = rows_and_lanes(width)
    moves.need(5, 6, 7)
    for start, count in ((0, RIM), (RIM + cells, tab.shape[0] - RIM - cells)):

        def source(i, carry, start=start):
            tab[start + i] = source_rows(tiles[start + i], sub)
            return carry

        lax.fori_loop(0, count, source, 0, unroll=4)

    moves.need(*range(10))
    moves.save(5, 6)
    run_jobs(
        lambda i: plan[JOB_ROW + i], lambda i: plan[JOB_CELL + i], plan[JOB_COUNT], tab, 0, mine, sums
    )
    for c in range(cells):
        row = jnp.sum(sums[c], axis=0, keepdims=True)
        active = lane < counts[c]
        safe = jnp.where(active, row, 1.0)
        value = STIFFNESS * (row - REST_DENSITY) / (safe * safe)
        q[c] = jnp.where(active, value, 0.0)
        rho[c : c + 1, :] = jnp.where(active, row, 0.0)
    q_tail[...] = jnp.zeros(q_tail.shape, F32)
    for r in range(RIM):
        q_head[r] = q[r]
        q_tail[r] = q[cells - RIM + r]
    for t in range(send_q.shape[0] // SLOTS):
        for k in range(SLOTS):
            pick = jnp.maximum(sends[0, 0, k, t], 0)
            send_q[t * SLOTS + k] = q[pick]


def first_features(tile, sub):
    bond = tile[7:8]
    value = jnp.where(
        sub < 3,
        tile * bond,
        jnp.where(sub == 3, bond, jnp.where(sub < 7, tile, 0.0)),
    )
    return jnp.concatenate(pieces(value, 2), 0).astype(BF16)


def second_features(tile, row_q, sub):
    spot = jnp.where(sub < 3, tile, 1.0)
    spot = jnp.where(sub < 4, spot, row_q * pltpu.roll(spot, 4, 0))
    value = spot * (1.5 * tile[3:4])
    rows = pieces(value, 3) + [jnp.zeros_like(value)]
    return jnp.concatenate(rows, 0).astype(BF16)


class Pairs:
    def __init__(self, near, tab, mine, feat1, feat2):
        self.near, self.tab, self.mine, self.feat1, self.feat2 = near, tab, mine, feat1, feat2

    def row(self, c, k):
        return RIM + c if k == 0 else self.near[k - 1, c]

    def make(self, c, k, part, odd, even):
        width = odd.shape[1] // 2
        half = width // 2
        source = self.tab[self.row(c, k), :, part * half : part * half + half]
        w = jnp.maximum(contract(source, self.mine[c], 0), 0.0)
        square = w * w
        once, high = w.astype(BF16), square.astype(BF16)
        rows = slice(k * width + part * half, k * width + part * half + half)
        odd[rows, :width] = once
        odd[rows, width:] = once * high
        even[rows, :width] = high
        even[rows, width:] = (square - high.astype(F32)).astype(BF16)

    def fill(self, c, odd, even):
        for k in range(self.near.shape[0] + 1):
            self.make(c, k, 0, odd, even)
            self.make(c, k, 1, odd, even)

    def step(self, c, odd, even, later, next_odd, next_even, sub):
        width = odd.shape[1] // 2
        first = second = 0.0
        for k in range(self.near.shape[0] + 1):
            row = self.row(c, k)
            rows = slice(k * width, k * width + width)
            self.make(later, k, 0, next_odd, next_even)
            first = first + contract(self.feat1[row], odd[rows], 1)
            self.make(later, k, 1, next_odd, next_even)
            second = second + contract(self.feat2[row], even[rows], 1)
        first = first[0:8] + first[8:16]
        first = jnp.where(sub < 4, first[:, :width], first[:, width:])
        second = second[:, :width] + second[:, width:]
        return first, second[0:8] + second[8:16] + second[16:24]


def sweep(pairs, order, start, count, buffers, finish, sub, moves):
    a, b = buffers[0:2], buffers[2:4]
    pairs.fill(order[start], *a)
    moves.need(*range(len(moves.ins)))

    def two(t, carry):
        for i, now, then in ((2 * t, a, b), (2 * t + 1, b, a)):
            c = order[start + i]
            later = order[start + jnp.minimum(i + 1, count - 1)]
            finish(i, c, *pairs.step(c, *now, later, *then, sub))
        return carry

    lax.fori_loop(0, count // 2, two, 0)


def advance(first, second, tile, row_q, row_rho, row_fluid, active, sub):
    mix = row_q * second + pltpu.roll(second, 4, 0) - first
    speed = pltpu.roll(tile, 4, 0)
    drag = pltpu.roll(first, 4, 0) - speed * row_rho
    acc = tile * mix[3:4] - mix + VISCOSITY * drag
    acc = acc - jnp.where(sub == 2, GRAVITY, 0.0)
    step = TIME_STEP * row_fluid
    speed = speed + step * acc
    place = tile + step * speed
    result = jnp.where(
        sub < 3,
        place,
        jnp.where(sub < 6, pltpu.roll(speed, 3, 0), jnp.where(sub == 6, row_rho, 0.0)),
    )
    return jnp.where(active, result, 0.0)


def rows_and_lanes(width):
    return (
        lax.broadcasted_iota(jnp.int32, (8, width), 0),
        lax.broadcasted_iota(jnp.int32, (1, width), 1),
    )


def forces_moving(
    moves, counts, near, plan, q_below, q_own, q_above, q_rest, tiles, rho, fluid, tab, mine,
    outbox, feat1, feat2, q, moved, *buffers,
):
    sub, lane = rows_and_lanes(tiles.shape[2])
    moves.need(3, 4, 5, 6, 7)

    def source(i, carry):
        tile = tiles[i]
        feat1[i] = first_features(tile, sub)
        feat2[i] = second_features(tile, q[i], sub)
        return carry

    lax.fori_loop(0, tiles.shape[0], source, 0, unroll=8)
    moves.save(1, 2)
    moves.need(*range(12))

    def finish(i, c, first, second):
        row = pl.ds(c, 1)
        moved[i] = advance(
            first, second, tiles[RIM + c], q[RIM + c], rho[row, :], fluid[row, :], lane < counts[c], sub
        )

    sweep(
        Pairs(near, tab, mine, feat1, feat2), plan, MOVING, MOVERS, buffers, finish, sub, moves
    )
    for t in range(outbox.shape[0] // SLOTS):
        for k in range(SLOTS):
            outbox[t * SLOTS + k] = moved[plan[OUTS + t * SLOTS + k]]


def forces_staying(
    moves, counts, near, plan, tab, mine, feat1, feat2, tiles, q, rho, fluid, stayed, *buffers
):
    sub, lane = rows_and_lanes(tiles.shape[2])
    moves.need(1, 2, 3, 4)

    def finish(i, c, first, second):
        row = pl.ds(c, 1)
        stayed[i] = advance(
            first, second, tiles[RIM + c], q[c], rho[row, :], fluid[row, :], lane < counts[c], sub
        )

    sweep(
        Pairs(near, tab, mine, feat1, feat2), plan, STAYING, stayed.shape[0], buffers, finish, sub, moves
    )


def settle(moves, landing, stayed, inbox, state, density):
    cells = state.shape[1]
    me = lax.axis_index("dev")
    moves.need(0, 1)

    def put(place, tile):
        for k in range(6):
            state[k, pl.ds(place, 1), :] = tile[k : k + 1]
        density[pl.ds(place, 1), :] = tile[6:7]

    for i in range(stayed.shape[0]):
        put(landing[1, me] + i, stayed[i])
    for t in range(inbox.shape[0] // SLOTS):

        @pl.when(landing[0, t] < cells)
        def _():
            for k in range(SLOTS):
                put(landing[0, t] + k, inbox[t * SLOTS + k])


def shards(positions, velocities, masses, counts, walls, neighbours, send_cells, owners):
    cells, width = masses.shape
    peers = lax.axis_size("dev")
    total = 2 * RIM + cells + SLOTS * peers
    groups = lax.axis_size("group")
    up = [(i, i + 1) for i in range(groups - 1)]
    down = [(i + 1, i) for i in range(groups - 1)]

    def exchange(x):
        return lax.all_to_all(x, "dev", split_axis=0, concat_axis=0, tiled=True)

    near = neighbours.T
    sends = jnp.swapaxes(send_cells, 2, 3)
    own, send, head, tail, fluid = call(
        prepare,
        4096,
        [counts, sends],
        [positions, velocities, masses, walls],
        [],
        [
            ((cells, 8, width), F32),
            ((SLOTS * peers, 8, width), F32),
            ((RIM, 8, width), F32),
            ((SLOTS * peers, 8, width), F32),
            ((cells, width), F32),
        ],
    )
    below = lax.ppermute(tail, "group", up)
    rest = exchange(send)
    above = lax.ppermute(head, "group", down)
    row_type, small = ((RIM, 1, width), F32), ((SLOTS * peers, 1, width), F32)
    pair_type, own_type = ((total, 48, width), BF16), ((cells, 48, width), BF16)
    sums, tab_own, mine, jobs = call(
        home,
        4096,
        [near],
        [own],
        [],
        [((cells + 1, 8, width), F32), own_type, own_type, ((PLAN,), jnp.int32)],
        [pltpu.SMEM((256,), jnp.int32)],
    )
    rho, q, q_head, q_tail, send_q, tab, tiles = call(
        densities,
        4096,
        [counts, jobs, sends],
        [tab_own, own, below, above, rest, mine, sums],
        [],
        [
            ((cells, width), F32),
            ((cells, 1, width), F32),
            row_type,
            small,
            small,
            pair_type,
            ((total, 8, width), F32),
        ],
        into=[
            (5, RIM, cells),
            (6, RIM, cells),
            (6, 0, RIM),
            (6, RIM + cells, RIM),
            (6, 2 * RIM + cells, SLOTS * peers),
        ],
    )
    q_below = lax.ppermute(q_tail, "group", up)
    q_rest = exchange(send_q)
    q_above = lax.ppermute(q_head, "group", down)
    plan, landing = call(
        functools.partial(routing, cells=cells),
        4096,
        [owners],
        [owners, q_head],
        [],
        [((PLAN,), jnp.int32), ((8, 128), jnp.int32)],
        [pltpu.SMEM((peers,), jnp.int32)],
    )
    partners = neighbours.shape[1] + 1
    buffers = [pltpu.VMEM((partners * width, 2 * width), BF16)] * 4
    outbox, feat1, feat2 = call(
        forces_moving,
        4096,
        [counts, near, plan],
        [q_below, q, q_above, q_rest, tiles, rho, fluid, tab, mine],
        [],
        [
            ((SLOTS * peers, 8, width), F32),
            ((total, 16, width), BF16),
            ((total, 32, width), BF16),
        ],
        [pltpu.VMEM((total, 1, width), F32), pltpu.VMEM((MOVERS, 8, width), F32)] + buffers,
        into=[
            (3, 0, RIM),
            (3, RIM, cells),
            (3, RIM + cells, RIM),
            (3, 2 * RIM + cells, SLOTS * peers),
        ],
    )
    inbox = exchange(outbox)
    [stayed] = call(
        forces_staying,
        4096,
        [counts, near, plan],
        [tab, mine, feat1, feat2, tiles, q, rho, fluid],
        [],
        [((cells - MOVERS, 8, width), F32)],
        buffers,
    )
    return call(
        settle,
        12000,
        [landing],
        [stayed],
        [inbox],
        [((6, cells, width), F32), ((cells, width), F32)],
    )


def solution(mesh):
    return jax.shard_map(
        shards,
        mesh=mesh,
        in_specs=(
            P(None, ("group", "dev"), None),
            P(None, ("group", "dev"), None),
            P(("group", "dev"), None),
            P(("group", "dev")),
            P(("group", "dev"), None),
            P(("group", "dev"), None),
            P("group", "dev", None, None),
            P("group", None),
        ),
        out_specs=(P(None, ("group", "dev"), None), P(("group", "dev"), None)),
        check_vma=False,
    )
```

```python
import jax
import jax.numpy as jnp
from jax import lax
from jax.experimental import pallas as pl
from jax.experimental.pallas import tpu as pltpu
from jax.sharding import PartitionSpec as P

RIM = 4
SLOTS = 2
MOVERS = 16
STEP = 8
WIDE = 512
JOB_ROW, JOB_CELL, JOB_COUNT, MOVING, STAYING, OUTS, PLAN = 0, 128, 256, 272, 304, 336, 512
STIFFNESS = 2.0
REST_DENSITY = 0.8
VISCOSITY = 0.5
COHESION = 0.3
ADHESION = 0.8
GRAVITY = 1.0
TIME_STEP = 0.5

F32 = jnp.float32
BF16 = jnp.bfloat16
HBM = pl.BlockSpec(memory_space=pltpu.HBM)
VMEM = pl.BlockSpec(memory_space=pltpu.VMEM)


class Moves:
    def __init__(self, ins, outs):
        self.ins, self.outs = list(ins), list(outs)
        self.waited, self.saved = set(), set()
        for copy in self.ins:
            copy.start()

    def need(self, *which):
        for i in which:
            if i not in self.waited:
                self.waited.add(i)
                self.ins[i].wait()

    def save(self, *which):
        for i in which:
            if i not in self.saved:
                self.saved.add(i)
                self.outs[i].start()


def call(kernel, room, ints, held, near, outs, scratch=(), into=()):
    n_in, n_near, n_out = len(ints) + len(held), len(near), len(outs)

    def body(*refs):
        sources, refs = refs[:n_in], refs[n_in:]
        close, refs = refs[:n_near], refs[n_near:]
        targets, refs = refs[:n_out], refs[n_out:]
        inner, refs = list(refs[: n_in - len(into)]), refs[n_in - len(into) :]
        results, refs = refs[:n_out], refs[n_out:]
        sources = list(sources)
        for i, (out, start, count) in enumerate(into):
            target = (*results, *refs[2:])[out]
            inner.insert(len(ints) + i, target.at[pl.ds(start, count)])
            sources[len(ints) + i] = sources[len(ints) + i].at[pl.ds(0, count)]
        in_sems, out_sems, rest = refs[0], refs[1], refs[2:]
        moves = Moves(
            [pltpu.make_async_copy(a, b, in_sems.at[i]) for i, (a, b) in enumerate(zip(sources, inner))],
            [
                pltpu.make_async_copy(a, b.at[pl.ds(0, a.shape[0])], out_sems.at[i])
                for i, (a, b) in enumerate(zip(results, targets))
            ],
        )
        kernel(moves, *inner, *close, *results, *rest)
        moves.need(*range(n_in))
        moves.save(*range(n_out))
        for copy in moves.outs:
            copy.wait()

    return pl.pallas_call(
        body,
        out_shape=[jax.ShapeDtypeStruct((*o[2:], *o[0][len(o) - 2 :]), o[1]) for o in outs],
        in_specs=[HBM] * n_in + [VMEM] * n_near,
        out_specs=[HBM] * n_out,
        scratch_shapes=[pltpu.SMEM(x.shape, x.dtype) for x in ints]
        + [pltpu.VMEM(x.shape, x.dtype) for x in held[len(into) :]]
        + [(pltpu.SMEM if len(o[0]) == 1 else pltpu.VMEM)(*o[:2]) for o in outs]
        + [pltpu.SemaphoreType.DMA((n_in,)), pltpu.SemaphoreType.DMA((n_out,))]
        + list(scratch),
        compiler_params=pltpu.CompilerParams(vmem_limit_bytes=(64 << 20) - (room << 10)),
        name=kernel.__name__,
    )(*ints, *held, *near)


def contract(a, b, dim):
    return lax.dot_general(a, b, (((dim,), (0,)), ((), ())), preferred_element_type=F32)


def pieces(value, count):
    parts = []
    for _ in range(count):
        part = value.astype(BF16).astype(F32)
        parts.append(part)
        value = value - part
    return parts


def prepare(moves, counts, sends, pos, vel, mass, walls, own, send, head, tail, fluid):
    cells, width = mass.shape
    moves.need(*range(6))
    m = mass[...]
    root = jnp.exp(jnp.log(m) * (1.0 / 3.0))
    root = root - (root * root * root - m) / (3.0 * root * root)
    wall = walls[...].astype(F32)
    bond = root * root * (COHESION + (ADHESION - COHESION) * wall)
    free = 1.0 - wall
    lane = lax.broadcasted_iota(jnp.int32, (1, width), 1)
    for c in range(cells):
        row = slice(c, c + 1)
        active = lane < counts[c]
        for k in range(3):
            own[c, k : k + 1, :] = pos[k, row, :]
            own[c, 4 + k : 5 + k, :] = vel[k, row, :]
        own[c, 3:4, :] = jnp.where(active, root[row], 0.0)
        own[c, 7:8, :] = jnp.where(active, bond[row], 0.0)
        fluid[row, :] = jnp.where(active, free[row], 0.0)
    head[...] = own[0:RIM]
    tail[...] = jnp.zeros(tail.shape, F32)
    tail[0:RIM] = own[cells - RIM : cells]
    moves.save(0, 2, 3, 4)
    for t in range(send.shape[0] // SLOTS):
        for k in range(SLOTS):
            cell = sends[0, 0, k, t]
            tile = own[jnp.maximum(cell, 0)]
            send[t * SLOTS + k] = jnp.where(cell >= 0, tile, 0.0)


def squared(tile, sub):
    return jnp.sum(jnp.where(sub < 3, tile * tile, 0.0), axis=0, keepdims=True)


def source_rows(tile, sub):
    root = tile[3:4]
    far = root * (1.0 - 0.25 * squared(tile, sub))
    value = jnp.where(
        sub < 3,
        tile * (0.5 * root),
        jnp.where(sub == 3, far, jnp.where(sub == 4, -0.25 * root, 0.0)),
    )
    a, b, c = pieces(value, 3)
    return jnp.concatenate([a, b, a, c, a, b], 0).astype(BF16)


def target_rows(tile, sub):
    value = jnp.where(
        sub < 3,
        tile,
        jnp.where(sub == 3, 1.0, jnp.where(sub == 4, squared(tile, sub), 0.0)),
    )
    a, b, c = pieces(value, 3)
    return jnp.concatenate([a, a, b, a, c, b], 0).astype(BF16)


def cubes(source, target):
    w = jnp.maximum(contract(source, target, 0), 0.0)
    return jnp.sum((w * w * w).reshape(w.shape[0] // 8, 8, w.shape[1]), axis=0)


def run_jobs(rows, cells, count, tab, first_row, mine, sums):
    last = mine.shape[0] - 1

    def some(t, carry):
        for k in range(STEP):
            c = cells(t * STEP + k)
            value = cubes(tab[rows(t * STEP + k) - first_row], mine[jnp.minimum(c, last)])
            sums[c] = sums[c] + value
        return carry

    lax.fori_loop(0, lax.div(count + (STEP - 1), STEP), some, 0)


def home(moves, near, tiles, sums, tab, mine, plan, jobs):
    cells, _, width = tiles.shape
    sub, _ = rows_and_lanes(width)
    moves.need(0, 1)

    def build(i, carry):
        tab[i] = source_rows(tiles[i], sub)
        mine[i] = target_rows(tiles[i], sub)
        return carry

    lax.fori_loop(0, cells, build, 0, unroll=4)
    moves.save(1, 2)

    def alone(t, carry):
        for k in range(STEP):
            c = t * STEP + k
            sums[c] = cubes(tab[c], mine[c])
        return carry

    lax.fori_loop(0, cells // STEP, alone, 0)
    sums[cells] = jnp.zeros((8, width), F32)
    local, away = jnp.int32(0), jnp.int32(0)
    for k in range(near.shape[0]):
        for c in range(cells):
            row = near[k, c]
            inside = (row >= RIM) & (row < RIM + cells)
            jobs[local] = row
            jobs[128 + local] = c
            plan[JOB_ROW + away] = row
            plan[JOB_CELL + away] = c
            local = local + inside.astype(jnp.int32)
            away = away + 1 - inside.astype(jnp.int32)
    for k in range(STEP):
        jobs[local + k] = RIM
        jobs[128 + local + k] = cells
        plan[JOB_ROW + away + k] = RIM
        plan[JOB_CELL + away + k] = cells
    plan[JOB_COUNT] = away
    run_jobs(lambda i: jobs[i], lambda i: jobs[128 + i], local, tab, RIM, mine, sums)
    moves.save(0)


def routing(moves, owners, owners_v, tiles, q, plan, landing, feat1, feat2_own, seen):
    cells, _, width = feat2_own.shape
    sub, _ = rows_and_lanes(width)
    moves.need(2, 3)

    def first(i, carry):
        feat1[i] = first_features(tiles[i], sub)
        return carry

    def second(i, carry):
        feat2_own[i] = second_features(tiles[RIM + i], q[i], sub)
        return carry

    lax.fori_loop(0, tiles.shape[0], first, 0, unroll=8)
    lax.fori_loop(0, cells, second, 0, unroll=8)
    moves.save(2, 3)
    me = lax.axis_index("dev")
    moves.need(0, 1)
    for d in range(seen.shape[0]):
        seen[d] = 0
    for i in range(seen.shape[0] * SLOTS):
        plan[OUTS + i] = 0
    moving, staying = jnp.int32(0), jnp.int32(0)
    for c in range(cells):
        to = owners[0, me * cells + c]
        leaves = (to != me).astype(jnp.int32)
        plan[MOVING + moving] = c
        plan[STAYING + staying] = c
        spot = jnp.where(to != me, to * SLOTS + seen[to], seen.shape[0] * SLOTS)
        plan[OUTS + spot] = moving
        seen[to] = seen[to] + leaves
        moving = moving + leaves
        staying = staying + 1 - leaves
    moves.save(0)
    entries = owners_v.shape[1]
    dev = lax.broadcasted_iota(jnp.int32, (entries, 128), 1)
    entry = lax.broadcasted_iota(jnp.int32, (entries, 128), 0)
    belongs = (entry >= dev * cells) & (entry < dev * cells + cells)
    ours = jnp.broadcast_to((owners_v[...] == me).astype(F32), (8, entries)).astype(BF16)
    arrivals = contract(ours, jnp.where(belongs, 1.0, 0.0).astype(BF16), 1)
    earlier = lax.broadcasted_iota(jnp.int32, (128, 128), 0) < lax.broadcasted_iota(
        jnp.int32, (128, 128), 1
    )
    before = contract(arrivals.astype(BF16), jnp.where(earlier, 1.0, 0.0).astype(BF16), 1)
    lane = lax.broadcasted_iota(jnp.int32, (8, 128), 1)
    kind = lax.broadcasted_iota(jnp.int32, (8, 128), 0)
    place = before.astype(jnp.int32)
    comes = (arrivals > 0.0) & (lane != me)
    landing[...] = jnp.where((kind == 0) & ~comes, cells, place)


def densities(
    moves, counts, plan, sends, below, above, rest, tab_own, tiles_own, mine, sums,
    rho, q, q_head, q_tail, send_q, tab, tiles,
):
    cells, _, width = mine.shape
    sub, lane = rows_and_lanes(width)
    moves.need(3, 4, 5)
    for start, count in ((0, RIM), (RIM + cells, tab.shape[0] - RIM - cells)):

        def source(i, carry, start=start):
            tab[start + i] = source_rows(tiles[start + i], sub)
            return carry

        lax.fori_loop(0, count, source, 0, unroll=4)

    moves.need(*range(10))
    moves.save(5, 6)
    run_jobs(
        lambda i: plan[JOB_ROW + i], lambda i: plan[JOB_CELL + i], plan[JOB_COUNT], tab, 0, mine, sums
    )
    for c in range(cells):
        row = jnp.sum(sums[c], axis=0, keepdims=True)
        active = lane < counts[c]
        safe = jnp.where(active, row, 1.0)
        value = STIFFNESS * (row - REST_DENSITY) / (safe * safe)
        q[c] = jnp.where(active, value, 0.0)
        rho[c : c + 1, :] = jnp.where(active, row, 0.0)
    q_tail[...] = jnp.zeros(q_tail.shape, F32)
    for r in range(RIM):
        q_head[r] = q[r]
        q_tail[r] = q[cells - RIM + r]
    for t in range(send_q.shape[0] // SLOTS):
        for k in range(SLOTS):
            pick = jnp.maximum(sends[0, 0, k, t], 0)
            send_q[t * SLOTS + k] = q[pick]


def first_features(tile, sub):
    bond = tile[7:8]
    value = jnp.where(
        sub < 3,
        tile * bond,
        jnp.where(sub == 3, bond, jnp.where(sub < 7, tile, 0.0)),
    )
    return jnp.concatenate(pieces(value, 2), 0).astype(BF16)


def second_features(tile, row_q, sub):
    spot = jnp.where(sub < 3, tile, 1.0)
    spot = jnp.where(sub < 4, spot, row_q * pltpu.roll(spot, 4, 0))
    value = spot * (1.5 * tile[3:4])
    rows = pieces(value, 3) + [jnp.zeros_like(value)]
    return jnp.concatenate(rows, 0).astype(BF16)


class Pairs:
    def __init__(self, near, tab, mine, feat1, feat2):
        self.near, self.tab, self.mine, self.feat1, self.feat2 = near, tab, mine, feat1, feat2

    def row(self, c, k):
        return RIM + c if k == 0 else self.near[k - 1, c]

    def make(self, c, k, part, odd, even):
        width = odd.shape[1] // 2
        half = width // 2
        source = self.tab[self.row(c, k), :, part * half : part * half + half]
        w = jnp.maximum(contract(source, self.mine[c], 0), 0.0)
        square = w * w
        once, high = w.astype(BF16), square.astype(BF16)
        rows = slice(k * width + part * half, k * width + part * half + half)
        odd[rows, :width] = once
        odd[rows, width:] = once * high
        even[rows, :width] = high
        even[rows, width:] = (square - high.astype(F32)).astype(BF16)

    def fill(self, c, odd, even):
        for k in range(self.near.shape[0] + 1):
            self.make(c, k, 0, odd, even)
            self.make(c, k, 1, odd, even)

    def step(self, c, odd, even, later, next_odd, next_even, sub):
        width = odd.shape[1] // 2
        first = second = 0.0
        for k in range(self.near.shape[0] + 1):
            row = self.row(c, k)
            rows = slice(k * width, k * width + width)
            first = first + contract(self.feat1[row], odd[rows], 1)
            self.make(later, k, 0, next_odd, next_even)
            second = second + contract(self.feat2[row], even[rows], 1)
            self.make(later, k, 1, next_odd, next_even)
        first = first[0:8] + first[8:16]
        first = jnp.where(sub < 4, first[:, :width], first[:, width:])
        second = second[:, :width] + second[:, width:]
        return first, second[0:8] + second[8:16] + second[16:24]


def sweep(pairs, order, start, count, buffers, finish, sub, moves):
    a, b = buffers[0:2], buffers[2:4]
    pairs.fill(order[start], *a)
    moves.need(*range(len(moves.ins)))

    def some(t, carry):
        for k in range(STEP):
            i = STEP * t + k
            now, then = (a, b) if k % 2 == 0 else (b, a)
            c = order[start + i]
            later = order[start + jnp.minimum(i + 1, count - 1)]
            finish(i, c, *pairs.step(c, *now, later, *then, sub))
        return carry

    lax.fori_loop(0, count // STEP, some, 0)


def advance(first, second, tile, row_q, row_rho, row_fluid, active, sub):
    mix = row_q * second + pltpu.roll(second, 4, 0) - first
    speed = pltpu.roll(tile, 4, 0)
    drag = pltpu.roll(first, 4, 0) - speed * row_rho
    acc = tile * mix[3:4] - mix + VISCOSITY * drag
    acc = acc - jnp.where(sub == 2, GRAVITY, 0.0)
    step = TIME_STEP * row_fluid
    speed = speed + step * acc
    place = tile + step * speed
    result = jnp.where(
        sub < 3,
        place,
        jnp.where(sub < 6, pltpu.roll(speed, 3, 0), jnp.where(sub == 6, row_rho, 0.0)),
    )
    return jnp.where(active, result, 0.0)


def rows_and_lanes(width):
    return (
        lax.broadcasted_iota(jnp.int32, (8, width), 0),
        lax.broadcasted_iota(jnp.int32, (1, width), 1),
    )


def forces_moving(
    moves, counts, near, plan, q_below, q_own, q_above, q_rest, feat2_own, tiles, rho, fluid, tab, mine, feat1,
    outbox, feat2, q, moved, *buffers,
):
    cells = rho.shape[0]
    sub, lane = rows_and_lanes(tiles.shape[2])
    moves.need(3, 5, 6, 8)

    def source(i, carry):
        feat2[i] = second_features(tiles[i], q[i], sub)
        return carry

    lax.fori_loop(0, RIM, source, 0, unroll=4)
    lax.fori_loop(RIM + cells, tiles.shape[0], source, 0, unroll=8)
    moves.need(4, 7)
    moves.save(1)
    moves.need(*range(14))

    def finish(i, c, first, second):
        row = pl.ds(c, 1)
        moved[i] = advance(
            first, second, tiles[RIM + c], q[RIM + c], rho[row, :], fluid[row, :], lane < counts[c], sub
        )

    sweep(
        Pairs(near, tab, mine, feat1, feat2), plan, MOVING, MOVERS, buffers, finish, sub, moves
    )
    for t in range(outbox.shape[0] // SLOTS):
        for k in range(SLOTS):
            outbox[t * SLOTS + k] = moved[plan[OUTS + t * SLOTS + k]]


def forces_staying(
    moves, counts, near, plan, tab, mine, feat1, feat2, tiles, q, rho, fluid, stayed, *buffers
):
    sub, lane = rows_and_lanes(tiles.shape[2])
    moves.need(1, 2, 3, 4)

    def finish(i, c, first, second):
        row = pl.ds(c, 1)
        stayed[i] = advance(
            first, second, tiles[RIM + c], q[c], rho[row, :], fluid[row, :], lane < counts[c], sub
        )

    sweep(
        Pairs(near, tab, mine, feat1, feat2), plan, STAYING, stayed.shape[0], buffers, finish, sub, moves
    )


def settle(moves, landing, stayed, inbox, state, density, _):
    cells = state.shape[1]
    me = lax.axis_index("dev")
    moves.need(0, 1)

    def put(place, tile):
        for k in range(6):
            state[k, pl.ds(place, 1), :] = tile[k : k + 1]
        density[pl.ds(place, 1), :] = tile[6:7]

    for i in range(stayed.shape[0]):
        put(landing[1, me] + i, stayed[i])
    for t in range(inbox.shape[0] // SLOTS):

        @pl.when(landing[0, t] < cells)
        def _():
            for k in range(SLOTS):
                put(landing[0, t] + k, inbox[t * SLOTS + k])


def shards(positions, velocities, masses, counts, walls, neighbours, send_cells, owners):
    cells, width = masses.shape
    peers = lax.axis_size("dev")
    total = 2 * RIM + cells + SLOTS * peers
    groups = lax.axis_size("group")
    up = [(i, i + 1) for i in range(groups - 1)]
    down = [(i + 1, i) for i in range(groups - 1)]

    def exchange(x):
        return lax.all_to_all(x, "dev", split_axis=0, concat_axis=0, tiled=True)

    near = neighbours.T
    sends = jnp.swapaxes(send_cells, 2, 3)
    own, send, head, tail, fluid = call(
        prepare,
        4096,
        [counts, sends],
        [positions, velocities, masses, walls],
        [],
        [
            ((cells, 8, width), F32),
            ((SLOTS * peers, 8, width), F32),
            ((RIM, 8, width), F32),
            ((SLOTS * peers, 8, width), F32),
            ((cells, width), F32),
        ],
    )
    below = lax.ppermute(tail, "group", up)
    rest = exchange(send)
    above = lax.ppermute(head, "group", down)
    row_type, small = ((RIM, 1, width), F32), ((SLOTS * peers, 1, width), F32)
    pair_type, own_type = ((total, 48, width), BF16), ((cells, 48, width), BF16)
    sums, tab_own, mine, jobs = call(
        home,
        4096,
        [near],
        [own],
        [],
        [((cells + 1, 8, width), F32), own_type, own_type, ((PLAN,), jnp.int32)],
        [pltpu.SMEM((256,), jnp.int32)],
    )
    rho, q, q_head, q_tail, send_q, tab, tiles = call(
        densities,
        4096,
        [counts, jobs, sends],
        [below, above, rest, tab_own, own, mine, sums],
        [],
        [
            ((cells, width), F32),
            ((cells, 1, width), F32),
            row_type,
            small,
            small,
            pair_type,
            ((total, 8, width), F32),
        ],
        into=[
            (6, 0, RIM),
            (6, RIM + cells, RIM),
            (6, 2 * RIM + cells, SLOTS * peers),
            (5, RIM, cells),
            (6, RIM, cells),
        ],
    )
    q_below = lax.ppermute(q_tail, "group", up)
    q_rest = exchange(send_q)
    q_above = lax.ppermute(q_head, "group", down)
    plan, landing, feat1, feat2_own = call(
        routing,
        4096,
        [owners],
        [owners, tiles, q],
        [],
        [
            ((PLAN,), jnp.int32),
            ((8, 128), jnp.int32),
            ((total, 16, width), BF16),
            ((cells, 32, width), BF16),
        ],
        [pltpu.SMEM((peers,), jnp.int32)],
    )
    partners = neighbours.shape[1] + 1
    buffers = [pltpu.VMEM((partners * width, 2 * width), BF16)] * 4
    outbox, feat2 = call(
        forces_moving,
        4096,
        [counts, near, plan],
        [q_below, q, q_above, q_rest, feat2_own, tiles, rho, fluid, tab, mine, feat1],
        [],
        [((SLOTS * peers, 8, width), F32), ((total, 32, width), BF16)],
        [pltpu.VMEM((total, 1, width), F32), pltpu.VMEM((MOVERS, 8, width), F32)] + buffers,
        into=[
            (2, 0, RIM),
            (2, RIM, cells),
            (2, RIM + cells, RIM),
            (2, 2 * RIM + cells, SLOTS * peers),
            (1, RIM, cells),
        ],
    )
    inbox = exchange(outbox)
    [stayed] = call(
        forces_staying,
        4096,
        [counts, near, plan],
        [tab, mine, feat1, feat2, tiles, q, rho, fluid],
        [],
        [((cells - MOVERS, 8, width), F32, WIDE)],
        buffers,
    )
    return call(
        settle,
        12000,
        [landing],
        [stayed],
        [inbox],
        [((6, cells, width), F32), ((cells, width), F32)],
        [pltpu.VMEM((cells - MOVERS, 8, width), F32)],
        into=[(2, 0, cells - MOVERS)],
    )


def solution(mesh):
    return jax.shard_map(
        shards,
        mesh=mesh,
        in_specs=(
            P(None, ("group", "dev"), None),
            P(None, ("group", "dev"), None),
            P(("group", "dev"), None),
            P(("group", "dev")),
            P(("group", "dev"), None),
            P(("group", "dev"), None),
            P("group", "dev", None, None),
            P("group", None),
        ),
        out_specs=(P(None, ("group", "dev"), None), P(("group", "dev"), None)),
        check_vma=False,
    )
```

```python
import jax
import jax.numpy as jnp
from jax import lax
from jax.experimental import pallas as pl
from jax.experimental.pallas import tpu as pltpu
from jax.sharding import PartitionSpec as P

RIM = 4
SLOTS = 2
MOVERS = 16
STEP = 8
WIDE = 512
JOB_ROW, JOB_CELL, JOB_COUNT, MOVING, STAYING, OUTS, PLAN = 0, 128, 256, 272, 304, 336, 512
STIFFNESS = 2.0
REST_DENSITY = 0.8
VISCOSITY = 0.5
COHESION = 0.3
ADHESION = 0.8
GRAVITY = 1.0
TIME_STEP = 0.5

F32 = jnp.float32
BF16 = jnp.bfloat16
HBM = pl.BlockSpec(memory_space=pltpu.HBM)
VMEM = pl.BlockSpec(memory_space=pltpu.VMEM)


class Moves:
    def __init__(self, ins, outs):
        self.ins, self.outs = list(ins), list(outs)
        self.waited, self.saved = set(), set()
        for copy in self.ins:
            copy.start()

    def need(self, *which):
        for i in which:
            if i not in self.waited:
                self.waited.add(i)
                self.ins[i].wait()

    def save(self, *which):
        for i in which:
            if i not in self.saved:
                self.saved.add(i)
                self.outs[i].start()


def call(kernel, room, ints, held, near, outs, scratch=(), into=()):
    n_in, n_near, n_out = len(ints) + len(held), len(near), len(outs)

    def body(*refs):
        sources, refs = refs[:n_in], refs[n_in:]
        close, refs = refs[:n_near], refs[n_near:]
        targets, refs = refs[:n_out], refs[n_out:]
        inner, refs = list(refs[: n_in - len(into)]), refs[n_in - len(into) :]
        results, refs = refs[:n_out], refs[n_out:]
        sources = list(sources)
        for i, (out, start, count) in enumerate(into):
            target = (*results, *refs[2:])[out]
            inner.insert(len(ints) + i, target.at[pl.ds(start, count)])
            sources[len(ints) + i] = sources[len(ints) + i].at[pl.ds(0, count)]
        in_sems, out_sems, rest = refs[0], refs[1], refs[2:]
        moves = Moves(
            [pltpu.make_async_copy(a, b, in_sems.at[i]) for i, (a, b) in enumerate(zip(sources, inner))],
            [
                pltpu.make_async_copy(a, b.at[pl.ds(0, a.shape[0])], out_sems.at[i])
                for i, (a, b) in enumerate(zip(results, targets))
            ],
        )
        kernel(moves, *inner, *close, *results, *rest)
        moves.need(*range(n_in))
        moves.save(*range(n_out))
        for copy in moves.outs:
            copy.wait()

    return pl.pallas_call(
        body,
        out_shape=[jax.ShapeDtypeStruct((*o[2:], *o[0][len(o) - 2 :]), o[1]) for o in outs],
        in_specs=[HBM] * n_in + [VMEM] * n_near,
        out_specs=[HBM] * n_out,
        scratch_shapes=[pltpu.SMEM(x.shape, x.dtype) for x in ints]
        + [pltpu.VMEM(x.shape, x.dtype) for x in held[len(into) :]]
        + [(pltpu.SMEM if len(o[0]) == 1 else pltpu.VMEM)(*o[:2]) for o in outs]
        + [pltpu.SemaphoreType.DMA((n_in,)), pltpu.SemaphoreType.DMA((n_out,))]
        + list(scratch),
        compiler_params=pltpu.CompilerParams(vmem_limit_bytes=(64 << 20) - (room << 10)),
        name=kernel.__name__,
    )(*ints, *held, *near)


def contract(a, b, dim):
    return lax.dot_general(a, b, (((dim,), (0,)), ((), ())), preferred_element_type=F32)


def pieces(value, count):
    parts = []
    for _ in range(count):
        part = value.astype(BF16).astype(F32)
        parts.append(part)
        value = value - part
    return parts


def prepare(moves, counts, sends, pos, vel, mass, walls, own, send, head, tail, fluid):
    cells, width = mass.shape
    moves.need(*range(6))
    m = mass[...]
    root = jnp.exp(jnp.log(m) * (1.0 / 3.0))
    root = root - (root * root * root - m) / (3.0 * root * root)
    wall = walls[...].astype(F32)
    bond = root * root * (COHESION + (ADHESION - COHESION) * wall)
    free = 1.0 - wall
    lane = lax.broadcasted_iota(jnp.int32, (1, width), 1)
    for c in range(cells):
        row = slice(c, c + 1)
        active = lane < counts[c]
        for k in range(3):
            own[c, k : k + 1, :] = pos[k, row, :]
            own[c, 4 + k : 5 + k, :] = vel[k, row, :]
        own[c, 3:4, :] = jnp.where(active, root[row], 0.0)
        own[c, 7:8, :] = jnp.where(active, bond[row], 0.0)
        fluid[row, :] = jnp.where(active, free[row], 0.0)
    head[...] = own[0:RIM]
    tail[...] = own[cells - RIM : cells]
    moves.save(0, 2, 3, 4)
    for t in range(send.shape[0] // SLOTS):
        for k in range(SLOTS):
            cell = sends[0, 0, k, t]
            tile = own[jnp.maximum(cell, 0)]
            send[t * SLOTS + k] = jnp.where(cell >= 0, tile, 0.0)


def squared(tile, sub):
    return jnp.sum(jnp.where(sub < 3, tile * tile, 0.0), axis=0, keepdims=True)


def source_rows(tile, sub):
    root = tile[3:4]
    far = root * (1.0 - 0.25 * squared(tile, sub))
    value = jnp.where(
        sub < 3,
        tile * (0.5 * root),
        jnp.where(sub == 3, far, jnp.where(sub == 4, -0.25 * root, 0.0)),
    )
    a, b, c = pieces(value, 3)
    return jnp.concatenate([a, b, a, c, a, b], 0).astype(BF16)


def target_rows(tile, sub):
    value = jnp.where(
        sub < 3,
        tile,
        jnp.where(sub == 3, 1.0, jnp.where(sub == 4, squared(tile, sub), 0.0)),
    )
    a, b, c = pieces(value, 3)
    return jnp.concatenate([a, a, b, a, c, b], 0).astype(BF16)


def cubes(source, target):
    w = jnp.maximum(contract(source, target, 0), 0.0)
    return jnp.sum((w * w * w).reshape(w.shape[0] // 8, 8, w.shape[1]), axis=0)


def run_jobs(rows, cells, count, tab, first_row, mine, sums):
    last = mine.shape[0] - 1

    def some(t, carry):
        for k in range(STEP):
            c = cells(t * STEP + k)
            value = cubes(tab[rows(t * STEP + k) - first_row], mine[jnp.minimum(c, last)])
            sums[c] = sums[c] + value
        return carry

    lax.fori_loop(0, lax.div(count + (STEP - 1), STEP), some, 0)


def home(moves, near, tiles, sums, tab, mine, plan, jobs):
    cells, _, width = tiles.shape
    sub, _ = rows_and_lanes(width)
    moves.need(0, 1)

    def build(i, carry):
        tab[i] = source_rows(tiles[i], sub)
        mine[i] = target_rows(tiles[i], sub)
        return carry

    lax.fori_loop(0, cells, build, 0, unroll=8)
    moves.save(1, 2)

    sums[cells] = jnp.zeros((8, width), F32)

    def alone(t, carry):
        local, away = carry
        for k in range(STEP):
            c = t * STEP + k
            sums[c] = cubes(tab[c], mine[c])
            for n in range(near.shape[0]):
                row = near[n, c]
                inside = (row >= RIM) & (row < RIM + cells)
                jobs[local] = row
                jobs[128 + local] = c
                plan[JOB_ROW + away] = row
                plan[JOB_CELL + away] = c
                local = local + inside.astype(jnp.int32)
                away = away + 1 - inside.astype(jnp.int32)
        return local, away

    local, away = lax.fori_loop(0, cells // STEP, alone, (jnp.int32(0), jnp.int32(0)))
    for k in range(STEP):
        jobs[local + k] = RIM
        jobs[128 + local + k] = cells
        plan[JOB_ROW + away + k] = RIM
        plan[JOB_CELL + away + k] = cells
    plan[JOB_COUNT] = away
    run_jobs(lambda i: jobs[i], lambda i: jobs[128 + i], local, tab, RIM, mine, sums)
    moves.save(0)


def routing(moves, owners, owners_v, tiles, q, plan, landing, feat1, feat2_own, seen):
    cells, _, width = feat2_own.shape
    sub, _ = rows_and_lanes(width)
    moves.need(2, 3)

    def first(i, carry):
        feat1[i] = first_features(tiles[i], sub)
        return carry

    def second(i, carry):
        feat2_own[i] = second_features(tiles[RIM + i], q[i], sub)
        return carry

    lax.fori_loop(0, tiles.shape[0], first, 0, unroll=8)
    lax.fori_loop(0, cells, second, 0, unroll=8)
    moves.save(2, 3)
    me = lax.axis_index("dev")
    moves.need(0, 1)
    for d in range(seen.shape[0]):
        seen[d] = 0
    for i in range(seen.shape[0] * SLOTS):
        plan[OUTS + i] = 0
    moving, staying = jnp.int32(0), jnp.int32(0)
    for c in range(cells):
        to = owners[0, me * cells + c]
        leaves = (to != me).astype(jnp.int32)
        plan[MOVING + moving] = c
        plan[STAYING + staying] = c
        spot = jnp.where(to != me, to * SLOTS + seen[to], seen.shape[0] * SLOTS)
        plan[OUTS + spot] = moving
        seen[to] = seen[to] + leaves
        moving = moving + leaves
        staying = staying + 1 - leaves
    moves.save(0)
    entries = owners_v.shape[1]
    dev = lax.broadcasted_iota(jnp.int32, (entries, 128), 1)
    entry = lax.broadcasted_iota(jnp.int32, (entries, 128), 0)
    belongs = (entry >= dev * cells) & (entry < dev * cells + cells)
    ours = jnp.broadcast_to((owners_v[...] == me).astype(F32), (8, entries)).astype(BF16)
    arrivals = contract(ours, jnp.where(belongs, 1.0, 0.0).astype(BF16), 1)
    earlier = lax.broadcasted_iota(jnp.int32, (128, 128), 0) < lax.broadcasted_iota(
        jnp.int32, (128, 128), 1
    )
    before = contract(arrivals.astype(BF16), jnp.where(earlier, 1.0, 0.0).astype(BF16), 1)
    lane = lax.broadcasted_iota(jnp.int32, (8, 128), 1)
    kind = lax.broadcasted_iota(jnp.int32, (8, 128), 0)
    place = before.astype(jnp.int32)
    comes = (arrivals > 0.0) & (lane != me)
    landing[...] = jnp.where((kind == 0) & ~comes, cells, place)


def densities(
    moves, counts, plan, sends, below, above, rest, tab_own, tiles_own, mine, sums,
    rho, q, q_head, q_tail, send_q, tab, tiles,
):
    cells, _, width = mine.shape
    sub, lane = rows_and_lanes(width)
    moves.need(3, 4, 5)
    for start, count in ((0, RIM), (RIM + cells, tab.shape[0] - RIM - cells)):

        def source(i, carry, start=start):
            tab[start + i] = source_rows(tiles[start + i], sub)
            return carry

        lax.fori_loop(0, count, source, 0, unroll=4)

    moves.need(*range(10))
    moves.save(5, 6)
    run_jobs(
        lambda i: plan[JOB_ROW + i], lambda i: plan[JOB_CELL + i], plan[JOB_COUNT], tab, 0, mine, sums
    )
    for c in range(cells):
        row = jnp.sum(sums[c], axis=0, keepdims=True)
        active = lane < counts[c]
        safe = jnp.where(active, row, 1.0)
        value = STIFFNESS * (row - REST_DENSITY) / (safe * safe)
        q[c] = jnp.where(active, value, 0.0)
        rho[c : c + 1, :] = jnp.where(active, row, 0.0)
    q_tail[...] = jnp.zeros(q_tail.shape, F32)
    for r in range(RIM):
        q_head[r] = q[r]
        q_tail[r] = q[cells - RIM + r]
    for t in range(send_q.shape[0] // SLOTS):
        for k in range(SLOTS):
            pick = jnp.maximum(sends[0, 0, k, t], 0)
            send_q[t * SLOTS + k] = q[pick]


def first_features(tile, sub):
    bond = tile[7:8]
    value = jnp.where(
        sub < 3,
        tile * bond,
        jnp.where(sub == 3, bond, jnp.where(sub < 7, tile, 0.0)),
    )
    return jnp.concatenate(pieces(value, 2), 0).astype(BF16)


def second_features(tile, row_q, sub):
    spot = jnp.where(sub < 3, tile, 1.0)
    spot = jnp.where(sub < 4, spot, row_q * pltpu.roll(spot, 4, 0))
    value = spot * (1.5 * tile[3:4])
    rows = pieces(value, 3) + [jnp.zeros_like(value)]
    return jnp.concatenate(rows, 0).astype(BF16)


class Pairs:
    def __init__(self, near, tab, mine, feat1, feat2):
        self.near, self.tab, self.mine, self.feat1, self.feat2 = near, tab, mine, feat1, feat2

    def row(self, c, k):
        return RIM + c if k == 0 else self.near[k - 1, c]

    def make(self, c, k, part, odd, even):
        width = odd.shape[1] // 2
        half = width // 2
        source = self.tab[self.row(c, k), :, part * half : part * half + half]
        w = jnp.maximum(contract(source, self.mine[c], 0), 0.0)
        square = w * w
        once, high = w.astype(BF16), square.astype(BF16)
        rows = slice(k * width + part * half, k * width + part * half + half)
        odd[rows, :width] = once
        odd[rows, width:] = once * high
        even[rows, :width] = high
        even[rows, width:] = (square - high.astype(F32)).astype(BF16)

    def fill(self, c, odd, even):
        for k in range(self.near.shape[0] + 1):
            self.make(c, k, 0, odd, even)
            self.make(c, k, 1, odd, even)

    def step(self, c, odd, even, later, next_odd, next_even, sub):
        width = odd.shape[1] // 2
        first = second = 0.0
        for k in range(self.near.shape[0] + 1):
            row = self.row(c, k)
            rows = slice(k * width, k * width + width)
            first = first + contract(self.feat1[row], odd[rows], 1)
            self.make(later, k, 0, next_odd, next_even)
            second = second + contract(self.feat2[row], even[rows], 1)
            self.make(later, k, 1, next_odd, next_even)
        first = first[0:8] + first[8:16]
        first = jnp.where(sub < 4, first[:, :width], first[:, width:])
        second = second[:, :width] + second[:, width:]
        return first, second[0:8] + second[8:16] + second[16:24]


def sweep(pairs, order, start, count, buffers, finish, sub, moves):
    a, b = buffers[0:2], buffers[2:4]
    pairs.fill(order[start], *a)
    moves.need(*range(len(moves.ins)))

    def some(t, carry):
        for k in range(STEP):
            i = STEP * t + k
            now, then = (a, b) if k % 2 == 0 else (b, a)
            c = order[start + i]
            later = order[start + jnp.minimum(i + 1, count - 1)]
            finish(i, c, *pairs.step(c, *now, later, *then, sub))
        return carry

    lax.fori_loop(0, count // STEP, some, 0)


def advance(first, second, tile, row_q, row_rho, row_fluid, active, sub):
    mix = row_q * second + pltpu.roll(second, 4, 0) - first
    speed = pltpu.roll(tile, 4, 0)
    drag = pltpu.roll(first, 4, 0) - speed * row_rho
    acc = tile * mix[3:4] - mix + VISCOSITY * drag
    acc = acc - jnp.where(sub == 2, GRAVITY, 0.0)
    step = TIME_STEP * row_fluid
    speed = speed + step * acc
    place = tile + step * speed
    result = jnp.where(
        sub < 3,
        place,
        jnp.where(sub < 6, pltpu.roll(speed, 3, 0), jnp.where(sub == 6, row_rho, 0.0)),
    )
    return jnp.where(active, result, 0.0)


def rows_and_lanes(width):
    return (
        lax.broadcasted_iota(jnp.int32, (8, width), 0),
        lax.broadcasted_iota(jnp.int32, (1, width), 1),
    )


def forces_moving(
    moves, counts, near, plan, q_below, q_own, q_above, q_rest, feat2_own, tiles, rho, fluid, tab, mine, feat1,
    outbox, feat2, q, moved, *buffers,
):
    cells = rho.shape[0]
    sub, lane = rows_and_lanes(tiles.shape[2])
    moves.need(3, 5, 6, 8)

    def source(i, carry):
        feat2[i] = second_features(tiles[i], q[i], sub)
        return carry

    lax.fori_loop(0, RIM, source, 0, unroll=4)
    lax.fori_loop(RIM + cells, tiles.shape[0], source, 0, unroll=8)
    moves.need(4, 7)
    moves.save(1)
    moves.need(*range(14))

    def finish(i, c, first, second):
        row = pl.ds(c, 1)
        moved[i] = advance(
            first, second, tiles[RIM + c], q[RIM + c], rho[row, :], fluid[row, :], lane < counts[c], sub
        )

    sweep(
        Pairs(near, tab, mine, feat1, feat2), plan, MOVING, MOVERS, buffers, finish, sub, moves
    )
    for t in range(outbox.shape[0] // SLOTS):
        for k in range(SLOTS):
            outbox[t * SLOTS + k] = moved[plan[OUTS + t * SLOTS + k]]


def forces_staying(
    moves, counts, near, plan, tab, mine, feat1, feat2, tiles, q, rho, fluid, stayed, *buffers
):
    sub, lane = rows_and_lanes(tiles.shape[2])
    moves.need(1, 2, 3, 4)

    def finish(i, c, first, second):
        row = pl.ds(c, 1)
        stayed[i] = advance(
            first, second, tiles[RIM + c], q[c], rho[row, :], fluid[row, :], lane < counts[c], sub
        )

    sweep(
        Pairs(near, tab, mine, feat1, feat2), plan, STAYING, stayed.shape[0], buffers, finish, sub, moves
    )


def settle(moves, landing, stayed, inbox, state, density, _):
    cells = state.shape[1]
    me = lax.axis_index("dev")
    moves.need(0, 1)

    def put(place, tile):
        for k in range(6):
            state[k, pl.ds(place, 1), :] = tile[k : k + 1]
        density[pl.ds(place, 1), :] = tile[6:7]

    for i in range(stayed.shape[0]):
        put(landing[1, me] + i, stayed[i])
    for t in range(inbox.shape[0] // SLOTS):

        @pl.when(landing[0, t] < cells)
        def _():
            for k in range(SLOTS):
                put(landing[0, t] + k, inbox[t * SLOTS + k])


def shards(positions, velocities, masses, counts, walls, neighbours, send_cells, owners):
    cells, width = masses.shape
    peers = lax.axis_size("dev")
    total = 2 * RIM + cells + SLOTS * peers
    groups = lax.axis_size("group")
    up = [(i, i + 1) for i in range(groups - 1)]
    down = [(i + 1, i) for i in range(groups - 1)]

    def exchange(x):
        return lax.all_to_all(x, "dev", split_axis=0, concat_axis=0, tiled=True)

    near = neighbours.T
    sends = jnp.swapaxes(send_cells, 2, 3)
    own, send, head, tail, fluid = call(
        prepare,
        4096,
        [counts, sends],
        [positions, velocities, masses, walls],
        [],
        [
            ((cells, 8, width), F32),
            ((SLOTS * peers, 8, width), F32),
            ((RIM, 8, width), F32),
            ((RIM, 8, width), F32),
            ((cells, width), F32),
        ],
    )
    rest = exchange(send)
    below = lax.ppermute(tail, "group", up)
    above = lax.ppermute(head, "group", down)
    row_type, small = ((RIM, 1, width), F32), ((SLOTS * peers, 1, width), F32)
    pair_type, own_type = ((total, 48, width), BF16), ((cells, 48, width), BF16)
    sums, tab_own, mine, jobs = call(
        home,
        4096,
        [near],
        [own],
        [],
        [((cells + 1, 8, width), F32), own_type, own_type, ((PLAN,), jnp.int32)],
        [pltpu.SMEM((256,), jnp.int32)],
    )
    rho, q, q_head, q_tail, send_q, tab, tiles = call(
        densities,
        4096,
        [counts, jobs, sends],
        [below, above, rest, tab_own, own, mine, sums],
        [],
        [
            ((cells, width), F32),
            ((cells, 1, width), F32),
            row_type,
            small,
            small,
            pair_type,
            ((total, 8, width), F32),
        ],
        into=[
            (6, 0, RIM),
            (6, RIM + cells, RIM),
            (6, 2 * RIM + cells, SLOTS * peers),
            (5, RIM, cells),
            (6, RIM, cells),
        ],
    )
    q_below = lax.ppermute(q_tail, "group", up)
    q_rest = exchange(send_q)
    q_above = lax.ppermute(q_head, "group", down)
    plan, landing, feat1, feat2_own = call(
        routing,
        4096,
        [owners],
        [owners, tiles, q],
        [],
        [
            ((PLAN,), jnp.int32),
            ((8, 128), jnp.int32),
            ((total, 16, width), BF16),
            ((cells, 32, width), BF16),
        ],
        [pltpu.SMEM((peers,), jnp.int32)],
    )
    partners = neighbours.shape[1] + 1
    buffers = [pltpu.VMEM((partners * width, 2 * width), BF16)] * 4
    outbox, feat2 = call(
        forces_moving,
        4096,
        [counts, near, plan],
        [q_below, q, q_above, q_rest, feat2_own, tiles, rho, fluid, tab, mine, feat1],
        [],
        [((SLOTS * peers, 8, width), F32), ((total, 32, width), BF16)],
        [pltpu.VMEM((total, 1, width), F32), pltpu.VMEM((MOVERS, 8, width), F32)] + buffers,
        into=[
            (2, 0, RIM),
            (2, RIM, cells),
            (2, RIM + cells, RIM),
            (2, 2 * RIM + cells, SLOTS * peers),
            (1, RIM, cells),
        ],
    )
    inbox = exchange(outbox)
    [stayed] = call(
        forces_staying,
        4096,
        [counts, near, plan],
        [tab, mine, feat1, feat2, tiles, q, rho, fluid],
        [],
        [((cells - MOVERS, 8, width), F32, WIDE)],
        buffers,
    )
    return call(
        settle,
        12000,
        [landing],
        [stayed],
        [inbox],
        [((6, cells, width), F32), ((cells, width), F32)],
        [pltpu.VMEM((cells - MOVERS, 8, width), F32)],
        into=[(2, 0, cells - MOVERS)],
    )


def solution(mesh):
    return jax.shard_map(
        shards,
        mesh=mesh,
        in_specs=(
            P(None, ("group", "dev"), None),
            P(None, ("group", "dev"), None),
            P(("group", "dev"), None),
            P(("group", "dev")),
            P(("group", "dev"), None),
            P(("group", "dev"), None),
            P("group", "dev", None, None),
            P("group", None),
        ),
        out_specs=(P(None, ("group", "dev"), None), P(("group", "dev"), None)),
        check_vma=False,
    )
```

```python
import jax
import jax.numpy as jnp
from jax import lax
from jax.experimental import pallas as pl
from jax.experimental.pallas import tpu as pltpu
from jax.sharding import PartitionSpec as P

RIM = 4
SLOTS = 2
PARTNERS = 4
MOVERS = 16
STEP = 8
WIDE = 512
JOB_ROW, JOB_CELL, JOB_COUNT, MOVING, STAYING, OUTS = 0, 128, 256, 272, 304, 336
COUNTS, SENDS, NEAR, PLAN = 512, 544, 640, 1024
WIDE_ROWS, WIDE_LIST = 4096, 1 << 20
STIFFNESS = 2.0
REST_DENSITY = 0.8
VISCOSITY = 0.5
COHESION = 0.3
ADHESION = 0.8
GRAVITY = 1.0
TIME_STEP = 0.5

F32 = jnp.float32
BF16 = jnp.bfloat16
HBM = pl.BlockSpec(memory_space=pltpu.HBM)
VMEM = pl.BlockSpec(memory_space=pltpu.VMEM)


class Moves:
    def __init__(self, ins, outs):
        self.ins, self.outs = list(ins), list(outs)
        self.waited, self.saved = set(), set()
        for copy in self.ins:
            copy.start()

    def need(self, *which):
        for i in which:
            if i not in self.waited:
                self.waited.add(i)
                self.ins[i].wait()

    def save(self, *which):
        for i in which:
            if i not in self.saved:
                self.saved.add(i)
                self.outs[i].start()


def call(kernel, room, ints, held, near, outs, scratch=(), into=()):
    used = [h[1] if isinstance(h, tuple) else h.shape[0] for h in held]
    held = [h[0] if isinstance(h, tuple) else h for h in held]
    n_in, n_near, n_out = len(ints) + len(held), len(near), len(outs)

    def body(*refs):
        sources, refs = refs[:n_in], refs[n_in:]
        close, refs = refs[:n_near], refs[n_near:]
        targets, refs = refs[:n_out], refs[n_out:]
        inner, refs = list(refs[: n_in - len(into)]), refs[n_in - len(into) :]
        results, refs = refs[:n_out], refs[n_out:]
        sources = [r.at[pl.ds(0, PLAN)] if r.shape == (WIDE_LIST,) else r for r in sources]
        for i, count in enumerate(used):
            sources[len(ints) + i] = sources[len(ints) + i].at[pl.ds(0, count)]
        for i, (out, start, count) in enumerate(into):
            target = (*results, *refs[2:])[out]
            inner.insert(len(ints) + i, target.at[pl.ds(start, count)])
            sources[len(ints) + i] = sources[len(ints) + i].at[pl.ds(0, count)]
        in_sems, out_sems, rest = refs[0], refs[1], refs[2:]
        moves = Moves(
            [pltpu.make_async_copy(a, b, in_sems.at[i]) for i, (a, b) in enumerate(zip(sources, inner))],
            [
                pltpu.make_async_copy(a, b.at[pl.ds(0, a.shape[0])], out_sems.at[i])
                for i, (a, b) in enumerate(zip(results, targets))
            ],
        )
        kernel(moves, *inner, *close, *results, *rest)
        moves.need(*range(n_in))
        moves.save(*range(n_out))
        for copy in moves.outs:
            copy.wait()

    return pl.pallas_call(
        body,
        out_shape=[jax.ShapeDtypeStruct((*o[2:], *o[0][len(o) - 2 :]), o[1]) for o in outs],
        in_specs=[HBM] * n_in + [VMEM] * n_near,
        out_specs=[HBM] * n_out,
        scratch_shapes=[
            pltpu.SMEM((PLAN,) if x.shape == (WIDE_LIST,) else x.shape, x.dtype) for x in ints
        ]
        + [
            pltpu.VMEM((n, *x.shape[1:]), x.dtype)
            for n, x in zip(used[len(into) :], held[len(into) :])
        ]
        + [(pltpu.SMEM if len(o[0]) == 1 else pltpu.VMEM)(*o[:2]) for o in outs]
        + [pltpu.SemaphoreType.DMA((n_in,)), pltpu.SemaphoreType.DMA((n_out,))]
        + list(scratch),
        compiler_params=pltpu.CompilerParams(vmem_limit_bytes=(64 << 20) - (room << 10)),
        name=kernel.__name__,
    )(*ints, *held, *near)


def contract(a, b, dim):
    return lax.dot_general(a, b, (((dim,), (0,)), ((), ())), preferred_element_type=F32)


def pieces(value, count):
    parts = []
    for _ in range(count):
        part = value.astype(BF16).astype(F32)
        parts.append(part)
        value = value - part
    return parts


def prepare(moves, counts, sends, pos, vel, mass, walls, own, send, head, tail, fluid):
    cells, width = mass.shape
    moves.need(*range(6))
    m = mass[...]
    root = jnp.exp(jnp.log(m) * (1.0 / 3.0))
    root = root - (root * root * root - m) / (3.0 * root * root)
    wall = walls[...].astype(F32)
    bond = root * root * (COHESION + (ADHESION - COHESION) * wall)
    free = 1.0 - wall
    lane = lax.broadcasted_iota(jnp.int32, (1, width), 1)
    for c in range(cells):
        row = slice(c, c + 1)
        active = lane < counts[c]
        for k in range(3):
            own[c, k : k + 1, :] = pos[k, row, :]
            own[c, 4 + k : 5 + k, :] = vel[k, row, :]
        own[c, 3:4, :] = jnp.where(active, root[row], 0.0)
        own[c, 7:8, :] = jnp.where(active, bond[row], 0.0)
        fluid[row, :] = jnp.where(active, free[row], 0.0)
    head[...] = own[0:RIM]
    tail[...] = own[cells - RIM : cells]
    moves.save(0, 2, 3, 4)
    for t in range(send.shape[0] // SLOTS):
        for k in range(SLOTS):
            cell = sends[0, 0, k, t]
            tile = own[jnp.maximum(cell, 0)]
            send[t * SLOTS + k] = jnp.where(cell >= 0, tile, 0.0)


def squared(tile, sub):
    return jnp.sum(jnp.where(sub < 3, tile * tile, 0.0), axis=0, keepdims=True)


def source_rows(tile, sub):
    root = tile[3:4]
    far = root * (1.0 - 0.25 * squared(tile, sub))
    value = jnp.where(
        sub < 3,
        tile * (0.5 * root),
        jnp.where(sub == 3, far, jnp.where(sub == 4, -0.25 * root, 0.0)),
    )
    a, b, c = pieces(value, 3)
    return jnp.concatenate([a, b, a, c, a, b], 0).astype(BF16)


def target_rows(tile, sub):
    value = jnp.where(
        sub < 3,
        tile,
        jnp.where(sub == 3, 1.0, jnp.where(sub == 4, squared(tile, sub), 0.0)),
    )
    a, b, c = pieces(value, 3)
    return jnp.concatenate([a, a, b, a, c, b], 0).astype(BF16)


def cubes(source, target):
    w = jnp.maximum(contract(source, target, 0), 0.0)
    return jnp.sum((w * w * w).reshape(w.shape[0] // 8, 8, w.shape[1]), axis=0)


def run_jobs(rows, cells, count, tab, first_row, mine, sums):
    last = mine.shape[0] - 1

    def some(t, carry):
        for k in range(STEP):
            c = cells(t * STEP + k)
            value = cubes(tab[rows(t * STEP + k) - first_row], mine[jnp.minimum(c, last)])
            sums[c] = sums[c] + value
        return carry

    lax.fori_loop(0, lax.div(count + (STEP - 1), STEP), some, 0)


def home(moves, near, counts, sends, tiles, sums, tab, mine, plan, jobs):
    cells, _, width = tiles.shape
    sub, _ = rows_and_lanes(width)
    moves.need(*range(4))

    def build(i, carry):
        tab[i] = source_rows(tiles[i], sub)
        mine[i] = target_rows(tiles[i], sub)
        return carry

    lax.fori_loop(0, cells, build, 0, unroll=8)
    moves.save(1, 2)

    sums[cells] = jnp.zeros((8, width), F32)

    def alone(t, carry):
        local, away = carry
        for k in range(STEP):
            c = t * STEP + k
            sums[c] = cubes(tab[c], mine[c])
            plan[COUNTS + c] = counts[c]
            for n in range(near.shape[0]):
                row = near[n, c]
                inside = (row >= RIM) & (row < RIM + cells)
                jobs[local] = row
                jobs[128 + local] = c
                plan[JOB_ROW + away] = row
                plan[JOB_CELL + away] = c
                local = local + inside.astype(jnp.int32)
                away = away + 1 - inside.astype(jnp.int32)
        return local, away

    local, away = lax.fori_loop(0, cells // STEP, alone, (jnp.int32(0), jnp.int32(0)))
    for t in range(sends.shape[3]):
        for k in range(SLOTS):
            plan[SENDS + t * SLOTS + k] = jnp.maximum(sends[0, 0, k, t], 0)
    for k in range(STEP):
        jobs[local + k] = RIM
        jobs[128 + local + k] = cells
        plan[JOB_ROW + away + k] = RIM
        plan[JOB_CELL + away + k] = cells
    plan[JOB_COUNT] = away
    run_jobs(lambda i: jobs[i], lambda i: jobs[128 + i], local, tab, RIM, mine, sums)
    moves.save(0)


def routing(moves, owners, near, counts, owners_v, tiles, q, plan, landing, feat1, feat2_own, seen):
    cells, _, width = feat2_own.shape
    sub, _ = rows_and_lanes(width)
    moves.need(4, 5)

    def first(i, carry):
        feat1[i] = first_features(tiles[i], sub)
        return carry

    def second(i, carry):
        feat2_own[i] = second_features(tiles[RIM + i], q[i], sub)
        return carry

    lax.fori_loop(0, tiles.shape[0], first, 0, unroll=8)
    lax.fori_loop(0, cells, second, 0, unroll=8)
    moves.save(2, 3)
    me = lax.axis_index("dev")
    moves.need(*range(4))
    for d in range(seen.shape[0]):
        seen[d] = 0
    for i in range(seen.shape[0] * SLOTS):
        plan[OUTS + i] = 0
    moving, staying = jnp.int32(0), jnp.int32(0)
    for c in range(cells):
        to = owners[0, me * cells + c]
        leaves = (to != me).astype(jnp.int32)
        plan[COUNTS + c] = counts[c]
        for k in range(near.shape[0]):
            plan[NEAR + k * cells + c] = near[k, c]
        plan[MOVING + moving] = c
        plan[STAYING + staying] = c
        spot = jnp.where(to != me, to * SLOTS + seen[to], seen.shape[0] * SLOTS)
        plan[OUTS + spot] = moving
        seen[to] = seen[to] + leaves
        moving = moving + leaves
        staying = staying + 1 - leaves
    moves.save(0)
    entries = owners_v.shape[1]
    dev = lax.broadcasted_iota(jnp.int32, (entries, 128), 1)
    entry = lax.broadcasted_iota(jnp.int32, (entries, 128), 0)
    belongs = (entry >= dev * cells) & (entry < dev * cells + cells)
    ours = jnp.broadcast_to((owners_v[...] == me).astype(F32), (8, entries)).astype(BF16)
    arrivals = contract(ours, jnp.where(belongs, 1.0, 0.0).astype(BF16), 1)
    earlier = lax.broadcasted_iota(jnp.int32, (128, 128), 0) < lax.broadcasted_iota(
        jnp.int32, (128, 128), 1
    )
    before = contract(arrivals.astype(BF16), jnp.where(earlier, 1.0, 0.0).astype(BF16), 1)
    lane = lax.broadcasted_iota(jnp.int32, (8, 128), 1)
    kind = lax.broadcasted_iota(jnp.int32, (8, 128), 0)
    place = before.astype(jnp.int32)
    comes = (arrivals > 0.0) & (lane != me)
    landing[...] = jnp.where((kind == 0) & ~comes, cells, place)


def densities(
    moves, plan, below, above, rest, tab_own, tiles_own, mine, sums,
    rho, q, q_head, q_tail, send_q, tab, tiles,
):
    cells, _, width = mine.shape
    sub, lane = rows_and_lanes(width)
    moves.need(1, 2, 3)
    for start, count in ((0, RIM), (RIM + cells, tab.shape[0] - RIM - cells)):

        def source(i, carry, start=start):
            tab[start + i] = source_rows(tiles[start + i], sub)
            return carry

        lax.fori_loop(0, count, source, 0, unroll=4)

    moves.need(*range(8))
    moves.save(5, 6)
    run_jobs(
        lambda i: plan[JOB_ROW + i], lambda i: plan[JOB_CELL + i], plan[JOB_COUNT], tab, 0, mine, sums
    )
    for c in range(cells):
        row = jnp.sum(sums[c], axis=0, keepdims=True)
        active = lane < plan[COUNTS + c]
        safe = jnp.where(active, row, 1.0)
        value = STIFFNESS * (row - REST_DENSITY) / (safe * safe)
        q[c] = jnp.where(active, value, 0.0)
        rho[c : c + 1, :] = jnp.where(active, row, 0.0)
    q_tail[...] = jnp.zeros(q_tail.shape, F32)
    for r in range(RIM):
        q_head[r] = q[r]
        q_tail[r] = q[cells - RIM + r]
    for t in range(send_q.shape[0] // SLOTS):
        for k in range(SLOTS):
            send_q[t * SLOTS + k] = q[plan[SENDS + t * SLOTS + k]]


def first_features(tile, sub):
    bond = tile[7:8]
    value = jnp.where(
        sub < 3,
        tile * bond,
        jnp.where(sub == 3, bond, jnp.where(sub < 7, tile, 0.0)),
    )
    return jnp.concatenate(pieces(value, 2), 0).astype(BF16)


def second_features(tile, row_q, sub):
    spot = jnp.where(sub < 3, tile, 1.0)
    spot = jnp.where(sub < 4, spot, row_q * pltpu.roll(spot, 4, 0))
    value = spot * (1.5 * tile[3:4])
    rows = pieces(value, 3) + [jnp.zeros_like(value)]
    return jnp.concatenate(rows, 0).astype(BF16)


class Pairs:
    def __init__(self, plan, tab, mine, feat1, feat2, partners):
        self.plan, self.tab, self.mine, self.feat1, self.feat2 = plan, tab, mine, feat1, feat2
        self.partners = partners

    def row(self, c, k):
        return RIM + c if k == 0 else self.plan[NEAR + (k - 1) * self.mine.shape[0] + c]

    def make(self, c, k, part, odd, even):
        width = odd.shape[1] // 2
        half = width // 2
        source = self.tab[self.row(c, k), :, part * half : part * half + half]
        w = jnp.maximum(contract(source, self.mine[c], 0), 0.0)
        square = w * w
        once, high = w.astype(BF16), square.astype(BF16)
        rows = slice(k * width + part * half, k * width + part * half + half)
        odd[rows, :width] = once
        odd[rows, width:] = once * high
        even[rows, :width] = high
        even[rows, width:] = (square - high.astype(F32)).astype(BF16)

    def fill(self, c, odd, even):
        for k in range(self.partners):
            self.make(c, k, 0, odd, even)
            self.make(c, k, 1, odd, even)

    def step(self, c, odd, even, later, next_odd, next_even, sub):
        width = odd.shape[1] // 2
        first = second = 0.0
        for k in range(self.partners):
            row = self.row(c, k)
            rows = slice(k * width, k * width + width)
            first = first + contract(self.feat1[row], odd[rows], 1)
            self.make(later, k, 0, next_odd, next_even)
            second = second + contract(self.feat2[row], even[rows], 1)
            self.make(later, k, 1, next_odd, next_even)
        first = first[0:8] + first[8:16]
        first = jnp.where(sub < 4, first[:, :width], first[:, width:])
        second = second[:, :width] + second[:, width:]
        return first, second[0:8] + second[8:16] + second[16:24]


def sweep(pairs, order, start, count, buffers, finish, sub, moves):
    a, b = buffers[0:2], buffers[2:4]
    pairs.fill(order[start], *a)
    moves.need(*range(len(moves.ins)))

    def some(t, carry):
        for k in range(STEP):
            i = STEP * t + k
            now, then = (a, b) if k % 2 == 0 else (b, a)
            c = order[start + i]
            later = order[start + jnp.minimum(i + 1, count - 1)]
            finish(i, c, *pairs.step(c, *now, later, *then, sub))
        return carry

    lax.fori_loop(0, count // STEP, some, 0)


def advance(first, second, tile, row_q, row_rho, row_fluid, active, sub):
    mix = row_q * second + pltpu.roll(second, 4, 0) - first
    speed = pltpu.roll(tile, 4, 0)
    drag = pltpu.roll(first, 4, 0) - speed * row_rho
    acc = tile * mix[3:4] - mix + VISCOSITY * drag
    acc = acc - jnp.where(sub == 2, GRAVITY, 0.0)
    step = TIME_STEP * row_fluid
    speed = speed + step * acc
    place = tile + step * speed
    result = jnp.where(
        sub < 3,
        place,
        jnp.where(sub < 6, pltpu.roll(speed, 3, 0), jnp.where(sub == 6, row_rho, 0.0)),
    )
    return jnp.where(active, result, 0.0)


def rows_and_lanes(width):
    return (
        lax.broadcasted_iota(jnp.int32, (8, width), 0),
        lax.broadcasted_iota(jnp.int32, (1, width), 1),
    )


def forces_moving(
    moves, plan, q_below, q_own, q_above, q_rest, feat2_own, tiles, rho, fluid, tab, mine, feat1,
    outbox, feat2, q, moved, *buffers,
):
    cells = rho.shape[0]
    sub, lane = rows_and_lanes(tiles.shape[2])
    moves.need(1, 3, 4, 6)

    def source(i, carry):
        feat2[i] = second_features(tiles[i], q[i], sub)
        return carry

    lax.fori_loop(0, RIM, source, 0, unroll=4)
    lax.fori_loop(RIM + cells, tiles.shape[0], source, 0, unroll=8)
    moves.need(2, 5)
    moves.save(1)
    moves.need(*range(12))

    def finish(i, c, first, second):
        row = pl.ds(c, 1)
        moved[i] = advance(
            first, second, tiles[RIM + c], q[RIM + c], rho[row, :], fluid[row, :], lane < plan[COUNTS + c], sub
        )

    sweep(
        Pairs(plan, tab, mine, feat1, feat2, PARTNERS), plan, MOVING, MOVERS, buffers, finish, sub, moves
    )
    for t in range(outbox.shape[0] // SLOTS):
        for k in range(SLOTS):
            outbox[t * SLOTS + k] = moved[plan[OUTS + t * SLOTS + k]]


def forces_staying(
    moves, plan, tab, mine, feat1, feat2, tiles, q, rho, fluid, stayed, *buffers
):
    sub, lane = rows_and_lanes(tiles.shape[2])
    moves.need(0, 1, 2)

    def finish(i, c, first, second):
        row = pl.ds(c, 1)
        stayed[i] = advance(
            first, second, tiles[RIM + c], q[c], rho[row, :], fluid[row, :], lane < plan[COUNTS + c], sub
        )

    sweep(
        Pairs(plan, tab, mine, feat1, feat2, PARTNERS), plan, STAYING, stayed.shape[0], buffers, finish, sub, moves
    )


def settle(moves, landing, stayed, inbox, state, density, _):
    cells = state.shape[1]
    me = lax.axis_index("dev")
    moves.need(0, 1)

    def put(place, tile):
        for k in range(6):
            state[k, pl.ds(place, 1), :] = tile[k : k + 1]
        density[pl.ds(place, 1), :] = tile[6:7]

    for i in range(stayed.shape[0]):
        put(landing[1, me] + i, stayed[i])
    for t in range(inbox.shape[0] // SLOTS):

        @pl.when(landing[0, t] < cells)
        def _():
            for k in range(SLOTS):
                put(landing[0, t] + k, inbox[t * SLOTS + k])


def shards(positions, velocities, masses, counts, walls, neighbours, send_cells, owners):
    cells, width = masses.shape
    peers = lax.axis_size("dev")
    total = 2 * RIM + cells + SLOTS * peers
    groups = lax.axis_size("group")
    up = [(i, i + 1) for i in range(groups - 1)]
    down = [(i + 1, i) for i in range(groups - 1)]

    def exchange(x):
        return lax.all_to_all(x, "dev", split_axis=0, concat_axis=0, tiled=True)

    near = neighbours.T
    sends = jnp.swapaxes(send_cells, 2, 3)
    own, send, head, tail, fluid = call(
        prepare,
        4096,
        [counts, sends],
        [positions, velocities, masses, walls],
        [],
        [
            ((cells, 8, width), F32, WIDE),
            ((SLOTS * peers, 8, width), F32),
            ((RIM, 8, width), F32),
            ((RIM, 8, width), F32),
            ((cells, width), F32, WIDE_ROWS),
        ],
    )
    rest = exchange(send)
    below = lax.ppermute(tail, "group", up)
    above = lax.ppermute(head, "group", down)
    row_type, small = ((RIM, 1, width), F32), ((SLOTS * peers, 1, width), F32)
    plan_type = ((PLAN,), jnp.int32, WIDE_LIST)
    pair_type, own_type = ((total, 48, width), BF16), ((cells, 48, width), BF16)
    sums, tab_own, mine, jobs = call(
        home,
        4096,
        [near, counts, sends],
        [(own, cells)],
        [],
        [((cells + 1, 8, width), F32, WIDE), own_type, own_type, plan_type],
        [pltpu.SMEM((256,), jnp.int32)],
    )
    rho, q, q_head, q_tail, send_q, tab, tiles = call(
        densities,
        11400,
        [jobs],
        [below, above, rest, tab_own, (own, cells), mine, (sums, cells + 1)],
        [],
        [
            ((cells, width), F32, WIDE_ROWS),
            ((cells, 1, width), F32, WIDE_ROWS),
            row_type,
            small,
            small,
            pair_type,
            ((total, 8, width), F32),
        ],
        into=[
            (6, 0, RIM),
            (6, RIM + cells, RIM),
            (6, 2 * RIM + cells, SLOTS * peers),
            (5, RIM, cells),
            (6, RIM, cells),
        ],
    )
    q_below = lax.ppermute(q_tail, "group", up)
    q_rest = exchange(send_q)
    q_above = lax.ppermute(q_head, "group", down)
    plan, landing, feat1, feat2_own = call(
        routing,
        4096,
        [owners, near, counts],
        [owners, tiles, (q, cells)],
        [],
        [
            plan_type,
            ((8, 128), jnp.int32),
            ((total, 16, width), BF16),
            ((cells, 32, width), BF16),
        ],
        [pltpu.SMEM((peers,), jnp.int32)],
    )
    partners = neighbours.shape[1] + 1
    buffers = [pltpu.VMEM((partners * width, 2 * width), BF16)] * 4
    outbox, feat2 = call(
        forces_moving,
        10700,
        [plan],
        [
            q_below,
            (q, cells),
            q_above,
            q_rest,
            feat2_own,
            tiles,
            (rho, cells),
            (fluid, cells),
            tab,
            mine,
            feat1,
        ],
        [],
        [((SLOTS * peers, 8, width), F32), ((total, 32, width), BF16)],
        [pltpu.VMEM((total, 1, width), F32), pltpu.VMEM((MOVERS, 8, width), F32)] + buffers,
        into=[
            (2, 0, RIM),
            (2, RIM, cells),
            (2, RIM + cells, RIM),
            (2, 2 * RIM + cells, SLOTS * peers),
            (1, RIM, cells),
        ],
    )
    inbox = exchange(outbox)
    [stayed] = call(
        forces_staying,
        4096,
        [plan],
        [tab, mine, feat1, feat2, tiles, (q, cells), (rho, cells), (fluid, cells)],
        [],
        [((cells - MOVERS, 8, width), F32, WIDE)],
        buffers,
    )
    return call(
        settle,
        12000,
        [landing],
        [stayed],
        [inbox],
        [((6, cells, width), F32), ((cells, width), F32)],
        [pltpu.VMEM((cells - MOVERS, 8, width), F32)],
        into=[(2, 0, cells - MOVERS)],
    )


def solution(mesh):
    return jax.shard_map(
        shards,
        mesh=mesh,
        in_specs=(
            P(None, ("group", "dev"), None),
            P(None, ("group", "dev"), None),
            P(("group", "dev"), None),
            P(("group", "dev")),
            P(("group", "dev"), None),
            P(("group", "dev"), None),
            P("group", "dev", None, None),
            P("group", None),
        ),
        out_specs=(P(None, ("group", "dev"), None), P(("group", "dev"), None)),
        check_vma=False,
    )
```

```python
import jax
import jax.numpy as jnp
from jax import lax
from jax.experimental import pallas as pl
from jax.experimental.pallas import tpu as pltpu
from jax.sharding import PartitionSpec as P

RIM = 4
SLOTS = 2
PARTNERS = 4
MOVERS = 16
STEP = 8
WIDE = 512
JOB_ROW, JOB_CELL, JOB_COUNT, MOVING, STAYING, OUTS = 0, 128, 256, 272, 304, 336
COUNTS, SENDS, NEAR, PLAN = 512, 544, 640, 1024
WIDE_ROWS, WIDE_LIST = 4096, 1 << 20
STIFFNESS = 2.0
REST_DENSITY = 0.8
VISCOSITY = 0.5
COHESION = 0.3
ADHESION = 0.8
GRAVITY = 1.0
TIME_STEP = 0.5

F32 = jnp.float32
BF16 = jnp.bfloat16
HBM = pl.BlockSpec(memory_space=pltpu.HBM)
VMEM = pl.BlockSpec(memory_space=pltpu.VMEM)


class Moves:
    def __init__(self, ins, outs):
        self.ins, self.outs = list(ins), list(outs)
        self.waited, self.saved = set(), set()
        for copy in self.ins:
            copy.start()

    def need(self, *which):
        for i in which:
            if i not in self.waited:
                self.waited.add(i)
                self.ins[i].wait()

    def save(self, *which):
        for i in which:
            if i not in self.saved:
                self.saved.add(i)
                self.outs[i].start()


def call(kernel, room, ints, held, near, outs, scratch=(), into=()):
    used = [h[1] if isinstance(h, tuple) else h.shape[0] for h in held]
    held = [h[0] if isinstance(h, tuple) else h for h in held]
    n_in, n_near, n_out = len(ints) + len(held), len(near), len(outs)

    def body(*refs):
        sources, refs = refs[:n_in], refs[n_in:]
        close, refs = refs[:n_near], refs[n_near:]
        targets, refs = refs[:n_out], refs[n_out:]
        inner, refs = list(refs[: n_in - len(into)]), refs[n_in - len(into) :]
        results, refs = refs[:n_out], refs[n_out:]
        sources = [r.at[pl.ds(0, PLAN)] if r.shape == (WIDE_LIST,) else r for r in sources]
        for i, count in enumerate(used):
            sources[len(ints) + i] = sources[len(ints) + i].at[pl.ds(0, count)]
        for i, (out, start, count) in enumerate(into):
            target = (*results, *refs[2:])[out]
            inner.insert(len(ints) + i, target.at[pl.ds(start, count)])
            sources[len(ints) + i] = sources[len(ints) + i].at[pl.ds(0, count)]
        in_sems, out_sems, rest = refs[0], refs[1], refs[2:]
        moves = Moves(
            [pltpu.make_async_copy(a, b, in_sems.at[i]) for i, (a, b) in enumerate(zip(sources, inner))],
            [
                pltpu.make_async_copy(a, b.at[pl.ds(0, a.shape[0])], out_sems.at[i])
                for i, (a, b) in enumerate(zip(results, targets))
            ],
        )
        kernel(moves, *inner, *close, *results, *rest)
        moves.need(*range(n_in))
        moves.save(*range(n_out))
        for copy in moves.outs:
            copy.wait()

    return pl.pallas_call(
        body,
        out_shape=[jax.ShapeDtypeStruct((*o[2:], *o[0][len(o) - 2 :]), o[1]) for o in outs],
        in_specs=[HBM] * n_in + [VMEM] * n_near,
        out_specs=[HBM] * n_out,
        scratch_shapes=[
            pltpu.SMEM((PLAN,) if x.shape == (WIDE_LIST,) else x.shape, x.dtype) for x in ints
        ]
        + [
            pltpu.VMEM((n, *x.shape[1:]), x.dtype)
            for n, x in zip(used[len(into) :], held[len(into) :])
        ]
        + [(pltpu.SMEM if len(o[0]) == 1 else pltpu.VMEM)(*o[:2]) for o in outs]
        + [pltpu.SemaphoreType.DMA((n_in,)), pltpu.SemaphoreType.DMA((n_out,))]
        + list(scratch),
        compiler_params=pltpu.CompilerParams(vmem_limit_bytes=(64 << 20) - (room << 10)),
        name=kernel.__name__,
    )(*ints, *held, *near)


def contract(a, b, dim):
    return lax.dot_general(a, b, (((dim,), (0,)), ((), ())), preferred_element_type=F32)


def pieces(value, count):
    parts = []
    for _ in range(count):
        part = value.astype(BF16).astype(F32)
        parts.append(part)
        value = value - part
    return parts


def prepare(moves, counts, sends, pos, vel, mass, walls, own, send, head, tail, fluid):
    cells, width = mass.shape
    moves.need(*range(6))
    m = mass[...]
    root = jnp.exp(jnp.log(m) * (1.0 / 3.0))
    root = root - (root * root * root - m) / (3.0 * root * root)
    wall = walls[...].astype(F32)
    bond = root * root * (COHESION + (ADHESION - COHESION) * wall)
    free = 1.0 - wall
    lane = lax.broadcasted_iota(jnp.int32, (1, width), 1)
    for c in range(cells):
        row = slice(c, c + 1)
        active = lane < counts[c]
        for k in range(3):
            own[c, k : k + 1, :] = pos[k, row, :]
            own[c, 4 + k : 5 + k, :] = vel[k, row, :]
        own[c, 3:4, :] = jnp.where(active, root[row], 0.0)
        own[c, 7:8, :] = jnp.where(active, bond[row], 0.0)
        fluid[row, :] = jnp.where(active, free[row], 0.0)
    head[...] = own[0:RIM]
    tail[...] = own[cells - RIM : cells]
    moves.save(0, 2, 3, 4)
    for t in range(send.shape[0] // SLOTS):
        for k in range(SLOTS):
            cell = sends[0, 0, k, t]
            tile = own[jnp.maximum(cell, 0)]
            send[t * SLOTS + k] = jnp.where(cell >= 0, tile, 0.0)


def squared(tile, sub):
    return jnp.sum(jnp.where(sub < 3, tile * tile, 0.0), axis=0, keepdims=True)


def source_rows(tile, sub):
    root = tile[3:4]
    far = root * (1.0 - 0.25 * squared(tile, sub))
    value = jnp.where(
        sub < 3,
        tile * (0.5 * root),
        jnp.where(sub == 3, far, jnp.where(sub == 4, -0.25 * root, 0.0)),
    )
    a, b, c = pieces(value, 3)
    return jnp.concatenate([a, b, a, c, a, b], 0).astype(BF16)


def target_rows(tile, sub):
    value = jnp.where(
        sub < 3,
        tile,
        jnp.where(sub == 3, 1.0, jnp.where(sub == 4, squared(tile, sub), 0.0)),
    )
    a, b, c = pieces(value, 3)
    return jnp.concatenate([a, a, b, a, c, b], 0).astype(BF16)


def cubes(source, target):
    w = jnp.maximum(contract(source, target, 0), 0.0)
    return jnp.sum((w * w * w).reshape(w.shape[0] // 8, 8, w.shape[1]), axis=0)


def run_jobs(rows, cells, count, tab, first_row, mine, sums):
    last = mine.shape[0] - 1

    def some(t, carry):
        for k in range(STEP):
            c = cells(t * STEP + k)
            value = cubes(tab[rows(t * STEP + k) - first_row], mine[jnp.minimum(c, last)])
            sums[c] = sums[c] + value
        return carry

    lax.fori_loop(0, lax.div(count + (STEP - 1), STEP), some, 0)


def home(moves, near, counts, sends, tiles, sums, tab, mine, plan, jobs):
    cells, _, width = tiles.shape
    sub, _ = rows_and_lanes(width)
    moves.need(*range(4))

    def build(i, carry):
        tab[i] = source_rows(tiles[i], sub)
        mine[i] = target_rows(tiles[i], sub)
        return carry

    lax.fori_loop(0, cells, build, 0, unroll=8)
    moves.save(1, 2)

    sums[cells] = jnp.zeros((8, width), F32)

    def alone(t, carry):
        local, away = carry
        for k in range(STEP):
            c = t * STEP + k
            sums[c] = cubes(tab[c], mine[c])
            plan[COUNTS + c] = counts[c]
            for n in range(near.shape[0]):
                row = near[n, c]
                inside = (row >= RIM) & (row < RIM + cells)
                jobs[local] = row
                jobs[128 + local] = c
                plan[JOB_ROW + away] = row
                plan[JOB_CELL + away] = c
                local = local + inside.astype(jnp.int32)
                away = away + 1 - inside.astype(jnp.int32)
        return local, away

    local, away = lax.fori_loop(0, cells // STEP, alone, (jnp.int32(0), jnp.int32(0)))
    for t in range(sends.shape[3]):
        for k in range(SLOTS):
            plan[SENDS + t * SLOTS + k] = jnp.maximum(sends[0, 0, k, t], 0)
    for k in range(STEP):
        jobs[local + k] = RIM
        jobs[128 + local + k] = cells
        plan[JOB_ROW + away + k] = RIM
        plan[JOB_CELL + away + k] = cells
    plan[JOB_COUNT] = away
    run_jobs(lambda i: jobs[i], lambda i: jobs[128 + i], local, tab, RIM, mine, sums)
    moves.save(0)


def routing(moves, owners, near, counts, owners_v, tiles, q, plan, landing, feat1, feat2_own, seen):
    cells, _, width = feat2_own.shape
    sub, _ = rows_and_lanes(width)
    moves.need(4, 5)

    def first(i, carry):
        feat1[i] = first_features(tiles[i], sub)
        return carry

    def second(i, carry):
        feat2_own[i] = second_features(tiles[RIM + i], q[i], sub)
        return carry

    lax.fori_loop(0, tiles.shape[0], first, 0, unroll=8)
    lax.fori_loop(0, cells, second, 0, unroll=8)
    moves.save(2, 3)
    me = lax.axis_index("dev")
    moves.need(*range(4))
    for d in range(seen.shape[0]):
        seen[d] = 0
    for i in range(seen.shape[0] * SLOTS):
        plan[OUTS + i] = 0
    moving, staying = jnp.int32(0), jnp.int32(0)
    for c in range(cells):
        to = owners[0, me * cells + c]
        leaves = (to != me).astype(jnp.int32)
        plan[COUNTS + c] = counts[c]
        for k in range(near.shape[0]):
            plan[NEAR + k * cells + c] = near[k, c]
        plan[MOVING + moving] = c
        plan[STAYING + staying] = c
        spot = jnp.where(to != me, to * SLOTS + seen[to], seen.shape[0] * SLOTS)
        plan[OUTS + spot] = moving
        seen[to] = seen[to] + leaves
        moving = moving + leaves
        staying = staying + 1 - leaves
    moves.save(0)
    entries = owners_v.shape[1]
    dev = lax.broadcasted_iota(jnp.int32, (entries, 128), 1)
    entry = lax.broadcasted_iota(jnp.int32, (entries, 128), 0)
    belongs = (entry >= dev * cells) & (entry < dev * cells + cells)
    ours = jnp.broadcast_to((owners_v[...] == me).astype(F32), (8, entries)).astype(BF16)
    arrivals = contract(ours, jnp.where(belongs, 1.0, 0.0).astype(BF16), 1)
    earlier = lax.broadcasted_iota(jnp.int32, (128, 128), 0) < lax.broadcasted_iota(
        jnp.int32, (128, 128), 1
    )
    before = contract(arrivals.astype(BF16), jnp.where(earlier, 1.0, 0.0).astype(BF16), 1)
    lane = lax.broadcasted_iota(jnp.int32, (8, 128), 1)
    kind = lax.broadcasted_iota(jnp.int32, (8, 128), 0)
    place = before.astype(jnp.int32)
    comes = (arrivals > 0.0) & (lane != me)
    landing[...] = jnp.where((kind == 0) & ~comes, cells, place)


def densities(
    moves, plan, below, above, rest, tab_own, tiles_own, mine, sums,
    rho, q, q_head, q_tail, send_q, tab, tiles,
):
    cells, _, width = mine.shape
    sub, lane = rows_and_lanes(width)
    moves.need(1, 2, 3)
    for start, count in ((0, RIM), (RIM + cells, tab.shape[0] - RIM - cells)):

        def source(i, carry, start=start):
            tab[start + i] = source_rows(tiles[start + i], sub)
            return carry

        lax.fori_loop(0, count, source, 0, unroll=4)

    moves.need(*range(8))
    moves.save(5, 6)
    run_jobs(
        lambda i: plan[JOB_ROW + i], lambda i: plan[JOB_CELL + i], plan[JOB_COUNT], tab, 0, mine, sums
    )
    for c in range(cells):
        row = jnp.sum(sums[c], axis=0, keepdims=True)
        active = lane < plan[COUNTS + c]
        safe = jnp.where(active, row, 1.0)
        value = STIFFNESS * (row - REST_DENSITY) / (safe * safe)
        q[c] = jnp.where(active, value, 0.0)
        rho[c : c + 1, :] = jnp.where(active, row, 0.0)
    for r in range(RIM):
        q_head[r] = q[r]
        q_tail[r] = q[cells - RIM + r]
    for t in range(send_q.shape[0] // SLOTS):
        for k in range(SLOTS):
            send_q[t * SLOTS + k] = q[plan[SENDS + t * SLOTS + k]]


def first_features(tile, sub):
    bond = tile[7:8]
    value = jnp.where(
        sub < 3,
        tile * bond,
        jnp.where(sub == 3, bond, jnp.where(sub < 7, tile, 0.0)),
    )
    return jnp.concatenate(pieces(value, 2), 0).astype(BF16)


def second_features(tile, row_q, sub):
    spot = jnp.where(sub < 3, tile, 1.0)
    spot = jnp.where(sub < 4, spot, row_q * pltpu.roll(spot, 4, 0))
    value = spot * (1.5 * tile[3:4])
    rows = pieces(value, 3) + [jnp.zeros_like(value)]
    return jnp.concatenate(rows, 0).astype(BF16)


class Pairs:
    def __init__(self, plan, tab, mine, feat1, feat2, partners):
        self.plan, self.tab, self.mine, self.feat1, self.feat2 = plan, tab, mine, feat1, feat2
        self.partners = partners

    def row(self, c, k):
        return RIM + c if k == 0 else self.plan[NEAR + (k - 1) * self.mine.shape[0] + c]

    def make(self, c, k, part, odd, even):
        width = odd.shape[1] // 2
        half = width // 2
        source = self.tab[self.row(c, k), :, part * half : part * half + half]
        w = jnp.maximum(contract(source, self.mine[c], 0), 0.0)
        square = w * w
        once, high = w.astype(BF16), square.astype(BF16)
        rows = slice(k * width + part * half, k * width + part * half + half)
        odd[rows, :width] = once
        odd[rows, width:] = once * high
        even[rows, :width] = high
        even[rows, width:] = (square - high.astype(F32)).astype(BF16)

    def fill(self, c, odd, even):
        for k in range(self.partners):
            self.make(c, k, 0, odd, even)
            self.make(c, k, 1, odd, even)

    def step(self, c, odd, even, later, next_odd, next_even, sub):
        width = odd.shape[1] // 2
        first = second = 0.0
        for k in range(self.partners):
            row = self.row(c, k)
            rows = slice(k * width, k * width + width)
            first = first + contract(self.feat1[row], odd[rows], 1)
            self.make(later, k, 0, next_odd, next_even)
            second = second + contract(self.feat2[row], even[rows], 1)
            self.make(later, k, 1, next_odd, next_even)
        first = first[0:8] + first[8:16]
        first = jnp.where(sub < 4, first[:, :width], first[:, width:])
        second = second[:, :width] + second[:, width:]
        return first, second[0:8] + second[8:16] + second[16:24]


def sweep(pairs, order, start, count, buffers, finish, sub, moves):
    a, b = buffers[0:2], buffers[2:4]
    pairs.fill(order[start], *a)
    moves.need(*range(len(moves.ins)))

    def some(t, carry):
        for k in range(STEP):
            i = STEP * t + k
            now, then = (a, b) if k % 2 == 0 else (b, a)
            c = order[start + i]
            later = order[start + jnp.minimum(i + 1, count - 1)]
            finish(i, c, *pairs.step(c, *now, later, *then, sub))
        return carry

    lax.fori_loop(0, count // STEP, some, 0)


def advance(first, second, tile, row_q, row_rho, row_fluid, active, sub):
    mix = row_q * second + pltpu.roll(second, 4, 0) - first
    speed = pltpu.roll(tile, 4, 0)
    drag = pltpu.roll(first, 4, 0) - speed * row_rho
    acc = tile * mix[3:4] - mix + VISCOSITY * drag
    acc = acc - jnp.where(sub == 2, GRAVITY, 0.0)
    step = TIME_STEP * row_fluid
    speed = speed + step * acc
    place = tile + step * speed
    result = jnp.where(
        sub < 3,
        place,
        jnp.where(sub < 6, pltpu.roll(speed, 3, 0), jnp.where(sub == 6, row_rho, 0.0)),
    )
    return jnp.where(active, result, 0.0)


def rows_and_lanes(width):
    return (
        lax.broadcasted_iota(jnp.int32, (8, width), 0),
        lax.broadcasted_iota(jnp.int32, (1, width), 1),
    )


def forces_moving(
    moves, plan, q_below, q_own, q_above, q_rest, feat2_own, tiles, rho, fluid, tab, mine, feat1,
    outbox, feat2, q, moved, *buffers,
):
    cells = rho.shape[0]
    sub, lane = rows_and_lanes(tiles.shape[2])
    moves.need(1, 3, 4, 6)

    def source(i, carry):
        feat2[i] = second_features(tiles[i], q[i], sub)
        return carry

    lax.fori_loop(0, RIM, source, 0, unroll=4)
    lax.fori_loop(RIM + cells, tiles.shape[0], source, 0, unroll=8)
    moves.need(2, 5)
    moves.save(1)
    moves.need(*range(12))

    def finish(i, c, first, second):
        row = pl.ds(c, 1)
        moved[i] = advance(
            first, second, tiles[RIM + c], q[RIM + c], rho[row, :], fluid[row, :], lane < plan[COUNTS + c], sub
        )

    sweep(
        Pairs(plan, tab, mine, feat1, feat2, PARTNERS), plan, MOVING, MOVERS, buffers, finish, sub, moves
    )
    for t in range(outbox.shape[0] // SLOTS):
        for k in range(SLOTS):
            outbox[t * SLOTS + k] = moved[plan[OUTS + t * SLOTS + k]]


def forces_staying(
    moves, plan, tab, mine, feat1, feat2, tiles, q, rho, fluid, stayed, *buffers
):
    sub, lane = rows_and_lanes(tiles.shape[2])
    moves.need(0, 1, 2)

    def finish(i, c, first, second):
        row = pl.ds(c, 1)
        stayed[i] = advance(
            first, second, tiles[RIM + c], q[c], rho[row, :], fluid[row, :], lane < plan[COUNTS + c], sub
        )

    sweep(
        Pairs(plan, tab, mine, feat1, feat2, PARTNERS), plan, STAYING, stayed.shape[0], buffers, finish, sub, moves
    )


def settle(moves, landing, stayed, inbox, state, density, _):
    cells = state.shape[1]
    me = lax.axis_index("dev")
    moves.need(0, 1)

    def put(place, tile):
        for k in range(6):
            state[k, pl.ds(place, 1), :] = tile[k : k + 1]
        density[pl.ds(place, 1), :] = tile[6:7]

    for i in range(stayed.shape[0]):
        put(landing[1, me] + i, stayed[i])
    for t in range(inbox.shape[0] // SLOTS):

        @pl.when(landing[0, t] < cells)
        def _():
            for k in range(SLOTS):
                put(landing[0, t] + k, inbox[t * SLOTS + k])


def shards(positions, velocities, masses, counts, walls, neighbours, send_cells, owners):
    cells, width = masses.shape
    peers = lax.axis_size("dev")
    total = 2 * RIM + cells + SLOTS * peers
    groups = lax.axis_size("group")
    up = [(i, i + 1) for i in range(groups - 1)]
    down = [(i + 1, i) for i in range(groups - 1)]

    def exchange(x):
        return lax.all_to_all(x, "dev", split_axis=0, concat_axis=0, tiled=True)

    near = neighbours.T
    sends = jnp.swapaxes(send_cells, 2, 3)
    own, send, head, tail, fluid = call(
        prepare,
        4096,
        [counts, sends],
        [positions, velocities, masses, walls],
        [],
        [
            ((cells, 8, width), F32, WIDE),
            ((SLOTS * peers, 8, width), F32),
            ((RIM, 8, width), F32),
            ((RIM, 8, width), F32),
            ((cells, width), F32, WIDE_ROWS),
        ],
    )
    rest = exchange(send)
    below = lax.ppermute(tail, "group", up)
    above = lax.ppermute(head, "group", down)
    row_type, small = ((RIM, 1, width), F32), ((SLOTS * peers, 1, width), F32)
    plan_type = ((PLAN,), jnp.int32, WIDE_LIST)
    pair_type, own_type = ((total, 48, width), BF16), ((cells, 48, width), BF16)
    sums, tab_own, mine, jobs = call(
        home,
        4096,
        [near, counts, sends],
        [(own, cells)],
        [],
        [((cells + 1, 8, width), F32, WIDE), own_type, own_type, plan_type],
        [pltpu.SMEM((256,), jnp.int32)],
    )
    rho, q, q_head, q_tail, send_q, tab, tiles = call(
        densities,
        11400,
        [jobs],
        [below, above, rest, tab_own, (own, cells), mine, (sums, cells + 1)],
        [],
        [
            ((cells, width), F32, WIDE_ROWS),
            ((cells, 1, width), F32, WIDE_ROWS),
            row_type,
            row_type,
            small,
            pair_type,
            ((total, 8, width), F32),
        ],
        into=[
            (6, 0, RIM),
            (6, RIM + cells, RIM),
            (6, 2 * RIM + cells, SLOTS * peers),
            (5, RIM, cells),
            (6, RIM, cells),
        ],
    )
    q_rest = exchange(send_q)
    q_below = lax.ppermute(q_tail, "group", up)
    q_above = lax.ppermute(q_head, "group", down)
    plan, landing, feat1, feat2_own = call(
        routing,
        4096,
        [owners, near, counts],
        [owners, tiles, (q, cells)],
        [],
        [
            plan_type,
            ((8, 128), jnp.int32),
            ((total, 16, width), BF16),
            ((cells, 32, width), BF16),
        ],
        [pltpu.SMEM((peers,), jnp.int32)],
    )
    partners = neighbours.shape[1] + 1
    buffers = [pltpu.VMEM((partners * width, 2 * width), BF16)] * 4
    outbox, feat2 = call(
        forces_moving,
        10700,
        [plan],
        [
            q_below,
            (q, cells),
            q_above,
            q_rest,
            feat2_own,
            tiles,
            (rho, cells),
            (fluid, cells),
            tab,
            mine,
            feat1,
        ],
        [],
        [((SLOTS * peers, 8, width), F32), ((total, 32, width), BF16)],
        [pltpu.VMEM((total, 1, width), F32), pltpu.VMEM((MOVERS, 8, width), F32)] + buffers,
        into=[
            (2, 0, RIM),
            (2, RIM, cells),
            (2, RIM + cells, RIM),
            (2, 2 * RIM + cells, SLOTS * peers),
            (1, RIM, cells),
        ],
    )
    inbox = exchange(outbox)
    [stayed] = call(
        forces_staying,
        4096,
        [plan],
        [tab, mine, feat1, feat2, tiles, (q, cells), (rho, cells), (fluid, cells)],
        [],
        [((cells - MOVERS, 8, width), F32, WIDE)],
        buffers,
    )
    return call(
        settle,
        12000,
        [landing],
        [stayed],
        [inbox],
        [((6, cells, width), F32), ((cells, width), F32)],
        [pltpu.VMEM((cells - MOVERS, 8, width), F32)],
        into=[(2, 0, cells - MOVERS)],
    )


def solution(mesh):
    return jax.shard_map(
        shards,
        mesh=mesh,
        in_specs=(
            P(None, ("group", "dev"), None),
            P(None, ("group", "dev"), None),
            P(("group", "dev"), None),
            P(("group", "dev")),
            P(("group", "dev"), None),
            P(("group", "dev"), None),
            P("group", "dev", None, None),
            P("group", None),
        ),
        out_specs=(P(None, ("group", "dev"), None), P(("group", "dev"), None)),
        check_vma=False,
    )
```

```python
import jax
import jax.numpy as jnp
from jax import lax
from jax.experimental import pallas as pl
from jax.experimental.pallas import tpu as pltpu
from jax.sharding import PartitionSpec as P

RIM = 4
SLOTS = 2
PARTNERS = 4
MOVERS = 16
STEP = 8
WIDE = 512
JOB_ROW, JOB_CELL, JOB_COUNT, MOVING, STAYING, OUTS = 0, 128, 256, 272, 304, 336
COUNTS, SENDS, NEAR, PLAN = 512, 544, 640, 1024
WIDE_ROWS, WIDE_LIST = 4096, 1 << 20
STIFFNESS = 2.0
REST_DENSITY = 0.8
VISCOSITY = 0.5
COHESION = 0.3
ADHESION = 0.8
GRAVITY = 1.0
TIME_STEP = 0.5

F32 = jnp.float32
BF16 = jnp.bfloat16
HBM = pl.BlockSpec(memory_space=pltpu.HBM)
VMEM = pl.BlockSpec(memory_space=pltpu.VMEM)


class Moves:
    def __init__(self, ins, outs):
        self.ins, self.outs = list(ins), list(outs)
        self.waited, self.saved = set(), set()
        for copy in self.ins:
            copy.start()

    def need(self, *which):
        for i in which:
            if i not in self.waited:
                self.waited.add(i)
                self.ins[i].wait()

    def save(self, *which):
        for i in which:
            if i not in self.saved:
                self.saved.add(i)
                self.outs[i].start()


def call(kernel, room, ints, held, near, outs, scratch=(), into=()):
    used = [h[1] if isinstance(h, tuple) else h.shape[0] for h in held]
    held = [h[0] if isinstance(h, tuple) else h for h in held]
    n_in, n_near, n_out = len(ints) + len(held), len(near), len(outs)

    def body(*refs):
        sources, refs = refs[:n_in], refs[n_in:]
        close, refs = refs[:n_near], refs[n_near:]
        targets, refs = refs[:n_out], refs[n_out:]
        inner, refs = list(refs[: n_in - len(into)]), refs[n_in - len(into) :]
        results, refs = refs[:n_out], refs[n_out:]
        sources = [r.at[pl.ds(0, PLAN)] if r.shape == (WIDE_LIST,) else r for r in sources]
        for i, count in enumerate(used):
            sources[len(ints) + i] = sources[len(ints) + i].at[pl.ds(0, count)]
        for i, (out, start, count) in enumerate(into):
            target = (*results, *refs[2:])[out]
            inner.insert(len(ints) + i, target.at[pl.ds(start, count)])
            sources[len(ints) + i] = sources[len(ints) + i].at[pl.ds(0, count)]
        in_sems, out_sems, rest = refs[0], refs[1], refs[2:]
        moves = Moves(
            [pltpu.make_async_copy(a, b, in_sems.at[i]) for i, (a, b) in enumerate(zip(sources, inner))],
            [
                pltpu.make_async_copy(a, b.at[pl.ds(0, a.shape[0])], out_sems.at[i])
                for i, (a, b) in enumerate(zip(results, targets))
            ],
        )
        kernel(moves, *inner, *close, *results, *rest)
        moves.need(*range(n_in))
        moves.save(*range(n_out))
        for copy in moves.outs:
            copy.wait()

    return pl.pallas_call(
        body,
        out_shape=[jax.ShapeDtypeStruct((*o[2:], *o[0][len(o) - 2 :]), o[1]) for o in outs],
        in_specs=[HBM] * n_in + [VMEM] * n_near,
        out_specs=[HBM] * n_out,
        scratch_shapes=[
            pltpu.SMEM((PLAN,) if x.shape == (WIDE_LIST,) else x.shape, x.dtype) for x in ints
        ]
        + [
            pltpu.VMEM((n, *x.shape[1:]), x.dtype)
            for n, x in zip(used[len(into) :], held[len(into) :])
        ]
        + [(pltpu.SMEM if len(o[0]) == 1 else pltpu.VMEM)(*o[:2]) for o in outs]
        + [pltpu.SemaphoreType.DMA((n_in,)), pltpu.SemaphoreType.DMA((n_out,))]
        + list(scratch),
        compiler_params=pltpu.CompilerParams(vmem_limit_bytes=(64 << 20) - (room << 10)),
        name=kernel.__name__,
    )(*ints, *held, *near)


def contract(a, b, dim):
    return lax.dot_general(a, b, (((dim,), (0,)), ((), ())), preferred_element_type=F32)


def pieces(value, count):
    parts = []
    for _ in range(count):
        part = value.astype(BF16).astype(F32)
        parts.append(part)
        value = value - part
    return parts


def prepare(moves, counts, sends, pos, vel, mass, walls, own, send, head, tail, fluid):
    cells, width = mass.shape
    moves.need(*range(6))
    m = mass[...]
    root = jnp.exp(jnp.log(m) * (1.0 / 3.0))
    root = root - (root * root * root - m) / (3.0 * root * root)
    wall = walls[...].astype(F32)
    bond = root * root * (COHESION + (ADHESION - COHESION) * wall)
    free = 1.0 - wall
    lane = lax.broadcasted_iota(jnp.int32, (1, width), 1)
    for c in range(cells):
        row = slice(c, c + 1)
        active = lane < counts[c]
        for k in range(3):
            own[c, k : k + 1, :] = pos[k, row, :]
            own[c, 4 + k : 5 + k, :] = vel[k, row, :]
        own[c, 3:4, :] = jnp.where(active, root[row], 0.0)
        own[c, 7:8, :] = jnp.where(active, bond[row], 0.0)
        fluid[row, :] = jnp.where(active, free[row], 0.0)
    head[...] = own[0:RIM]
    tail[...] = own[cells - RIM : cells]
    moves.save(0, 2, 3, 4)
    for t in range(send.shape[0] // SLOTS):
        for k in range(SLOTS):
            cell = sends[0, 0, k, t]
            tile = own[jnp.maximum(cell, 0)]
            send[t * SLOTS + k] = jnp.where(cell >= 0, tile, 0.0)


def squared(tile, sub):
    return jnp.sum(jnp.where(sub < 3, tile * tile, 0.0), axis=0, keepdims=True)


def source_rows(tile, sub):
    root = tile[3:4]
    far = root * (1.0 - 0.25 * squared(tile, sub))
    value = jnp.where(
        sub < 3,
        tile * (0.5 * root),
        jnp.where(sub == 3, far, jnp.where(sub == 4, -0.25 * root, 0.0)),
    )
    a, b, c = pieces(value, 3)
    return jnp.concatenate([a, b, a, c, a, b], 0).astype(BF16)


def target_rows(tile, sub):
    value = jnp.where(
        sub < 3,
        tile,
        jnp.where(sub == 3, 1.0, jnp.where(sub == 4, squared(tile, sub), 0.0)),
    )
    a, b, c = pieces(value, 3)
    return jnp.concatenate([a, a, b, a, c, b], 0).astype(BF16)


def cubes(source, target):
    w = jnp.maximum(contract(source, target, 0), 0.0)
    return jnp.sum((w * w * w).reshape(w.shape[0] // 8, 8, w.shape[1]), axis=0)


def run_jobs(rows, cells, count, tab, first_row, mine, sums):
    last = mine.shape[0] - 1

    def some(t, carry):
        for k in range(STEP):
            c = cells(t * STEP + k)
            value = cubes(tab[rows(t * STEP + k) - first_row], mine[jnp.minimum(c, last)])
            sums[c] = sums[c] + value
        return carry

    lax.fori_loop(0, lax.div(count + (STEP - 1), STEP), some, 0)


def home(moves, near, counts, sends, tiles, sums, tab, mine, plan, jobs):
    cells, _, width = tiles.shape
    sub, _ = rows_and_lanes(width)
    moves.need(*range(4))

    def build(i, carry):
        tab[i] = source_rows(tiles[i], sub)
        mine[i] = target_rows(tiles[i], sub)
        return carry

    lax.fori_loop(0, cells, build, 0, unroll=8)
    moves.save(1, 2)

    sums[cells] = jnp.zeros((8, width), F32)

    def alone(t, carry):
        local, away = carry
        for k in range(STEP):
            c = t * STEP + k
            sums[c] = cubes(tab[c], mine[c])
            plan[COUNTS + c] = counts[c]
            for n in range(near.shape[0]):
                row = near[n, c]
                inside = (row >= RIM) & (row < RIM + cells)
                jobs[local] = row
                jobs[128 + local] = c
                plan[JOB_ROW + away] = row
                plan[JOB_CELL + away] = c
                local = local + inside.astype(jnp.int32)
                away = away + 1 - inside.astype(jnp.int32)
        return local, away

    local, away = lax.fori_loop(0, cells // STEP, alone, (jnp.int32(0), jnp.int32(0)))
    for t in range(sends.shape[3]):
        for k in range(SLOTS):
            plan[SENDS + t * SLOTS + k] = jnp.maximum(sends[0, 0, k, t], 0)
    for k in range(STEP):
        jobs[local + k] = RIM
        jobs[128 + local + k] = cells
        plan[JOB_ROW + away + k] = RIM
        plan[JOB_CELL + away + k] = cells
    plan[JOB_COUNT] = away
    run_jobs(lambda i: jobs[i], lambda i: jobs[128 + i], local, tab, RIM, mine, sums)
    moves.save(0)


def routing(moves, owners, near, counts, owners_v, tiles, q, plan, landing, feat1, feat2_own, seen):
    cells, _, width = feat2_own.shape
    sub, _ = rows_and_lanes(width)
    moves.need(4, 5)

    def first(i, carry):
        feat1[i] = first_features(tiles[i], sub)
        return carry

    def second(i, carry):
        feat2_own[i] = second_features(tiles[RIM + i], q[i], sub)
        return carry

    lax.fori_loop(0, tiles.shape[0], first, 0, unroll=8)
    lax.fori_loop(0, cells, second, 0, unroll=8)
    moves.save(2, 3)
    me = lax.axis_index("dev")
    moves.need(*range(4))
    for d in range(seen.shape[0]):
        seen[d] = 0
    for i in range(seen.shape[0] * SLOTS):
        plan[OUTS + i] = 0
    moving, staying = jnp.int32(0), jnp.int32(0)
    for c in range(cells):
        to = owners[0, me * cells + c]
        leaves = (to != me).astype(jnp.int32)
        plan[COUNTS + c] = counts[c]
        for k in range(near.shape[0]):
            plan[NEAR + k * cells + c] = near[k, c]
        plan[MOVING + moving] = c
        plan[STAYING + staying] = c
        spot = jnp.where(to != me, to * SLOTS + seen[to], seen.shape[0] * SLOTS)
        plan[OUTS + spot] = moving
        seen[to] = seen[to] + leaves
        moving = moving + leaves
        staying = staying + 1 - leaves
    moves.save(0)
    entries = owners_v.shape[1]
    dev = lax.broadcasted_iota(jnp.int32, (entries, 128), 1)
    entry = lax.broadcasted_iota(jnp.int32, (entries, 128), 0)
    belongs = (entry >= dev * cells) & (entry < dev * cells + cells)
    ours = jnp.broadcast_to((owners_v[...] == me).astype(F32), (8, entries)).astype(BF16)
    arrivals = contract(ours, jnp.where(belongs, 1.0, 0.0).astype(BF16), 1)
    earlier = lax.broadcasted_iota(jnp.int32, (128, 128), 0) < lax.broadcasted_iota(
        jnp.int32, (128, 128), 1
    )
    before = contract(arrivals.astype(BF16), jnp.where(earlier, 1.0, 0.0).astype(BF16), 1)
    lane = lax.broadcasted_iota(jnp.int32, (8, 128), 1)
    kind = lax.broadcasted_iota(jnp.int32, (8, 128), 0)
    place = before.astype(jnp.int32)
    comes = (arrivals > 0.0) & (lane != me)
    landing[...] = jnp.where((kind == 0) & ~comes, cells, place)


def densities(
    moves, plan, below, above, rest, tab_own, tiles_own, mine, sums,
    rho, q, q_head, q_tail, send_q, tab, tiles,
):
    cells, _, width = mine.shape
    sub, lane = rows_and_lanes(width)
    moves.need(1, 2, 3)
    for start, count in ((0, RIM), (RIM + cells, tab.shape[0] - RIM - cells)):

        def source(i, carry, start=start):
            tab[start + i] = source_rows(tiles[start + i], sub)
            return carry

        lax.fori_loop(0, count, source, 0, unroll=min(count, 17))

    moves.need(*range(8))
    moves.save(5, 6)
    run_jobs(
        lambda i: plan[JOB_ROW + i], lambda i: plan[JOB_CELL + i], plan[JOB_COUNT], tab, 0, mine, sums
    )
    for c in range(cells):
        row = jnp.sum(sums[c], axis=0, keepdims=True)
        active = lane < plan[COUNTS + c]
        safe = jnp.where(active, row, 1.0)
        value = STIFFNESS * (row - REST_DENSITY) / (safe * safe)
        q[c] = jnp.where(active, value, 0.0)
        rho[c : c + 1, :] = jnp.where(active, row, 0.0)
    for r in range(RIM):
        q_head[r] = q[r]
        q_tail[r] = q[cells - RIM + r]
    for t in range(send_q.shape[0] // SLOTS):
        for k in range(SLOTS):
            send_q[t * SLOTS + k] = q[plan[SENDS + t * SLOTS + k]]


def first_features(tile, sub):
    bond = tile[7:8]
    value = jnp.where(
        sub < 3,
        tile * bond,
        jnp.where(sub == 3, bond, jnp.where(sub < 7, tile, 0.0)),
    )
    return jnp.concatenate(pieces(value, 2), 0).astype(BF16)


def second_features(tile, row_q, sub):
    spot = jnp.where(sub < 3, tile, 1.0)
    spot = jnp.where(sub < 4, spot, row_q * pltpu.roll(spot, 4, 0))
    value = spot * (1.5 * tile[3:4])
    rows = pieces(value, 3) + [jnp.zeros_like(value)]
    return jnp.concatenate(rows, 0).astype(BF16)


class Pairs:
    def __init__(self, plan, tab, mine, feat1, feat2, partners):
        self.plan, self.tab, self.mine, self.feat1, self.feat2 = plan, tab, mine, feat1, feat2
        self.partners = partners

    def row(self, c, k):
        return RIM + c if k == 0 else self.plan[NEAR + (k - 1) * self.mine.shape[0] + c]

    def make(self, c, k, part, odd, even):
        width = odd.shape[1] // 2
        half = width // 2
        source = self.tab[self.row(c, k), :, part * half : part * half + half]
        w = jnp.maximum(contract(source, self.mine[c], 0), 0.0)
        square = w * w
        once, high = w.astype(BF16), square.astype(BF16)
        rows = slice(k * width + part * half, k * width + part * half + half)
        odd[rows, :width] = once
        odd[rows, width:] = once * high
        even[rows, :width] = high
        even[rows, width:] = (square - high.astype(F32)).astype(BF16)

    def fill(self, c, odd, even):
        for k in range(self.partners):
            self.make(c, k, 0, odd, even)
            self.make(c, k, 1, odd, even)

    def step(self, c, odd, even, later, next_odd, next_even, sub):
        width = odd.shape[1] // 2
        first = second = 0.0
        for k in range(self.partners):
            row = self.row(c, k)
            rows = slice(k * width, k * width + width)
            first = first + contract(self.feat1[row], odd[rows], 1)
            self.make(later, k, 0, next_odd, next_even)
            second = second + contract(self.feat2[row], even[rows], 1)
            self.make(later, k, 1, next_odd, next_even)
        first = first[0:8] + first[8:16]
        first = jnp.where(sub < 4, first[:, :width], first[:, width:])
        second = second[:, :width] + second[:, width:]
        return first, second[0:8] + second[8:16] + second[16:24]


def sweep(pairs, order, start, count, buffers, finish, sub, moves):
    a, b = buffers[0:2], buffers[2:4]
    pairs.fill(order[start], *a)
    moves.need(*range(len(moves.ins)))

    def some(t, carry):
        for k in range(STEP):
            i = STEP * t + k
            now, then = (a, b) if k % 2 == 0 else (b, a)
            c = order[start + i]
            later = order[start + jnp.minimum(i + 1, count - 1)]
            finish(i, c, *pairs.step(c, *now, later, *then, sub))
        return carry

    lax.fori_loop(0, count // STEP, some, 0)


def advance(first, second, tile, row_q, row_rho, row_fluid, active, sub):
    mix = row_q * second + pltpu.roll(second, 4, 0) - first
    speed = pltpu.roll(tile, 4, 0)
    drag = pltpu.roll(first, 4, 0) - speed * row_rho
    acc = tile * mix[3:4] - mix + VISCOSITY * drag
    acc = acc - jnp.where(sub == 2, GRAVITY, 0.0)
    step = TIME_STEP * row_fluid
    speed = speed + step * acc
    place = tile + step * speed
    result = jnp.where(
        sub < 3,
        place,
        jnp.where(sub < 6, pltpu.roll(speed, 3, 0), jnp.where(sub == 6, row_rho, 0.0)),
    )
    return jnp.where(active, result, 0.0)


def rows_and_lanes(width):
    return (
        lax.broadcasted_iota(jnp.int32, (8, width), 0),
        lax.broadcasted_iota(jnp.int32, (1, width), 1),
    )


def forces_moving(
    moves, plan, q_below, q_own, q_above, q_rest, feat2_own, tiles, rho, fluid, tab, mine, feat1,
    outbox, feat2, q, moved, *buffers,
):
    cells = rho.shape[0]
    sub, lane = rows_and_lanes(tiles.shape[2])
    moves.need(1, 3, 4, 6)

    def source(i, carry):
        feat2[i] = second_features(tiles[i], q[i], sub)
        return carry

    lax.fori_loop(0, RIM, source, 0, unroll=4)
    lax.fori_loop(RIM + cells, tiles.shape[0], source, 0, unroll=8)
    moves.need(2, 5)
    moves.save(1)
    moves.need(*range(12))

    def finish(i, c, first, second):
        row = pl.ds(c, 1)
        moved[i] = advance(
            first, second, tiles[RIM + c], q[RIM + c], rho[row, :], fluid[row, :], lane < plan[COUNTS + c], sub
        )

    sweep(
        Pairs(plan, tab, mine, feat1, feat2, PARTNERS), plan, MOVING, MOVERS, buffers, finish, sub, moves
    )
    for t in range(outbox.shape[0] // SLOTS):
        for k in range(SLOTS):
            outbox[t * SLOTS + k] = moved[plan[OUTS + t * SLOTS + k]]


def forces_staying(
    moves, plan, tab, mine, feat1, feat2, tiles, q, rho, fluid, stayed, *buffers
):
    sub, lane = rows_and_lanes(tiles.shape[2])
    moves.need(0, 1, 2)

    def finish(i, c, first, second):
        row = pl.ds(c, 1)
        stayed[i] = advance(
            first, second, tiles[RIM + c], q[c], rho[row, :], fluid[row, :], lane < plan[COUNTS + c], sub
        )

    sweep(
        Pairs(plan, tab, mine, feat1, feat2, PARTNERS), plan, STAYING, stayed.shape[0], buffers, finish, sub, moves
    )


def settle(moves, landing, stayed, inbox, state, density, _):
    cells = state.shape[1]
    me = lax.axis_index("dev")
    moves.need(0, 1)

    def put(place, tile):
        for k in range(6):
            state[k, pl.ds(place, 1), :] = tile[k : k + 1]
        density[pl.ds(place, 1), :] = tile[6:7]

    for i in range(stayed.shape[0]):
        put(landing[1, me] + i, stayed[i])
    for t in range(inbox.shape[0] // SLOTS):

        @pl.when(landing[0, t] < cells)
        def _():
            for k in range(SLOTS):
                put(landing[0, t] + k, inbox[t * SLOTS + k])


def shards(positions, velocities, masses, counts, walls, neighbours, send_cells, owners):
    cells, width = masses.shape
    peers = lax.axis_size("dev")
    total = 2 * RIM + cells + SLOTS * peers
    groups = lax.axis_size("group")
    up = [(i, i + 1) for i in range(groups - 1)]
    down = [(i + 1, i) for i in range(groups - 1)]

    def exchange(x):
        return lax.all_to_all(x, "dev", split_axis=0, concat_axis=0, tiled=True)

    near = neighbours.T
    sends = jnp.swapaxes(send_cells, 2, 3)
    own, send, head, tail, fluid = call(
        prepare,
        4096,
        [counts, sends],
        [positions, velocities, masses, walls],
        [],
        [
            ((cells, 8, width), F32, WIDE),
            ((SLOTS * peers, 8, width), F32),
            ((RIM, 8, width), F32),
            ((RIM, 8, width), F32),
            ((cells, width), F32, WIDE_ROWS),
        ],
    )
    rest = exchange(send)
    below = lax.ppermute(tail, "group", up)
    above = lax.ppermute(head, "group", down)
    row_type, small = ((RIM, 1, width), F32), ((SLOTS * peers, 1, width), F32)
    plan_type = ((PLAN,), jnp.int32, WIDE_LIST)
    pair_type, own_type = ((total, 48, width), BF16), ((cells, 48, width), BF16)
    sums, tab_own, mine, jobs = call(
        home,
        4096,
        [near, counts, sends],
        [(own, cells)],
        [],
        [((cells + 1, 8, width), F32, WIDE), own_type, own_type, plan_type],
        [pltpu.SMEM((256,), jnp.int32)],
    )
    rho, q, q_head, q_tail, send_q, tab, tiles = call(
        densities,
        11400,
        [jobs],
        [below, above, rest, tab_own, (own, cells), mine, (sums, cells + 1)],
        [],
        [
            ((cells, width), F32, WIDE_ROWS),
            ((cells, 1, width), F32, WIDE_ROWS),
            row_type,
            row_type,
            small,
            pair_type,
            ((total, 8, width), F32),
        ],
        into=[
            (6, 0, RIM),
            (6, RIM + cells, RIM),
            (6, 2 * RIM + cells, SLOTS * peers),
            (5, RIM, cells),
            (6, RIM, cells),
        ],
    )
    q_rest = exchange(send_q)
    q_below = lax.ppermute(q_tail, "group", up)
    q_above = lax.ppermute(q_head, "group", down)
    plan, landing, feat1, feat2_own = call(
        routing,
        4096,
        [owners, near, counts],
        [owners, tiles, (q, cells)],
        [],
        [
            plan_type,
            ((8, 128), jnp.int32),
            ((total, 16, width), BF16),
            ((cells, 32, width), BF16),
        ],
        [pltpu.SMEM((peers,), jnp.int32)],
    )
    partners = neighbours.shape[1] + 1
    buffers = [pltpu.VMEM((partners * width, 2 * width), BF16)] * 4
    outbox, feat2 = call(
        forces_moving,
        10700,
        [plan],
        [
            q_below,
            (q, cells),
            q_above,
            q_rest,
            feat2_own,
            tiles,
            (rho, cells),
            (fluid, cells),
            tab,
            mine,
            feat1,
        ],
        [],
        [((SLOTS * peers, 8, width), F32), ((total, 32, width), BF16)],
        [pltpu.VMEM((total, 1, width), F32), pltpu.VMEM((MOVERS, 8, width), F32)] + buffers,
        into=[
            (2, 0, RIM),
            (2, RIM, cells),
            (2, RIM + cells, RIM),
            (2, 2 * RIM + cells, SLOTS * peers),
            (1, RIM, cells),
        ],
    )
    inbox = exchange(outbox)
    [stayed] = call(
        forces_staying,
        4096,
        [plan],
        [tab, mine, feat1, feat2, tiles, (q, cells), (rho, cells), (fluid, cells)],
        [],
        [((cells - MOVERS, 8, width), F32, WIDE)],
        buffers,
    )
    return call(
        settle,
        12000,
        [landing],
        [stayed],
        [inbox],
        [((6, cells, width), F32), ((cells, width), F32)],
        [pltpu.VMEM((cells - MOVERS, 8, width), F32)],
        into=[(2, 0, cells - MOVERS)],
    )


def solution(mesh):
    return jax.shard_map(
        shards,
        mesh=mesh,
        in_specs=(
            P(None, ("group", "dev"), None),
            P(None, ("group", "dev"), None),
            P(("group", "dev"), None),
            P(("group", "dev")),
            P(("group", "dev"), None),
            P(("group", "dev"), None),
            P("group", "dev", None, None),
            P("group", None),
        ),
        out_specs=(P(None, ("group", "dev"), None), P(("group", "dev"), None)),
        check_vma=False,
    )
```
